32 devices in a mesh: dp: 32 (over z, y, x, core).
Axes of the slice: x: 2, y: 2, z: 4, core: 2. Of those that a mesh axis runs over, the one named last changes fastest.
Arguments:
- tokens: bfloat16 [28224, 768], P('dp'), may hold values from -6 to 6
- ln1_gain: bfloat16 [768], P('dp'), may hold values from 0.5 to 1.5
- ln1_bias: bfloat16 [768], P('dp'), may hold values from -1.796875 to 1.796875
- qkv_weight: bfloat16 [768, 2304], P('dp'), may hold values from -0.21875 to 0.21875
- query_bias: bfloat16 [768], P('dp'), may hold values from -3 to 3
- value_bias: bfloat16 [768], P('dp'), may hold values from -0.29882812 to 0.29882812
- out_weight: bfloat16 [768, 768], P('dp'), may hold values from -1.25 to 1.25
- out_bias: bfloat16 [768], P('dp'), may hold values from -1.796875 to 1.796875
- ln2_gain: bfloat16 [768], P('dp'), may hold values from 0.5 to 1.5
- ln2_bias: bfloat16 [768], P('dp'), may hold values from -1.796875 to 1.796875
- fc1_weight: bfloat16 [768, 3072], P('dp'), may hold values from -0.21875 to 0.21875
- fc1_bias: bfloat16 [3072], P('dp'), may hold values from -3 to 3
- fc2_weight: bfloat16 [3072, 768], P('dp'), may hold values from -0.109375 to 0.109375
- fc2_bias: bfloat16 [768], P('dp'), may hold values from -1.796875 to 1.796875
- dec_weight: bfloat16 [768, 512], P('dp'), may hold values from -0.21875 to 0.21875
- dec_bias: bfloat16 [512], P('dp'), may hold values from -1.796875 to 1.796875
- mask_token: bfloat16 [512], P('dp'), may hold values from -4 to 4
- kept_offsets: int32 [4032, 7], P('dp'), may hold values from 0 to 13, as said below
- kept_count: int32 [192], P('dp'), may hold values from 3 to 7, as said below
- res_id: int32 [192], P('dp'), may hold values from 0 to 1, as said below
- dec_owner: int32 [4032], P('dp'), may hold values from 0 to 31, as said below
- dec_cot: bfloat16 [57344, 512], P('dp'), may hold values from -6 to 6
Outputs:
- decoded: bfloat16 [57344, 512], P('dp')
- grad_tokens: bfloat16 [28224, 768], P('dp')
- grad_ln1_gain: float32 [768], P('dp')
- grad_ln1_bias: float32 [768], P('dp')
- grad_qkv_weight: float32 [768, 2304], P('dp')
- grad_query_bias: float32 [768], P('dp')
- grad_value_bias: float32 [768], P('dp')
- grad_out_weight: float32 [768, 768], P('dp')
- grad_out_bias: float32 [768], P('dp')
- grad_ln2_gain: float32 [768], P('dp')
- grad_ln2_bias: float32 [768], P('dp')
- grad_fc1_weight: float32 [768, 3072], P('dp')
- grad_fc1_bias: float32 [3072], P('dp')
- grad_fc2_weight: float32 [3072, 768], P('dp')
- grad_fc2_bias: float32 [768], P('dp')
- grad_dec_weight: float32 [768, 512], P('dp')
- grad_dec_bias: float32 [512], P('dp')
- grad_mask_token: float32 [512], P('dp')
The draws below stay inside these ranges and needn't reach their ends.
Inputs may be any that keep to these rules, and one draw needn't show every extreme that they name: `kept_offsets`: each row lists 7 different cells of its window in keeping order; only the first k of a window are kept. `kept_count`: every window of an image keeps this many cells; on every device some image keeps 7. `res_id`: 1 marks an image of side 2 * 14, 0 one of side 14; each device holds exactly 1 images marked 1. `dec_owner`: A device gives at most 4 of its windows to any one owner, and exactly 4 to some owner.
All inputs are finite; a program needn't handle non-finite values.
Results may differ from the reference program's by a relative error of at most 0.013.
Values may be sent and summed in bfloat16 or wider, within the bound.
No kernel may reach another device: no remote copies, remote signals or barrier semaphores. Data moves between devices by JAX's collectives and lax.ppermute only.
A program may use at most 256 MiB of HBM per device.

```python
import jax
import jax.numpy as jnp
from jax import lax

D = 768
HEADS = 12
FF = 3072
DD = 512
GRID = 14
KMIN = 3
KMAX = 7
SETS = 1
IMG_DEV = 6
WIN_DEV = 126
VIS_DEV = 882
WPP = 4
IMAGES = 192
WINDOWS = 4032
ROWS = 28224
DEC_ROWS = 57344
N_DP = 32


def draw_kept_offsets(key, part):
    key = jax.random.fold_in(key, 11)
    key_list = jax.random.split(key, WINDOWS)
    orders = jax.vmap(lambda single: jax.random.permutation(single, GRID))(key_list)
    return orders[:, :KMAX].astype(jnp.int32)


def draw_kept_count(key, part):
    key = jax.random.fold_in(key, 12)
    key_first, key_second = jax.random.split(key)
    counts = jax.random.randint(key_first, (N_DP, IMG_DEV), KMIN, KMAX + 1)
    chosen = jax.random.randint(key_second, (N_DP, 1), 0, IMG_DEV)
    image_ids = jnp.arange(IMG_DEV)[None, :]
    return jnp.where(image_ids == chosen, KMAX, counts).reshape(IMAGES).astype(jnp.int32)


def draw_res_id(key, part):
    key = jax.random.fold_in(key, 13)
    key_list = jax.random.split(key, N_DP)
    orders = jax.vmap(lambda single: jax.random.permutation(single, IMG_DEV))(key_list)
    return (orders < SETS).astype(jnp.int32).reshape(IMAGES)


def draw_dec_owner(key, part):
    key = jax.random.fold_in(key, 14)
    key_list = jax.random.split(key, N_DP)
    orders = jax.vmap(lambda single: jax.random.permutation(single, WIN_DEV))(key_list)
    devices = jnp.arange(N_DP)[:, None]
    return ((devices + orders) % N_DP).astype(jnp.int32).reshape(WINDOWS)


def block_scale(own_key, extent, cuts, low, high):
    def one(dim, shards_of):
        draws = jax.random.uniform(jax.random.fold_in(jax.random.fold_in(own_key, 6), dim), (shards_of,), jnp.float32, low / len(cuts), high / len(cuts))
        return jnp.repeat(jnp.exp(draws), extent[dim] // shards_of).reshape((-1,) + (1,) * (len(extent) - dim - 1))

    gain = one(*cuts[0])
    for cut in cuts[1:]:
        gain = gain * one(*cut)
    return gain


def normal_values(rng, extent, spread, limit, cuts=(), kind=jnp.bfloat16):
    result = jax.random.normal(rng, extent, jnp.float32) * spread
    if len(cuts) > 0:
        result = block_scale(rng, extent, cuts, -0.22, 0.18) * result
    return jnp.clip(result, min=-limit, max=limit).astype(kind)


def setup_inputs(seed: int = 0) -> dict:
    splits = jax.random.split(jax.random.key(seed), 23)
    return {
        "tokens": normal_values(splits[0], (ROWS, D), 1.0, 6.0, ((0, 32),)),
        "ln1_gain": jnp.clip(1.0 + 0.1 * jax.random.normal(splits[1], (D,), jnp.float32), 0.5, 1.5).astype(jnp.bfloat16),
        "ln1_bias": normal_values(splits[2], (D,), 0.3, 1.796875, ((0, 32),)),
        "qkv_weight": normal_values(splits[3], (D, 3 * D), D ** -0.5, 0.21875, ((0, 32),)),
        "query_bias": normal_values(splits[4], (D,), 0.5, 3.0, ((0, 32),)),
        "value_bias": normal_values(splits[5], (D,), 0.05, 0.29882812, ((0, 32),)),
        "out_weight": normal_values(splits[6], (D, D), (D // 32) ** -0.5, 1.25, ((0, 32),)),
        "out_bias": normal_values(splits[7], (D,), 0.3, 1.796875, ((0, 32),)),
        "ln2_gain": jnp.clip(1.0 + 0.1 * jax.random.normal(splits[8], (D,), jnp.float32), 0.5, 1.5).astype(jnp.bfloat16),
        "ln2_bias": normal_values(splits[9], (D,), 0.3, 1.796875, ((0, 32),)),
        "fc1_weight": normal_values(splits[10], (D, FF), D ** -0.5, 0.21875, ((0, 32),)),
        "fc1_bias": normal_values(splits[11], (FF,), 0.5, 3.0, ((0, 32),)),
        "fc2_weight": normal_values(splits[12], (FF, D), FF ** -0.5, 0.109375, ((0, 32),)),
        "fc2_bias": normal_values(splits[13], (D,), 0.3, 1.796875, ((0, 32),)),
        "dec_weight": normal_values(splits[14], (D, DD), D ** -0.5, 0.21875, ((0, 32),)),
        "dec_bias": normal_values(splits[15], (DD,), 0.3, 1.796875, ((0, 32),)),
        "mask_token": normal_values(splits[16], (DD,), 1.0, 4.0, ((0, 32),)),
        "kept_offsets": draw_kept_offsets(jax.random.fold_in(splits[22], 71), 0),
        "kept_count": draw_kept_count(jax.random.fold_in(splits[22], 71), 0),
        "res_id": draw_res_id(jax.random.fold_in(splits[22], 71), 0),
        "dec_owner": draw_dec_owner(jax.random.fold_in(splits[22], 71), 0),
        "dec_cot": normal_values(splits[21], (DEC_ROWS, DD), 1.0, 6.0, ((0, 32),)),
    }


NORM_EPS = 1e-06
MASK_FILL = -1e+30
EXACT = lax.Precision.HIGHEST

@jax.custom_vjp
def low(v):
    return lax.optimization_barrier(v.astype(jnp.bfloat16)).astype(jnp.float32)

@jax.custom_vjp
def low_back(v):
    return v

def low_keep(v):
    return (low(v), None)

def low_pass(kept, grad):
    return (grad,)

def back_keep(v):
    return (v, None)

def back_low(kept, grad):
    return (low(grad),)
low.defvjp(low_keep, low_pass)
low_back.defvjp(back_keep, back_low)

def layer_norm(values, gain_vec, bias_vec):
    row_mean = lax.optimization_barrier(jnp.mean(values, axis=-1, keepdims=True))
    centered = values - row_mean
    variance = lax.optimization_barrier(jnp.mean(centered * centered, axis=-1, keepdims=True))
    return centered * lax.rsqrt(variance + NORM_EPS) * gain_vec + bias_vec

def matmul_exact(left, right):
    return jnp.dot(left, right, precision=EXACT, preferred_element_type=jnp.float32)

def sincos_table(position, side_len, table_width):
    quarter = table_width // 4
    freq_scale = 1.0 / 10000.0 ** (jnp.arange(quarter, dtype=jnp.float32) / quarter)
    column = (position % side_len).astype(jnp.float32)[..., None] * freq_scale
    row_pos = (position // side_len).astype(jnp.float32)[..., None] * freq_scale
    return jnp.concatenate([jnp.sin(column), jnp.cos(column), jnp.sin(row_pos), jnp.cos(row_pos)], axis=-1)

def window_layout(res_vec, count_vec, num_windows):
    per_image = (GRID * (1 + 3 * res_vec)).astype(jnp.int32)
    starts = (jnp.cumsum(per_image) - per_image).astype(jnp.int32)
    window_ids = jnp.arange(num_windows, dtype=jnp.int32)
    image_of = lax.optimization_barrier(jnp.sum((window_ids[:, None] >= starts[None, :]).astype(jnp.int32), axis=1)).astype(jnp.int32) - 1
    picker = (image_of[:, None] == jnp.arange(res_vec.shape[0], dtype=jnp.int32)[None, :]).astype(jnp.int32)
    kept_win = lax.optimization_barrier(jnp.sum(picker * count_vec[None, :], axis=1)).astype(jnp.int32)
    side_win = (GRID * (1 + lax.optimization_barrier(jnp.sum(picker * res_vec[None, :], axis=1)))).astype(jnp.int32)
    start_win = lax.optimization_barrier(jnp.sum(picker * starts[None, :], axis=1)).astype(jnp.int32)
    return (image_of, kept_win, side_win, window_ids - start_win)

def owner_rank(owner_vec):
    window_ids = jnp.arange(owner_vec.shape[0], dtype=jnp.int32)
    earlier = (owner_vec[:, None] == owner_vec[None, :]) & (window_ids[None, :] < window_ids[:, None])
    return lax.optimization_barrier(jnp.sum(earlier.astype(jnp.int32), axis=1)).astype(jnp.int32)

def placement(offsets, kept_win):
    slot_ids = jnp.arange(offsets.shape[-1], dtype=jnp.int32)
    cell_ids = jnp.arange(GRID, dtype=jnp.int32)
    live_slot = slot_ids < kept_win[..., None]
    cell_hits = (offsets[..., None, :] == cell_ids[:, None]) & live_slot[..., None, :]
    return cell_hits.astype(jnp.float32)

def encoder_block(weights, tok_rows, image_rows, live_rows):
    gain_one, bias_one, qkv_weight, query_bias, value_bias, out_weight, out_bias, gain_two, bias_two, fc1_weight, fc1_bias, fc2_weight, fc2_bias = weights
    model_width = tok_rows.shape[1]
    head_dim = model_width // HEADS
    normed = low(layer_norm(tok_rows, gain_one, bias_one))
    qkv_bias = jnp.concatenate([query_bias, jnp.zeros_like(query_bias), value_bias])
    qkv_all = matmul_exact(normed, qkv_weight) + qkv_bias
    qry_rows = low_back(low(qkv_all[:, :model_width])).reshape(-1, HEADS, head_dim)
    key_rows = low_back(low(qkv_all[:, model_width:2 * model_width])).reshape(-1, HEADS, head_dim)
    val_rows = low_back(low(qkv_all[:, 2 * model_width:])).reshape(-1, HEADS, head_dim)
    scores = low_back(jnp.einsum('qhd,khd->hqk', qry_rows, key_rows, precision=EXACT) * head_dim ** (-0.5))
    allowed = (image_rows[:, None] == image_rows[None, :]) & live_rows[None, :]
    scores = jnp.where(allowed[None], scores, MASK_FILL)
    row_top = lax.optimization_barrier(jnp.max(scores, axis=-1, keepdims=True))
    expo_vals = jnp.exp(scores - row_top)
    softmaxed = expo_vals / lax.optimization_barrier(jnp.sum(expo_vals, axis=-1, keepdims=True))
    attended = jnp.einsum('hqk,khd->qhd', low(softmaxed), val_rows, precision=EXACT).reshape(-1, model_width)
    attended = low_back(low(attended))
    attn_out = low_back(matmul_exact(attended, out_weight) + out_bias)
    residual = tok_rows + attn_out
    normed_two = low(layer_norm(residual, gain_two, bias_two))
    hidden = low_back(matmul_exact(normed_two, fc1_weight) + fc1_bias)
    activated = low(jax.nn.gelu(hidden, approximate=False))
    return residual + matmul_exact(activated, fc2_weight) + fc2_bias

def reference(tokens, ln1_gain, ln1_bias, qkv_weight, query_bias, value_bias, out_weight, out_bias, ln2_gain, ln2_bias, fc1_weight, fc1_bias, fc2_weight, fc2_bias, dec_weight, dec_bias, mask_token, kept_offsets, kept_count, res_id, dec_owner, dec_cot):
    params = tuple((single.astype(jnp.float32) for single in (ln1_gain, ln1_bias, qkv_weight, query_bias, value_bias, out_weight, out_bias, ln2_gain, ln2_bias, fc1_weight, fc1_bias, fc2_weight, fc2_bias, dec_weight, dec_bias, mask_token)))
    res_all = res_id.reshape(N_DP, IMG_DEV)
    count_all = kept_count.reshape(N_DP, IMG_DEV)
    image_of, kept_win, side_win, win_in_image = jax.vmap(lambda res_vec, count_vec: window_layout(res_vec, count_vec, WIN_DEV))(res_all, count_all)
    owner_all = dec_owner.reshape(N_DP, WIN_DEV)
    rank_all = jax.vmap(owner_rank)(owner_all)
    slot_ids = jnp.arange(KMAX, dtype=jnp.int32)
    live_rows = (slot_ids[None, None, :] < kept_win[:, :, None]).reshape(N_DP, VIS_DEV)
    image_rows = jnp.repeat(image_of, KMAX, axis=1)
    cell_hits = placement(kept_offsets.reshape(N_DP, WIN_DEV, KMAX), kept_win)
    mask_cells = 1.0 - lax.optimization_barrier(jnp.sum(cell_hits, axis=-1))
    cell_ids = jnp.arange(GRID, dtype=jnp.int32)
    positions = win_in_image[:, :, None] * GRID + cell_ids[None, None, :]
    pos_table = sincos_table(positions, side_win[:, :, None], DD)
    device_ids = jnp.arange(N_DP, dtype=jnp.int32)[:, None]
    target = (owner_all * (N_DP * WPP) + device_ids * WPP + rank_all).reshape(-1)

    def forward(weights, inputs):
        block_weights = weights[:13]
        dec_weight_f, dec_bias_f, mask_f = (weights[13], weights[14], weights[15])
        run_block = jax.checkpoint(lambda packed: encoder_block(block_weights, packed[0], packed[1], packed[2]))
        outputs = lax.map(run_block, (inputs.reshape(N_DP, VIS_DEV, -1), image_rows, live_rows))
        outputs = low_back(low(outputs))
        embedded = low(jnp.einsum('nrc,cd->nrd', outputs, dec_weight_f, precision=EXACT) + dec_bias_f)
        embedded = embedded.reshape(N_DP, WIN_DEV, KMAX, -1)
        placed = jnp.einsum('nwgk,nwkd->nwgd', cell_hits, embedded, precision=EXACT)
        decoded = placed + mask_cells[..., None] * mask_f + pos_table
        canvas = jnp.zeros((N_DP * N_DP * WPP, GRID, decoded.shape[-1]), jnp.float32)
        canvas = canvas.at[target].set(decoded.reshape(-1, GRID, decoded.shape[-1]))
        return canvas.reshape(DEC_ROWS, -1)
    decoded, back_fn = jax.vjp(forward, params, tokens.astype(jnp.float32))
    grads, grad_in = back_fn(dec_cot.astype(jnp.float32))
    return (decoded.astype(jnp.bfloat16), grad_in.astype(jnp.bfloat16), grads[0], grads[1], grads[2], grads[3], grads[4], grads[5], grads[6], grads[7], grads[8], grads[9], grads[10], grads[11], grads[12], grads[13], grads[14], grads[15])
```

```python
import functools

import jax
import jax.numpy as jnp
from jax import lax
from jax.experimental import pallas as pl
from jax.experimental.pallas import tpu as pltpu
from jax.sharding import PartitionSpec as P

HEADS = 12
GRID = 14
NORM_EPS = 1e-06
MASK_FILL = -1e30
BF = jnp.bfloat16
F32 = jnp.float32
MIB = 1 << 20


class Slice:
    def __init__(self, count):
        chips = count // 2
        side = 2 if chips <= 16 else 4
        self.count = count
        self.size = {"c": 2, "x": side, "y": side, "z": chips // (side * side)}
        self.stride = {"c": 1, "x": 2, "y": 2 * side, "z": 2 * side * side}

    def coord(self, axis):
        return (lax.axis_index("dp") // self.stride[axis]) % self.size[axis]

    def shift(self, values, axis, steps):
        stride, size = self.stride[axis], self.size[axis]
        pairs = []
        for source in range(self.count):
            place = (source // stride) % size
            pairs.append((source, source + ((place + steps) % size - place) * stride))
        return lax.ppermute(values, "dp", pairs)

    def spread(self, values, axis):
        return jnp.stack(
            [values] + [self.shift(values, axis, k) for k in range(1, self.size[axis])]
        )

    def groups(self, axes):
        seen, found = set(), []
        for first in range(self.count):
            if first in seen:
                continue
            members = [first]
            for axis in axes:
                members = [
                    m + k * self.stride[axis] for m in members for k in range(self.size[axis])
                ]
            found.append(members)
            seen.update(members)
        return found


def cost(flops, moved, trans=0):
    return pl.CostEstimate(
        flops=int(flops), bytes_accessed=int(moved), transcendentals=int(trans)
    )


def params(mib):
    return pltpu.CompilerParams(vmem_limit_bytes=mib * MIB)


def whole(shape):
    zeros = (0,) * len(shape)
    return pl.BlockSpec(shape, lambda *_: zeros)


SMEM = pl.BlockSpec(memory_space=pltpu.SMEM)


def assemble_kernel(sizes, widths, place, part_a, part_b, from_a, from_b, *outs):
    nz, ny, nx = sizes
    own_z, own_y, own_x, own_c = place[0], place[1], place[2], place[3]
    for kz in range(nz):
        at_z = lax.rem(own_z - kz + nz, nz)
        for ky in range(ny):
            at_y = lax.rem(own_y - ky + ny, ny)
            for kx in range(nx):
                at_x = lax.rem(own_x - kx + nx, nx)
                chip = (at_z * ny + at_y) * nx + at_x
                for core, left, right in ((own_c, part_a, part_b), (1 - own_c, from_a, from_b)):
                    row, start = chip * 2 + core, 0
                    for out, width in zip(outs, widths):
                        half = width // 2
                        out[row, :, :half] = left[ky, kx, kz, :, start : start + half]
                        out[row, :, half:] = right[kx, ky, kz, :, start : start + half]
                        start += half


def gather_start(dev, shards):
    if len(shards) == 1:
        local = shards[0]
    else:
        halves = [s.shape[1] // 2 for s in shards]
        local = jnp.concatenate(
            [s[:, :h] for s, h in zip(shards, halves)] + [s[:, h:] for s, h in zip(shards, halves)],
            axis=1,
        )
    return dev.spread(local, "z")


def gather_finish(dev, shards, along_z):
    rows = shards[0].shape[0]
    widths = [s.shape[1] for s in shards]
    half = sum(widths) // 2
    part_a = dev.spread(dev.spread(along_z[:, :, :half], "x"), "y")
    part_b = dev.spread(dev.spread(along_z[:, :, half:], "y"), "x")
    from_a, from_b = dev.shift(part_a, "c", 1), dev.shift(part_b, "c", 1)
    place = jnp.stack([dev.coord(axis) for axis in "zyxc"]).astype(jnp.int32)
    sizes = (dev.size["z"], dev.size["y"], dev.size["x"])
    kind = shards[0].dtype
    outs = pl.pallas_call(
        functools.partial(assemble_kernel, sizes, widths),
        name="assemble",
        out_shape=[jax.ShapeDtypeStruct((dev.count, rows, w), kind) for w in widths],
        in_specs=[SMEM] + [pl.BlockSpec(memory_space=pltpu.VMEM)] * 4,
        out_specs=[pl.BlockSpec(memory_space=pltpu.VMEM)] * len(widths),
        compiler_params=params(40),
        cost_estimate=cost(0, 4 * dev.count * rows * sum(widths)),
    )(place, part_a, part_b, from_a, from_b)
    return [o.reshape(dev.count * rows, w) for o, w in zip(outs, widths)]


def scatter_group(dev, partials):
    count = dev.count
    rows = partials[0].shape[0] // count
    nz, plane = dev.size["z"], dev.size["y"] * dev.size["x"]
    core = dev.coord("c")

    def pick(values, which):
        split = values.reshape(nz, plane, 2, rows, values.shape[1])
        return jnp.where(which == 0, split[:, :, 0], split[:, :, 1])

    sent = jnp.concatenate([pick(v, 1 - core) for v in partials], axis=-1)
    kept = jnp.concatenate([pick(v, core) for v in partials], axis=-1)
    got = dev.shift(sent, "c", 1)
    chip = (kept.astype(F32) + got.astype(F32)).transpose(1, 0, 2, 3).astype(BF)
    chip = chip.reshape(plane, nz * rows, chip.shape[-1])
    chip = lax.all_to_all(chip, "dp", 0, 0, axis_index_groups=dev.groups("yx"), tiled=True)
    line = jnp.sum(chip.astype(F32), axis=0).astype(BF).reshape(nz, rows, -1)
    line = lax.all_to_all(line, "dp", 0, 0, axis_index_groups=dev.groups("z"), tiled=True)
    total = jnp.sum(line.astype(F32), axis=0)
    out, start = [], 0
    for v in partials:
        out.append(total[:, start : start + v.shape[1]])
        start += v.shape[1]
    return out


def dot(left, right):
    return jnp.dot(left, right, preferred_element_type=F32)


def dot_rows(left, right):
    return lax.dot_general(left, right, (((0,), (0,)), ((), ())), preferred_element_type=F32)


def dot_cols(left, right):
    return lax.dot_general(left, right, (((1,), (1,)), ((), ())), preferred_element_type=F32)


def one_hot(column, row):
    return jnp.where(column == row, 1.0, 0.0).astype(BF)


def row_sum(values):
    return jnp.sum(values, axis=0, keepdims=True)


def normalised(values):
    mean = jnp.mean(values, axis=1, keepdims=True)
    centered = values - mean
    variance = jnp.mean(centered * centered, axis=1, keepdims=True)
    scale = lax.rsqrt(variance + NORM_EPS)
    return centered * scale, scale


def norm_back(unit, scale, gain, grad):
    weighted = grad * gain
    first = jnp.mean(weighted, axis=1, keepdims=True)
    second = jnp.mean(weighted * unit, axis=1, keepdims=True)
    return scale * (weighted - first - unit * second)


class Layout:
    def __init__(self, images, slots):
        self.images, self.slots = images, slots
        self.small, self.large = GRID * slots, 4 * GRID * slots
        self.small_pad = -(-self.small // 16) * 16
        self.large_pad = -(-self.large // 16) * 16
        self.starts = [self.large_pad + i * self.small_pad for i in range(images - 1)]
        self.rows = self.large_pad + (images - 1) * self.small_pad

    def describe(self, big, count_vec, bucket):
        row = jnp.arange(self.rows, dtype=jnp.int32)
        small_id = jnp.maximum(row - self.large_pad, 0) // self.small_pad
        in_large = row < self.large_pad
        offset = jnp.where(in_large, row, row - self.large_pad - small_id * self.small_pad)
        real = offset < jnp.where(in_large, self.large, self.small)
        image = jnp.where(in_large, big, small_id + (small_id >= big).astype(jnp.int32))
        window = GRID * image + 3 * GRID * (image > big).astype(jnp.int32) + offset // self.slots
        slot = offset % self.slots
        kept = jnp.sum(
            jnp.where(
                image[:, None] == jnp.arange(self.images, dtype=jnp.int32)[None, :],
                count_vec[None, :],
                0,
            ),
            axis=1,
        )
        live = real & (slot < kept)
        windows = bucket.shape[0]
        target = jnp.sum(
            jnp.where(
                window[:, None] == jnp.arange(windows, dtype=jnp.int32)[None, :], bucket[None, :], 0
            ),
            axis=1,
        )
        source = jnp.where(real, window * self.slots + slot, -1)
        place = jnp.where(live, target * self.slots + slot, -1)
        return source, live, place


def owner_kernel(slots, wins, cot, off_col, live_col, off_row, info_col, present_row, mask_tok,
                 de_out, base_out, sums_out):
    step = pl.program_id(0)
    cells, rows = wins * GRID, wins * slots
    width = cot.shape[1]
    quarter = width // 4
    grads = cot[...]
    slot_row = lax.broadcasted_iota(jnp.int32, (rows, 1), 0)
    cell_lane = lax.broadcasted_iota(jnp.int32, (1, cells), 1)
    want = jnp.where(live_col[...] > 0, (slot_row // slots) * GRID + off_col[...], -1)
    pick = one_hot(want, cell_lane)
    picked = dot(pick, grads)
    de_out[...] = picked.astype(BF)
    taken = jnp.sum(jnp.where(want == cell_lane, 1.0, 0.0), axis=0, keepdims=True)
    masked = present_row[0].astype(F32) - taken
    mask_sum = dot(jnp.broadcast_to(masked, (8, cells)).astype(BF), grads)[:1]

    cell_row = lax.broadcasted_iota(jnp.int32, (cells, 1), 0)
    want_lane = jnp.where(
        off_row[0] >= 0,
        (lax.broadcasted_iota(jnp.int32, (1, rows), 1) // slots) * GRID + off_row[0],
        -1,
    )
    filled = jnp.sum(jnp.where(cell_row == want_lane, 1.0, 0.0), axis=1, keepdims=True)
    present = info_col[:, 0:1]
    along = info_col[:, 1:2]
    across = info_col[:, 2:3]
    depth = 32
    place = lax.broadcasted_iota(jnp.int32, (depth, quarter), 0).astype(F32)
    index = lax.broadcasted_iota(jnp.int32, (depth, quarter), 1).astype(F32) / quarter
    angle = place * (1.0 / jnp.exp(index * jnp.log(F32(10000.0))))
    table = jnp.concatenate([jnp.sin(angle), jnp.cos(angle)], axis=1)
    high = table.astype(BF)
    rest = table - high.astype(F32)
    middle = rest.astype(BF)
    low = (rest - middle.astype(F32)).astype(BF)
    stacked = jnp.concatenate([high, middle, low], axis=0)
    lane = lax.broadcasted_iota(jnp.int32, (1, 3 * depth), 1) % depth
    shown = present > 0
    first = dot(one_hot(jnp.where(shown, along, -1), lane), stacked)
    second = dot(one_hot(jnp.where(shown, across, -1), lane), stacked)
    bare = present.astype(F32) - filled
    base_out[:, : 2 * quarter] = first + bare * mask_tok[:, : 2 * quarter]
    base_out[:, 2 * quarter :] = second + bare * mask_tok[:, 2 * quarter :]

    @pl.when(step == 0)
    def _():
        sums_out[...] = jnp.zeros_like(sums_out)

    sums_out[0:1, :] += mask_sum
    sums_out[1:2, :] += row_sum(picked)


def decode_kernel(slots, wins, got, off_row, base, out):
    cells, rows = wins * GRID, wins * slots
    cell_row = lax.broadcasted_iota(jnp.int32, (cells, 1), 0)
    want_lane = jnp.where(
        off_row[0] >= 0,
        (lax.broadcasted_iota(jnp.int32, (1, rows), 1) // slots) * GRID + off_row[0],
        -1,
    )
    out[...] = (dot(one_hot(cell_row, want_lane), got[...]) + base[...]).astype(BF)


def first_norm_kernel(tokens, source, gain, bias, x_out, h_out):
    lane = lax.broadcasted_iota(jnp.int32, (1, tokens.shape[0]), 1)
    moved = dot(one_hot(source[...], lane), tokens[...])
    x_out[...] = moved.astype(BF)
    unit, _ = normalised(moved)
    h_out[...] = (unit * gain[...] + bias[...]).astype(BF)


def softmax_rows(scores):
    top = jnp.max(scores, axis=1, keepdims=True)
    expo = jnp.exp(scores - top)
    return (expo * (1.0 / jnp.sum(expo, axis=1, keepdims=True))).astype(BF)


def attention_kernel(lay, chunk, head_dim, h_in, w_q, w_k, w_v, b_q, b_v, mask_l, mask_s,
                     q_out, k_out, v_out, pl_out, ps_out, o_out, scores):
    big, small = lay.large_pad, lay.small_pad
    normed = h_in[...]
    q_out[...] = ((dot(normed, w_q[...]) + b_q[...]) * (head_dim**-0.5)).astype(BF)
    k_out[...] = dot(normed, w_k[...]).astype(BF)
    v_out[...] = (dot(normed, w_v[...]) + b_v[...]).astype(BF)
    lane = lax.broadcasted_iota(jnp.int32, (1, 2 * head_dim), 1)
    low = lane < head_dim
    halves = (jnp.where(low, 1.0, 0.0).astype(BF), jnp.where(low, 0.0, 1.0).astype(BF))
    for pair in range(q_out.shape[1] // (2 * head_dim)):
        cols = slice(pair * 2 * head_dim, (pair + 1) * 2 * head_dim)
        first = []
        for half in range(2):
            head = 2 * pair + half
            query = q_out[:big, cols] * halves[half]
            scores[...] = dot_cols(query, k_out[:big, cols])
            for start in range(0, big, chunk):
                part = scores[start : start + chunk, :] + mask_l[...]
                pl_out[head, start : start + chunk, :] = softmax_rows(part)
            outs = [dot(pl_out[head], v_out[:big, cols])]
            for i, start in enumerate(lay.starts):
                rows = slice(start, start + small)
                query = q_out[rows, cols] * halves[half]
                part = dot_cols(query, k_out[rows, cols]) + mask_s[i : i + 1, :]
                weights = softmax_rows(part)
                ps_out[head, i] = weights
                outs.append(dot(weights, v_out[rows, cols]))
            if half == 0:
                first = outs
        spans = [(0, big)] + [(s, small) for s in lay.starts]
        for (start, size), left, right in zip(spans, first, outs):
            o_out[start : start + size, cols] = jnp.where(low, left, right).astype(BF)


def out_kernel(o_in, w_out, bias, x_in, gain, offset, r_out, h_out):
    residual = x_in[...].astype(F32) + dot(o_in[...], w_out[...]) + bias[...]
    r_out[...] = residual
    unit, _ = normalised(residual)
    h_out[...] = (unit * gain[...] + offset[...]).astype(BF)


def fc1_kernel(chunk, h_in, weight, bias, g_out, d_out, hidden):
    hidden[...] = dot(h_in[...], weight[...])
    for start in range(0, hidden.shape[0], chunk):
        rows = slice(start, start + chunk)
        u = hidden[rows, :] + bias[...]
        half = 0.5 + 0.5 * lax.erf(u * (0.5**0.5))
        g_out[rows, :] = (u * half).astype(BF)
        density = jnp.exp(u * u * -0.5) * 0.3989422804014327
        d_out[rows, :] = (half + u * density).astype(BF)


def fc2_kernel(g_in, w_two, b_two, r_in, w_dec, b_dec, place, y_out, e_out, kept):
    step = pl.program_id(0)
    rows = g_in.shape[0]
    y = (r_in[...] + dot(g_in[...], w_two[...]) + b_two[...]).astype(BF)
    y_out[...] = y
    kept[pl.ds(pl.multiple_of(step * rows, rows), rows), :] = (
        dot(y, w_dec[...]) + b_dec[...]
    ).astype(BF)

    @pl.when(step == pl.num_programs(0) - 1)
    def _():
        target = lax.broadcasted_iota(jnp.int32, (e_out.shape[0], 1), 0)
        e_out[...] = dot(one_hot(target, place[...]), kept[...]).astype(BF)


def dec_back_kernel(got, place, w_dec, y_in, dy_out, dw_out, db_out):
    lane = lax.broadcasted_iota(jnp.int32, (1, got.shape[0]), 1)
    grad = dot(one_hot(place[...], lane), got[...]).astype(BF)
    dy = dot_cols(grad, w_dec[...]).astype(BF)
    dy_out[...] = dy
    dw_out[...] = dot_rows(y_in[...], grad).astype(BF)
    db_out[...] = row_sum(dy.astype(F32))


def fc2_back_kernel(dy_in, w_two, g_in, d_in, du_out, dw_out, db_out):
    dy = dy_in[...]
    du = (dot_cols(dy, w_two[...]) * d_in[...].astype(F32)).astype(BF)
    du_out[...] = du
    db_out[...] = row_sum(du.astype(F32))
    dw_out[...] = dot_rows(g_in[...], dy).astype(BF)


def fc1_back_kernel(du_in, w_one, h_in, dh_out, dw_out, turned):
    step = pl.program_id(0)

    @pl.when(step == 0)
    def _():
        turned[...] = h_in[...].T
        dh_out[...] = jnp.zeros_like(dh_out)

    du = du_in[...]
    dw_out[...] = dot(turned[...], du).astype(BF)
    dh_out[...] += dot_cols(du, w_one[...])


def out_back_kernel(dh_in, r_in, dy_in, gain, w_out, o_in, dr_out, do_out, dw_out, sums, total):
    step = pl.program_id(0)
    unit, scale = normalised(r_in[...])
    grad = dh_in[...]
    dr = dy_in[...].astype(F32) + norm_back(unit, scale, gain[...], grad)
    dr_out[...] = dr
    da = dr.astype(BF)
    do_out[...] = dot_cols(da, w_out[...]).astype(BF)

    @pl.when(step == 0)
    def _():
        sums[...] = jnp.zeros_like(sums)
        total[...] = jnp.zeros_like(total)

    sums[0:1, :] += row_sum(grad * unit)
    sums[1:2, :] += row_sum(grad)
    sums[2:3, :] += row_sum(da.astype(F32))
    total[...] += dot_rows(o_in[...], da)

    @pl.when(step == pl.num_programs(0) - 1)
    def _():
        dw_out[...] = total[...].astype(BF)


def attention_back_kernel(lay, chunk, head_dim, h_in, q_in, k_in, v_in, pl_in, ps_in, do_in,
                          dq_out, dk_out, dv_out, wq_out, wk_out, wv_out, sums, turned, scores, ds_big):
    step = pl.program_id(0)
    big, small = lay.large_pad, lay.small_pad

    @pl.when(step == 0)
    def _():
        turned[...] = h_in[...].T

    lane = lax.broadcasted_iota(jnp.int32, (1, 2 * head_dim), 1)
    low = lane < head_dim
    halves = (jnp.where(low, 1.0, 0.0).astype(BF), jnp.where(low, 0.0, 1.0).astype(BF))

    def back_rows(weights, grad):
        p = weights.astype(F32)
        inner = jnp.sum(grad * p, axis=1, keepdims=True)
        return (p * (grad - inner)).astype(BF)

    for pair in range(q_in.shape[1] // (2 * head_dim)):
        cols = slice(pair * 2 * head_dim, (pair + 1) * 2 * head_dim)
        spans = [(0, big)] + [(s, small) for s in lay.starts]
        first = []
        for half in range(2):
            head = 2 * pair + half
            found = []
            for i, (start, size) in enumerate(spans):
                rows = slice(start, start + size)
                grad_o = do_in[rows, cols] * halves[half]
                if i == 0:
                    scores[...] = dot_cols(grad_o, v_in[rows, cols])
                    for s in range(0, big, chunk):
                        ds_big[s : s + chunk, :] = back_rows(
                            pl_in[head, s : s + chunk, :], scores[s : s + chunk, :]
                        )
                    weights, ds = pl_in[head], ds_big[...]
                else:
                    weights = ps_in[head, i - 1]
                    ds = back_rows(weights, dot_cols(grad_o, v_in[rows, cols]))
                found.append(
                    (
                        dot(ds, k_in[rows, cols]),
                        dot_rows(ds, q_in[rows, cols]),
                        dot_rows(weights, do_in[rows, cols]),
                    )
                )
            if half == 0:
                first = found
        for (start, size), left, right in zip(spans, first, found):
            rows = slice(start, start + size)
            dq_out[rows, cols] = (
                jnp.where(low, left[0], right[0]) * (head_dim**-0.5)
            ).astype(BF)
            dk_out[rows, cols] = jnp.where(low, left[1], right[1]).astype(BF)
            dv_out[rows, cols] = jnp.where(low, left[2], right[2]).astype(BF)
    wq_out[...] = dot(turned[...], dq_out[...]).astype(BF)
    wk_out[...] = dot(turned[...], dk_out[...]).astype(BF)
    wv_out[...] = dot(turned[...], dv_out[...]).astype(BF)
    sums[0:1, :] = row_sum(dq_out[...].astype(F32))
    sums[1:2, :] = row_sum(dv_out[...].astype(F32))


def first_back_kernel(dq_in, dk_in, dv_in, w_qkv, x_in, dr_in, gain, source, out, sums, kept):
    step = pl.program_id(0)
    rows, width = x_in.shape
    grad = dot_cols(dq_in[...], w_qkv[:, :width])
    grad += dot_cols(dk_in[...], w_qkv[:, width : 2 * width])
    grad += dot_cols(dv_in[...], w_qkv[:, 2 * width :])
    unit, scale = normalised(x_in[...].astype(F32))
    moved = dr_in[...] + norm_back(unit, scale, gain[...], grad)
    kept[pl.ds(pl.multiple_of(step * rows, rows), rows), :] = moved.astype(BF)

    @pl.when(step == 0)
    def _():
        sums[...] = jnp.zeros_like(sums)

    sums[0:1, :] += row_sum(grad * unit)
    sums[1:2, :] += row_sum(grad)

    @pl.when(step == pl.num_programs(0) - 1)
    def _():
        slot = lax.broadcasted_iota(jnp.int32, (out.shape[0], 1), 0)
        out[...] = dot(one_hot(slot, source[...]), kept[...]).astype(BF)


def owner_rank(owner_vec):
    window_ids = jnp.arange(owner_vec.shape[0], dtype=jnp.int32)
    earlier = (owner_vec[:, None] == owner_vec[None, :]) & (
        window_ids[None, :] < window_ids[:, None]
    )
    return jnp.sum(earlier.astype(jnp.int32), axis=1)


def spec(shape, index):
    return pl.BlockSpec(shape, index)


def local(tokens, ln1_gain, ln1_bias, qkv_weight, query_bias, value_bias, out_weight, out_bias,
          ln2_gain, ln2_bias, fc1_weight, fc1_bias, fc2_weight, fc2_bias, dec_weight, dec_bias,
          mask_token, kept_offsets, kept_count, res_id, dec_owner, dec_cot):
    count = lax.axis_size("dp")
    dev = Slice(count)
    vis, D = tokens.shape
    dec_width = dec_cot.shape[1]
    windows, slots = kept_offsets.shape
    images = res_id.shape[0]
    hidden = fc1_weight.shape[1]
    head_dim = D // HEADS
    per_peer = (windows + count - 1) // count
    total = count * per_peer
    lay = Layout(images, slots)
    R = lay.rows
    sd = jax.ShapeDtypeStruct

    vectors = [ln1_gain, ln1_bias, query_bias, value_bias, out_bias, ln2_gain, ln2_bias, fc1_bias,
               fc2_bias, dec_bias, mask_token]
    packed = jnp.concatenate(vectors)
    packed = lax.all_to_all(
        jnp.broadcast_to(packed[None, :], (count, packed.shape[0])), "dp", 0, 0, tiled=True
    ).astype(F32)
    full, start = [], 0
    for v in vectors:
        full.append(packed[:, start : start + v.shape[0]].reshape(1, -1))
        start += v.shape[0]
    (g1, b1, bq, bv, bo, g2, b2, bf1, bf2, bdec, mask_tok) = full

    group_a, group_b, group_c = [qkv_weight], [out_weight, dec_weight, fc1_weight], [fc2_weight]
    z_a = gather_start(dev, group_a)
    (w_qkv,) = gather_finish(dev, group_a, z_a)
    z_b = gather_start(dev, group_b)
    w_out, w_dec, w_one = gather_finish(dev, group_b, z_b)
    z_c = gather_start(dev, group_c)
    (w_two,) = gather_finish(dev, group_c, z_c)

    image_ids = jnp.arange(images, dtype=jnp.int32)
    big = jnp.sum(image_ids * res_id)
    bucket = dec_owner * per_peer + owner_rank(dec_owner)
    source, live, place = lay.describe(big, kept_count, bucket)
    source_col, source_row = source[:, None], source[None, :]
    place_col, place_row = place[:, None], place[None, :]
    mask_all = jnp.where(live, 0.0, MASK_FILL).astype(F32)
    mask_l = mask_all[None, : lay.large_pad]
    mask_s = mask_all[lay.large_pad :].reshape(images - 1, lay.small_pad)

    win = jnp.arange(windows, dtype=jnp.int32)
    big_start = GRID * big
    in_big = (win >= big_start) & (win < big_start + 4 * GRID)
    after = win >= big_start + 4 * GRID
    image_win = jnp.where(in_big, big, jnp.where(after, win // GRID - 3, win // GRID))
    in_image = jnp.where(in_big, win - big_start, win % GRID)
    kept_win = jnp.sum(
        jnp.where(image_win[:, None] == image_ids[None, :], kept_count[None, :], 0), axis=1
    )
    side_win = jnp.where(in_big, 2 * GRID, GRID)
    info = jnp.concatenate(
        [jnp.stack([jnp.ones_like(win), kept_win, in_image, side_win], axis=1), kept_offsets], axis=1
    )
    slot_of = jnp.arange(total, dtype=jnp.int32)
    info_send = jnp.sum(
        jnp.where((slot_of[:, None] == bucket[None, :])[:, :, None], info[None, :, :], 0), axis=1
    )
    info_got = lax.all_to_all(
        info_send.reshape(count, per_peer, -1), "dp", 0, 0, tiled=True
    ).reshape(total, -1)

    wins = 16
    steps = total // wins
    off_live = jnp.where(
        jnp.arange(slots, dtype=jnp.int32)[None, :] < info_got[:, 1:2], info_got[:, 4:], -1
    )
    off_col = jnp.maximum(off_live, 0).reshape(-1, 1)
    live_col = (off_live >= 0).astype(jnp.int32).reshape(-1, 1)
    off_row = off_live.reshape(steps, 1, wins * slots)
    present_row = jnp.repeat(info_got[:, 0:1], GRID, axis=1).reshape(steps, 1, wins * GRID)
    spot = info_got[:, 2:3] * GRID + jnp.arange(GRID, dtype=jnp.int32)[None, :]
    side = jnp.maximum(info_got[:, 3:4], 1)
    info_col = jnp.stack(
        [jnp.broadcast_to(info_got[:, 0:1], spot.shape), spot % side, spot // side], axis=-1
    ).reshape(total * GRID, 3)
    cells_w, rows_w = wins * GRID, wins * slots
    by_step = lambda shape: spec(shape, lambda i: (i,) + (0,) * (len(shape) - 1))
    de_send, base, owner_sums = pl.pallas_call(
        functools.partial(owner_kernel, slots, wins),
        name="owner_side",
        grid=(steps,),
        in_specs=[by_step((cells_w, dec_width)), by_step((rows_w, 1)), by_step((rows_w, 1)),
                  by_step((1, 1, rows_w)), by_step((cells_w, 3)), by_step((1, 1, cells_w)),
                  whole((1, dec_width))],
        out_specs=[by_step((rows_w, dec_width)), by_step((cells_w, dec_width)), whole((8, dec_width))],
        out_shape=[sd((total * slots, dec_width), BF), sd((total * GRID, dec_width), F32),
                   sd((8, dec_width), F32)],
        compiler_params=params(32),
        cost_estimate=cost(4e9, 8e6, 1e5),
    )(dec_cot, off_col, live_col, off_row, info_col, present_row, mask_tok)
    de_got = lax.all_to_all(
        de_send.reshape(count, per_peer * slots, dec_width), "dp", 0, 0, tiled=True
    ).reshape(total * slots, dec_width)

    tile = R // 3
    rows_of = lambda width: spec((tile, width), lambda i: (i, 0))
    x_rows, h_one = pl.pallas_call(
        first_norm_kernel,
        name="first_norm",
        grid=(3,),
        in_specs=[whole((vis, D)), rows_of(1), whole((1, D)), whole((1, D))],
        out_specs=[rows_of(D), rows_of(D)],
        out_shape=[sd((R, D), BF), sd((R, D), BF)],
        compiler_params=params(32),
        cost_estimate=cost(2 * R * vis * D, 4e6),
    )(tokens, source_col, g1, b1)

    group = 4
    parts = HEADS // group
    gw = group * head_dim
    chunk = lay.large_pad // 5
    col_of = lambda base_: spec((D, gw), lambda i: (0, base_ * parts + i))
    act = spec((R, gw), lambda i: (0, i))
    vec = spec((1, gw), lambda i: (0, i))
    p_big = spec((group, lay.large_pad, lay.large_pad), lambda i: (i, 0, 0))
    p_small = spec((group, images - 1, lay.small_pad, lay.small_pad), lambda i: (i, 0, 0, 0))
    p_big_t = sd((HEADS, lay.large_pad, lay.large_pad), BF)
    p_small_t = sd((HEADS, images - 1, lay.small_pad, lay.small_pad), BF)
    q_rows, k_rows, v_rows, prob_l, prob_s, att = pl.pallas_call(
        functools.partial(attention_kernel, lay, chunk, head_dim),
        name="attention",
        grid=(parts,),
        in_specs=[whole((R, D)), col_of(0), col_of(1), col_of(2), vec, vec,
                  whole((1, lay.large_pad)), whole((images - 1, lay.small_pad))],
        out_specs=[act, act, act, p_big, p_small, act],
        out_shape=[sd((R, D), BF)] * 3 + [p_big_t, p_small_t, sd((R, D), BF)],
        scratch_shapes=[pltpu.VMEM((lay.large_pad, lay.large_pad), F32)],
        compiler_params=params(48),
        cost_estimate=cost(2 * R * D * 3 * D + 4e9, 2e7, 3e6),
    )(h_one, w_qkv, w_qkv, w_qkv, bq, bv, mask_l, mask_s)

    r_one, h_two = pl.pallas_call(
        out_kernel,
        name="out_projection",
        grid=(3,),
        in_specs=[rows_of(D), whole((D, D)), whole((1, D)), rows_of(D), whole((1, D)), whole((1, D))],
        out_specs=[rows_of(D), rows_of(D)],
        out_shape=[sd((R, D), F32), sd((R, D), BF)],
        compiler_params=params(32),
        cost_estimate=cost(2 * R * D * D, 9e6),
    )(att, w_out, bo, x_rows, g2, b2)

    ht = hidden // 6
    act_h, d_gelu = pl.pallas_call(
        functools.partial(fc1_kernel, R // 24),
        name="fc1",
        grid=(6,),
        in_specs=[whole((R, D)), spec((D, ht), lambda i: (0, i)), spec((1, ht), lambda i: (0, i))],
        out_specs=[spec((R, ht), lambda i: (0, i))] * 2,
        out_shape=[sd((R, hidden), BF)] * 2,
        scratch_shapes=[pltpu.VMEM((R, ht), F32)],
        compiler_params=params(32),
        cost_estimate=cost(2 * R * D * hidden, 2e7, 6e6),
    )(h_two, w_one, bf1)

    y_rows, e_send = pl.pallas_call(
        fc2_kernel,
        name="fc2_and_embed",
        grid=(3,),
        in_specs=[rows_of(hidden), whole((hidden, D)), whole((1, D)), rows_of(D),
                  whole((D, dec_width)), whole((1, dec_width)), whole((1, R))],
        out_specs=[rows_of(D), whole((total * slots, dec_width))],
        out_shape=[sd((R, D), BF), sd((total * slots, dec_width), BF)],
        scratch_shapes=[pltpu.VMEM((R, dec_width), BF)],
        compiler_params=params(48),
        cost_estimate=cost(2 * R * D * hidden + 4 * R * D * dec_width, 2e7),
    )(act_h, w_two, bf2, r_one, w_dec, bdec, place_row)

    e_got = lax.all_to_all(
        e_send.reshape(count, per_peer * slots, dec_width), "dp", 0, 0, tiled=True
    ).reshape(total * slots, dec_width)
    decoded = pl.pallas_call(
        functools.partial(decode_kernel, slots, wins),
        name="decode",
        grid=(steps,),
        in_specs=[by_step((rows_w, dec_width)), by_step((1, 1, rows_w)), by_step((cells_w, dec_width))],
        out_specs=by_step((cells_w, dec_width)),
        out_shape=sd((total * GRID, dec_width), BF),
        compiler_params=params(32),
        cost_estimate=cost(1e9, 7e6),
    )(e_got, off_row, base)

    dy, dw_dec, db_two = pl.pallas_call(
        dec_back_kernel,
        name="embed_back",
        in_specs=[pl.BlockSpec(memory_space=pltpu.VMEM)] * 4,
        out_specs=[pl.BlockSpec(memory_space=pltpu.VMEM)] * 3,
        out_shape=[sd((R, D), BF), sd((D, dec_width), BF), sd((1, D), F32)],
        compiler_params=params(40),
        cost_estimate=cost(6 * R * D * dec_width, 7e6),
    )(de_got, place_col, w_dec, y_rows)

    ht = hidden // 4
    du, dw_two, db_one = pl.pallas_call(
        fc2_back_kernel,
        name="fc2_back",
        grid=(4,),
        in_specs=[whole((R, D)), spec((ht, D), lambda i: (i, 0)), spec((R, ht), lambda i: (0, i)),
                  spec((R, ht), lambda i: (0, i))],
        out_specs=[spec((R, ht), lambda i: (0, i)), spec((ht, D), lambda i: (i, 0)),
                   spec((1, ht), lambda i: (0, i))],
        out_shape=[sd((R, hidden), BF), sd((hidden, D), BF), sd((1, hidden), F32)],
        compiler_params=params(48),
        cost_estimate=cost(4 * R * D * hidden, 3e7),
    )(dy, w_two, act_h, d_gelu)

    dh_two, dw_one = pl.pallas_call(
        fc1_back_kernel,
        name="fc1_back",
        grid=(4,),
        in_specs=[spec((R, ht), lambda i: (0, i)), spec((D, ht), lambda i: (0, i)), whole((R, D))],
        out_specs=[whole((R, D)), spec((D, ht), lambda i: (0, i))],
        out_shape=[sd((R, D), F32), sd((D, hidden), BF)],
        scratch_shapes=[pltpu.VMEM((D, R), BF)],
        compiler_params=params(48),
        cost_estimate=cost(4 * R * D * hidden, 2e7),
    )(du, w_one, h_two)

    dr, d_att, dw_out, sums_two = pl.pallas_call(
        out_back_kernel,
        name="out_back",
        grid=(3,),
        in_specs=[rows_of(D), rows_of(D), rows_of(D), whole((1, D)), whole((D, D)), rows_of(D)],
        out_specs=[rows_of(D), rows_of(D), whole((D, D)), whole((8, D))],
        out_shape=[sd((R, D), F32), sd((R, D), BF), sd((D, D), BF), sd((8, D), F32)],
        scratch_shapes=[pltpu.VMEM((D, D), F32)],
        compiler_params=params(40),
        cost_estimate=cost(4 * R * D * D, 2e7),
    )(dh_two, r_one, dy, g2, w_out, att)

    dq, dk, dv, dw_q, dw_k, dw_v, sums_qv = pl.pallas_call(
        functools.partial(attention_back_kernel, lay, chunk, head_dim),
        name="attention_back",
        grid=(parts,),
        in_specs=[whole((R, D)), act, act, act, p_big, p_small, act],
        out_specs=[act, act, act] + [spec((D, gw), lambda i: (0, i))] * 3 + [spec((8, gw), lambda i: (0, i))],
        out_shape=[sd((R, D), BF)] * 3 + [sd((D, D), BF)] * 3 + [sd((8, D), F32)],
        scratch_shapes=[pltpu.VMEM((D, R), BF), pltpu.VMEM((lay.large_pad, lay.large_pad), F32),
                        pltpu.VMEM((lay.large_pad, lay.large_pad), BF)],
        compiler_params=params(56),
        cost_estimate=cost(2 * R * D * 3 * D + 8e9, 3e7),
    )(h_one, q_rows, k_rows, v_rows, prob_l, prob_s, d_att)

    grad_tokens, sums_one = pl.pallas_call(
        first_back_kernel,
        name="first_back",
        grid=(3,),
        in_specs=[rows_of(D), rows_of(D), rows_of(D), whole((D, 3 * D)), rows_of(D), rows_of(D),
                  whole((1, D)), whole((1, R))],
        out_specs=[whole((vis, D)), whole((8, D))],
        out_shape=[sd((vis, D), BF), sd((8, D), F32)],
        scratch_shapes=[pltpu.VMEM((R, D), BF)],
        compiler_params=params(48),
        cost_estimate=cost(2 * R * D * 3 * D + 2 * R * vis * D, 2e7),
    )(dq, dk, dv, w_qkv, x_rows, dr, g1, source_row)

    (grad_two,) = scatter_group(dev, [dw_two])
    grad_one, grad_dec = scatter_group(dev, [dw_one, dw_dec])
    grad_out, grad_q, grad_k, grad_v = scatter_group(dev, [dw_out, dw_q, dw_k, dw_v])
    grad_qkv = jnp.concatenate([grad_q, grad_k, grad_v], axis=1)

    small = [sums_one[0], sums_one[1], sums_qv[0], sums_qv[1], sums_two[2], sums_two[0], sums_two[1],
             db_one[0], db_two[0], owner_sums[1], owner_sums[0]]
    rows = jnp.concatenate([v.reshape(count, -1) for v in small], axis=1)
    rows = jnp.sum(lax.all_to_all(rows, "dp", 0, 0, tiled=True), axis=0)
    vec_grads, start = [], 0
    for v in vectors:
        vec_grads.append(rows[start : start + v.shape[0]])
        start += v.shape[0]
    (gg1, gb1, gbq, gbv, gbo, gg2, gb2, gbf1, gbf2, gbdec, gmask) = vec_grads
    return (decoded, grad_tokens, gg1, gb1, grad_qkv, gbq, gbv, grad_out, gbo, gg2, gb2, grad_one,
            gbf1, grad_two, gbf2, grad_dec, gbdec, gmask)


def solution(mesh):
    mat, vec = P("dp", None), P("dp")
    in_specs = (mat, vec, vec, mat, vec, vec, mat, vec, vec, vec, mat, vec, mat, vec, mat, vec, vec,
                mat, vec, vec, vec, mat)
    out_specs = (mat, mat, vec, vec, mat, vec, vec, mat, vec, vec, vec, mat, vec, mat, vec, mat, vec,
                 vec)
    return jax.shard_map(local, mesh=mesh, in_specs=in_specs, out_specs=out_specs, check_vma=False)
```

```python
import functools

import jax
import jax.numpy as jnp
from jax import lax
from jax.experimental import pallas as pl
from jax.experimental.pallas import tpu as pltpu
from jax.sharding import PartitionSpec as P

HEADS = 12
GRID = 14
NORM_EPS = 1e-06
MASK_FILL = -1e30
BF = jnp.bfloat16
F32 = jnp.float32
MIB = 1 << 20


class Slice:
    def __init__(self, count):
        chips = count // 2
        side = 2 if chips <= 16 else 4
        self.count = count
        self.size = {"c": 2, "x": side, "y": side, "z": chips // (side * side)}
        self.stride = {"c": 1, "x": 2, "y": 2 * side, "z": 2 * side * side}

    def coord(self, axis):
        return (lax.axis_index("dp") // self.stride[axis]) % self.size[axis]

    def shift(self, values, axis, steps):
        stride, size = self.stride[axis], self.size[axis]
        pairs = []
        for source in range(self.count):
            place = (source // stride) % size
            pairs.append((source, source + ((place + steps) % size - place) * stride))
        return lax.ppermute(values, "dp", pairs)

    def copies(self, values, axis):
        return [values] + [self.shift(values, axis, k) for k in range(1, self.size[axis])]

    def shift_plane(self, values, ky, kx):
        pairs = []
        for source in range(self.count):
            target = source
            for axis, steps in (("y", ky), ("x", kx)):
                stride, size = self.stride[axis], self.size[axis]
                place = (source // stride) % size
                target += ((place + steps) % size - place) * stride
            pairs.append((source, target))
        return lax.ppermute(values, "dp", pairs)

    def groups(self, axes):
        seen, found = set(), []
        for first in range(self.count):
            if first in seen:
                continue
            members = [first]
            for axis in axes:
                members = [
                    m + k * self.stride[axis] for m in members for k in range(self.size[axis])
                ]
            found.append(members)
            seen.update(members)
        return found


def cost(flops, moved, trans=0, weight=1):
    return pl.CostEstimate(
        flops=int(weight * flops), bytes_accessed=int(weight * moved), transcendentals=int(trans)
    )


def params():
    return pltpu.CompilerParams(vmem_limit_bytes=60 * MIB)


def whole(shape):
    zeros = (0,) * len(shape)
    return pl.BlockSpec(shape, lambda *_: zeros)


SMEM = pl.BlockSpec(memory_space=pltpu.SMEM)
VMEM = pl.BlockSpec(memory_space=pltpu.VMEM)


def assemble_kernel(sizes, widths, place, part_a, part_b, from_a, from_b, *outs):
    nz, ny, nx = sizes
    own_z, own_y, own_x, own_c = place[0], place[1], place[2], place[3]
    for kz in range(nz):
        at_z = lax.rem(own_z - kz + nz, nz)
        for ky in range(ny):
            at_y = lax.rem(own_y - ky + ny, ny)
            for kx in range(nx):
                at_x = lax.rem(own_x - kx + nx, nx)
                chip = (at_z * ny + at_y) * nx + at_x
                for core, left, right in ((own_c, part_a, part_b), (1 - own_c, from_a, from_b)):
                    row, start = chip * 2 + core, 0
                    for out, width in zip(outs, widths):
                        half = width // 2
                        out[row, :, :half] = left[ky, kx, kz, :, start : start + half]
                        out[row, :, half:] = right[kx, ky, kz, :, start : start + half]
                        start += half


def held(values, *others):
    others = [o for o in others if o is not None]
    return lax.optimization_barrier((values, others))[0] if others else values


class Gather:
    def __init__(self, dev, shards):
        self.dev = dev
        self.rows = shards[0].shape[0]
        self.widths = [s.shape[1] for s in shards]
        self.half = sum(self.widths) // 2
        if len(shards) == 1:
            self.local = shards[0]
        else:
            halves = [s.shape[1] // 2 for s in shards]
            self.local = jnp.concatenate(
                [s[:, :h] for s, h in zip(shards, halves)]
                + [s[:, h:] for s, h in zip(shards, halves)],
                axis=1,
            )

    def along_z(self, *after):
        self.arrived = self.dev.copies(held(self.local, *after), "z")
        return self.arrived

    def first(self, *after):
        line = jnp.stack(held(self.arrived, *after))
        part_a, part_b = line[:, :, : self.half], line[:, :, self.half :]
        self.sent = [part_a, part_b]
        self.arrived = self.dev.copies(part_a, "x"), self.dev.copies(part_b, "y")
        return self.arrived[0] + self.arrived[1]

    def second(self, *after):
        part_a, part_b = (jnp.stack(v) for v in held(self.arrived, *after))
        self.sent = [part_a, part_b]
        self.arrived = self.dev.copies(part_a, "y"), self.dev.copies(part_b, "x")
        return self.arrived[0] + self.arrived[1]

    def swap(self, *after):
        self.part_a, self.part_b = (jnp.stack(v) for v in held(self.arrived, *after))
        self.sent = [self.part_a, self.part_b]
        self.from_a = self.dev.shift(self.part_a, "c", 1)
        self.from_b = self.dev.shift(self.part_b, "c", 1)
        return [self.from_a, self.from_b]

    def result(self, place):
        dev, rows = self.dev, self.rows
        sizes = (dev.size["z"], dev.size["y"], dev.size["x"])
        kind = self.local.dtype
        outs = pl.pallas_call(
            functools.partial(assemble_kernel, sizes, self.widths),
            name="assemble",
            out_shape=[jax.ShapeDtypeStruct((dev.count, rows, w), kind) for w in self.widths],
            in_specs=[SMEM] + [VMEM] * 4,
            out_specs=[VMEM] * len(self.widths),
            compiler_params=params(),
            cost_estimate=cost(0, 4 * dev.count * rows * sum(self.widths)),
        )(place, self.part_a, self.part_b, self.from_a, self.from_b)
        return [o.reshape(dev.count * rows, w) for o, w in zip(outs, self.widths)]


def chip_sum_kernel(sizes, pairs, place, *refs):
    nz, ny, nx = sizes
    owns, gots, outs = refs[:pairs], refs[pairs : 2 * pairs], refs[2 * pairs :]
    own_y, own_x = place[1], place[2]
    for ky in range(ny):
        for kx in range(nx):
            at = lax.rem(own_y + ky, ny) * nx + lax.rem(own_x + kx, nx)
            for z in range(nz):
                start = 0
                for own, got in zip(owns, gots):
                    width = own.shape[-1]
                    chip = z * ny * nx + at
                    total = own[chip].astype(F32) + got[chip].astype(F32)
                    outs[ky * nx + kx][z, :, start : start + width] = total.astype(BF)
                    start += width


class Scatter:
    def __init__(self, dev, pairs, place):
        self.dev, self.place = dev, place
        self.own = [p[0] for p in pairs]
        self.sent = [p[1] for p in pairs]
        self.rows = self.own[0].shape[1]
        self.widths = [p[0].shape[2] for p in pairs]
        self.got = []

    def swap(self, *after):
        waiting = held(self.sent[len(self.got) :], *after)
        found = [self.dev.shift(v, "c", 1) for v in waiting]
        self.got = self.got + found
        return found

    def more(self, own, sent):
        self.own, self.sent = self.own + [own], self.sent + [sent]
        self.widths = self.widths + [own.shape[2]]

    def add(self, *after):
        self.got = held(self.got, *after)
        dev, rows = self.dev, self.rows
        sizes = (dev.size["z"], dev.size["y"], dev.size["x"])
        plane, width = sizes[1] * sizes[2], sum(self.widths)
        pairs, chips = len(self.own), dev.count // 2
        self.steps = next(n for n in (4, 3, 2, 1) if all(w % (128 * n) == 0 for w in self.widths))
        tiles = [w // self.steps for w in self.widths]
        halves = [pl.BlockSpec((chips, rows, t), lambda i: (0, 0, i)) for t in tiles]
        out_tile = pl.BlockSpec((sizes[0], rows, sum(tiles)), lambda i: (0, 0, i))
        self.blocks = pl.pallas_call(
            functools.partial(chip_sum_kernel, sizes, pairs),
            name="chip_sum",
            grid=(self.steps,),
            out_shape=[jax.ShapeDtypeStruct((sizes[0], rows, width), BF)] * plane,
            in_specs=[SMEM] + halves + halves,
            out_specs=[out_tile] * plane,
            compiler_params=params(),
            cost_estimate=cost(0, 6 * dev.count // 2 * rows * width),
        )(self.place, *self.own, *self.got)
        self.terms = [self.blocks[0]]
        return self.blocks

    def near(self, *after):
        return self._plane(lambda ky, kx: ky == 0 or kx == 0, after)

    def far(self, *after):
        return self._plane(lambda ky, kx: ky > 0 and kx > 0, after)

    def _plane(self, chosen, after):
        dev, ny, nx = self.dev, self.dev.size["y"], self.dev.size["x"]
        blocks = held(self.blocks, *after)
        found = [
            dev.shift_plane(blocks[ky * nx + kx], ky, kx)
            for ky in range(ny)
            for kx in range(nx)
            if (ky or kx) and chosen(ky, kx)
        ]
        self.terms += found
        return found


def line_kernel(nz, counts, place, *refs):
    terms, outs = refs[: sum(counts)], refs[sum(counts) :]
    joined = len(outs) == 1
    rows = outs[0].shape[-2]
    for k in range(nz):
        at, first, start = k if joined else lax.rem(place[0] + k, nz), 0, 0
        out = outs[0].at[k] if joined else outs[k]
        for count in counts:
            group = terms[first : first + count]
            total = group[0][at].astype(F32)
            for term in group[1:]:
                total += term[at].astype(F32)
            first, width = first + count, total.shape[1]
            for piece in range(total.shape[0] // rows):
                out[:, start : start + width] = total[piece * rows : (piece + 1) * rows].astype(BF)
                start += width


def finish(dev, place, scatters, joined, *after):
    nz, rows = dev.size["z"], min(s.rows for s in scatters)
    width = sum(w * (s.rows // rows) for s in scatters for w in s.widths)
    terms = held([t for s in scatters for t in s.terms], *after)
    blocks = pl.pallas_call(
        functools.partial(line_kernel, nz, [len(s.terms) for s in scatters]),
        name="plane_sum",
        out_shape=[jax.ShapeDtypeStruct((nz, rows, width), BF)]
        if joined
        else [jax.ShapeDtypeStruct((rows, width), BF)] * nz,
        in_specs=[SMEM] + [VMEM] * len(terms),
        out_specs=[VMEM] * (1 if joined else nz),
        compiler_params=params(),
        cost_estimate=cost(0, 8 * nz * rows * width),
    )(place, *terms)
    if joined:
        line = lax.all_to_all(
            blocks[0], "dp", 0, 0, axis_index_groups=dev.groups("z"), tiled=True
        )
        return blocks, line
    return blocks, [blocks[0]] + [dev.shift(blocks[k], "z", k) for k in range(1, nz)]


def totals(arrived, scatters):
    if isinstance(arrived, list):
        total = sum(v.astype(F32) for v in arrived)
    else:
        total = jnp.sum(arrived.astype(F32), axis=0)
    rows, start, out = total.shape[0], 0, []
    for s in scatters:
        pieces, width = s.rows // rows, sum(s.widths)
        parts = [total[:, start + i * width : start + (i + 1) * width] for i in range(pieces)]
        whole_rows = parts[0] if pieces == 1 else jnp.concatenate(parts, axis=0)
        start += pieces * width
        tiles, span = [w // s.steps for w in s.widths], width // s.steps
        for t, tile in enumerate(tiles):
            at = sum(tiles[:t])
            found = [whole_rows[:, i * span + at : i * span + at + tile] for i in range(s.steps)]
            out.append(found[0] if len(found) == 1 else jnp.concatenate(found, axis=1))
    return out


def split_cores(value, rows, core, own, sent):
    if rows % 8 == 0:
        parts = value.reshape(-1, 2, rows, value.shape[1])
        own[...] = jnp.where(core == 0, parts[:, 0], parts[:, 1]).astype(BF)
        sent[...] = jnp.where(core == 0, parts[:, 1], parts[:, 0]).astype(BF)
        return
    for chip in range(value.shape[0] // (2 * rows)):
        first = value[2 * chip * rows : (2 * chip + 1) * rows]
        second = value[(2 * chip + 1) * rows : (2 * chip + 2) * rows]
        own[chip] = jnp.where(core == 0, first, second).astype(BF)
        sent[chip] = jnp.where(core == 0, second, first).astype(BF)


def dot(left, right):
    return jnp.dot(left, right, preferred_element_type=F32)


def dot_rows(left, right):
    return lax.dot_general(left, right, (((0,), (0,)), ((), ())), preferred_element_type=F32)


def dot_cols(left, right):
    return lax.dot_general(left, right, (((1,), (1,)), ((), ())), preferred_element_type=F32)


def one_hot(column, row):
    return jnp.where(column == row, 1.0, 0.0).astype(BF)


def row_sum(values):
    return jnp.sum(values, axis=0, keepdims=True)


def normalised(values):
    mean = jnp.mean(values, axis=1, keepdims=True)
    centered = values - mean
    variance = jnp.mean(centered * centered, axis=1, keepdims=True)
    scale = lax.rsqrt(variance + NORM_EPS)
    return centered * scale, scale


def norm_back(unit, scale, gain, grad):
    weighted = grad * gain
    first = jnp.mean(weighted, axis=1, keepdims=True)
    second = jnp.mean(weighted * unit, axis=1, keepdims=True)
    return scale * (weighted - first - unit * second)


class Layout:
    def __init__(self, images, slots):
        self.images, self.slots = images, slots
        self.small, self.large = GRID * slots, 4 * GRID * slots
        self.small_pad = -(-self.small // 16) * 16
        self.large_pad = -(-self.large // 16) * 16
        self.starts = [self.large_pad + i * self.small_pad for i in range(images - 1)]
        self.rows = self.large_pad + (images - 1) * self.small_pad

    def rows_of(self, row, big):
        small_id = jnp.maximum(row - self.large_pad, 0) // self.small_pad
        in_large = row < self.large_pad
        offset = jnp.where(in_large, row, row - self.large_pad - small_id * self.small_pad)
        real = offset < jnp.where(in_large, self.large, self.small)
        image = jnp.where(in_large, big, small_id + jnp.where(small_id >= big, 1, 0))
        window = (
            GRID * image + jnp.where(image > big, 3 * GRID, 0) + offset // self.slots
        )
        return window, offset % self.slots, real

    def source(self, row, big):
        window, slot, real = self.rows_of(row, big)
        return jnp.where(real, window * self.slots + slot, -1)

    def place(self, big, count_vec, bucket, lane_slots):
        row = jnp.arange(self.rows, dtype=jnp.int32)
        window, slot, real = self.rows_of(row, big)
        in_large = row < self.large_pad
        small_id = jnp.maximum(row - self.large_pad, 0) // self.small_pad
        image = jnp.where(in_large, big, small_id + jnp.where(small_id >= big, 1, 0))
        kept = jnp.sum(
            jnp.where(
                image[:, None] == jnp.arange(self.images, dtype=jnp.int32)[None, :],
                count_vec[None, :],
                0,
            ),
            axis=1,
        )
        windows = bucket.shape[0]
        target = jnp.sum(
            jnp.where(
                window[:, None] == jnp.arange(windows, dtype=jnp.int32)[None, :], bucket[None, :], 0
            ),
            axis=1,
        )
        return jnp.where(real & (slot < kept), target * lane_slots + slot, -1)

    def key_mask(self, size, real, kept):
        lane = lax.broadcasted_iota(jnp.int32, (1, size), 1)
        live = (lane < real) & (lane % self.slots < kept)
        return jnp.where(live, 0.0, MASK_FILL)


LANE_SLOTS = 8


def slot_targets(info, slots, wins, axis):
    rows = wins * LANE_SLOTS
    shape = (rows, 1) if axis == 0 else (1, rows)
    spread = (rows, wins) if axis == 0 else (wins, rows)
    owner = lax.broadcasted_iota(jnp.int32, spread, axis) // LANE_SLOTS
    window = lax.broadcasted_iota(jnp.int32, spread, 1 - axis)
    pick = jnp.where(owner == window, 1.0, 0.0).astype(BF)
    fields = dot(pick, info) if axis == 0 else dot_rows(info, pick)
    slot = lax.broadcasted_iota(jnp.int32, shape, axis) % LANE_SLOTS
    field = (lambda i: fields[:, i : i + 1]) if axis == 0 else (lambda i: fields[i : i + 1, :])
    cell = jnp.zeros(shape, F32)
    for j in range(slots):
        cell = cell + jnp.where(slot == j, field(4 + j), 0.0)
    first = (lax.broadcasted_iota(jnp.int32, shape, axis) // LANE_SLOTS) * GRID
    live = slot.astype(F32) < field(1)
    return jnp.where(live, first + cell.astype(jnp.int32), -1)


def owner_kernel(slots, wins, cot, info_in, vec_dec, de_out, base_out, sums_out):
    step = pl.program_id(0)
    cells = wins * GRID
    width = cot.shape[1]
    quarter = width // 4
    grads = cot[...]
    info = info_in[...]
    cell_lane = lax.broadcasted_iota(jnp.int32, (1, cells), 1)
    want = slot_targets(info, slots, wins, 0)
    pick = one_hot(want, cell_lane)
    picked = dot(pick, grads)
    de_out[...] = picked.astype(BF)
    taken = jnp.sum(jnp.where(want == cell_lane, 1.0, 0.0), axis=0, keepdims=True)
    window = lax.broadcasted_iota(jnp.int32, (wins, cells), 0)
    inside = jnp.where(
        window == lax.broadcasted_iota(jnp.int32, (wins, cells), 1) // GRID, 1.0, 0.0
    ).astype(BF)
    present_row = dot_rows(info, inside)[0:1, :]
    mask_sum = dot(jnp.broadcast_to(present_row - taken, (8, cells)).astype(BF), grads)[:1]

    cell_row = lax.broadcasted_iota(jnp.int32, (cells, 1), 0)
    filled = jnp.sum(
        jnp.where(cell_row == slot_targets(info, slots, wins, 1), 1.0, 0.0), axis=1, keepdims=True
    )
    owner = lax.broadcasted_iota(jnp.int32, (cells, wins), 0) // GRID
    fields = dot(one_hot(owner, lax.broadcasted_iota(jnp.int32, (cells, wins), 1)), info)
    present = fields[:, 0:1]
    turn = fields[:, 2:3].astype(jnp.int32)
    wide = fields[:, 3:4] > GRID
    cell = cell_row % GRID
    along = jnp.where(wide, (turn % 2) * GRID + cell, cell)
    across = jnp.where(wide, turn // 2, turn)
    depth = 32
    place = lax.broadcasted_iota(jnp.int32, (depth, quarter), 0).astype(F32)
    index = lax.broadcasted_iota(jnp.int32, (depth, quarter), 1).astype(F32) / quarter
    angle = place * (1.0 / jnp.exp(index * jnp.log(F32(10000.0))))
    table = jnp.concatenate([jnp.sin(angle), jnp.cos(angle)], axis=1)
    high = table.astype(BF)
    rest = table - high.astype(F32)
    middle = rest.astype(BF)
    low = (rest - middle.astype(F32)).astype(BF)
    stacked = jnp.concatenate([high, middle, low], axis=0)
    lane = lax.broadcasted_iota(jnp.int32, (1, 3 * depth), 1) % depth
    shown = present > 0.5
    first = dot(one_hot(jnp.where(shown, along, -1), lane), stacked)
    second = dot(one_hot(jnp.where(shown, across, -1), lane), stacked)
    bare = present - filled
    base_out[:, : 2 * quarter] = first + bare * vec_dec[1:2, : 2 * quarter]
    base_out[:, 2 * quarter :] = second + bare * vec_dec[1:2, 2 * quarter :]

    @pl.when(step == 0)
    def _():
        sums_out[...] = jnp.zeros_like(sums_out)

    sums_out[0:1, :] += row_sum(picked)
    sums_out[1:2, :] += mask_sum


def decode_kernel(slots, wins, got, info_in, base, out):
    cell_row = lax.broadcasted_iota(jnp.int32, (wins * GRID, 1), 0)
    want = slot_targets(info_in[...], slots, wins, 1)
    out[...] = (dot(one_hot(cell_row, want), got[...]) + base[...]).astype(BF)


BIG, KEPT = 4, 5


def first_norm_kernel(lay, meta, tokens, vecs, x_out, h_out):
    rows = x_out.shape[0]
    row = lax.broadcasted_iota(jnp.int32, (rows, 1), 0) + pl.program_id(0) * rows
    lane = lax.broadcasted_iota(jnp.int32, (1, tokens.shape[0]), 1)
    moved = dot(one_hot(lay.source(row, meta[BIG]), lane), tokens[...])
    x_out[...] = moved.astype(BF)
    unit, _ = normalised(moved)
    h_out[...] = (unit * vecs[0:1, :] + vecs[1:2, :]).astype(BF)


def softmax_rows(scores):
    top = jnp.max(scores, axis=1, keepdims=True)
    expo = jnp.exp(scores - top)
    return (expo * (1.0 / jnp.sum(expo, axis=1, keepdims=True))).astype(BF)


def attention_kernel(lay, chunk, head_dim, meta, h_in, w_q, w_k, w_v, vecs,
                     q_out, k_out, v_out, pl_out, ps_out, o_out, scores):
    big, small = lay.large_pad, lay.small_pad
    normed = h_in[...]
    q_out[...] = ((dot(normed, w_q[...]) + vecs[2:3, :]) * (head_dim**-0.5)).astype(BF)
    k_out[...] = dot(normed, w_k[...]).astype(BF)
    v_out[...] = (dot(normed, w_v[...]) + vecs[3:4, :]).astype(BF)
    lane = lax.broadcasted_iota(jnp.int32, (1, 2 * head_dim), 1)
    low = lane < head_dim
    halves = (jnp.where(low, 1.0, 0.0).astype(BF), jnp.where(low, 0.0, 1.0).astype(BF))
    mask_l = lay.key_mask(big, lay.large, meta[KEPT])
    masks = [lay.key_mask(small, lay.small, meta[KEPT + 1 + i]) for i in range(lay.images - 1)]
    for pair in range(q_out.shape[1] // (2 * head_dim)):
        cols = slice(pair * 2 * head_dim, (pair + 1) * 2 * head_dim)
        first = []
        for half in range(2):
            head = 2 * pair + half
            query = q_out[:big, cols] * halves[half]
            scores[...] = dot_cols(query, k_out[:big, cols])
            for start in range(0, big, chunk):
                part = scores[start : start + chunk, :] + mask_l
                pl_out[head, start : start + chunk, :] = softmax_rows(part)
            outs = [dot(pl_out[head], v_out[:big, cols])]
            for i, start in enumerate(lay.starts):
                rows = slice(start, start + small)
                query = q_out[rows, cols] * halves[half]
                part = dot_cols(query, k_out[rows, cols]) + masks[i]
                weights = softmax_rows(part)
                ps_out[head, i] = weights
                outs.append(dot(weights, v_out[rows, cols]))
            if half == 0:
                first = outs
        spans = [(0, big)] + [(s, small) for s in lay.starts]
        for (start, size), left, right in zip(spans, first, outs):
            o_out[start : start + size, cols] = jnp.where(low, left, right).astype(BF)


def out_kernel(parts, *refs):
    o_in = refs[:parts]
    w_out, vecs, x_in, r_out, h_out = refs[parts:]
    residual = x_in[...].astype(F32) + vecs[4:5, :]
    width = o_in[0].shape[1]
    for i, o in enumerate(o_in):
        residual += dot(o[...], w_out[i * width : (i + 1) * width, :])
    r_out[...] = residual
    unit, _ = normalised(residual)
    h_out[...] = (unit * vecs[5:6, :] + vecs[6:7, :]).astype(BF)


def fc1_kernel(chunk, h_in, weight, bias, g_out, d_out, hidden):
    hidden[...] = dot(h_in[...], weight[...])
    for start in range(0, hidden.shape[0], chunk):
        rows = slice(start, start + chunk)
        u = hidden[rows, :] + bias[...]
        half = 0.5 + 0.5 * lax.erf(u * (0.5**0.5))
        g_out[rows, :] = (u * half).astype(BF)
        density = jnp.exp(u * u * -0.5) * 0.3989422804014327
        d_out[rows, :] = (half + u * density).astype(BF)


def fc2_kernel(g_one, g_two, w_two, vecs, r_in, w_dec, w_dec_more, vec_dec, place, y_out, e_out, kept):
    step = pl.program_id(0)
    rows, half = g_one.shape
    y = r_in[...] + dot(g_one[...], w_two[:half, :]) + dot(g_two[...], w_two[half:, :])
    y = (y + vecs[7:8, :]).astype(BF)
    y_out[...] = y
    kept[pl.ds(pl.multiple_of(step * rows, rows), rows), :] = (
        dot(y, jnp.concatenate([w_dec[...], w_dec_more[...]], axis=1)) + vec_dec[0:1, :]
    ).astype(BF)

    @pl.when(step == pl.num_programs(0) - 1)
    def _():
        target = lax.broadcasted_iota(jnp.int32, (e_out.shape[0], 1), 0)
        e_out[...] = dot(one_hot(target, place[...]), kept[...]).astype(BF)


def dec_back_kernel(rows, spot, got, place, w_dec, w_dec_more, y_in, dy_out, own_out, sent_out, db_out):
    target = lax.broadcasted_iota(jnp.int32, (got.shape[0], 1), 0)
    grad = dot_rows(one_hot(target, place[...]), got[...]).astype(BF)
    half = w_dec.shape[1]
    dy = dot_cols(grad[:, :half], w_dec[...]) + dot_cols(grad[:, half:], w_dec_more[...])
    dy = dy.astype(BF)
    dy_out[...] = dy
    split_cores(dot_rows(y_in[...], grad), rows, spot[3], own_out, sent_out)
    db_out[...] = row_sum(dy.astype(F32))


def fc2_back_kernel(rows, spot, dy_in, w_two, g_one, d_one, g_two, d_two, du_out, own_out, sent_out, db_out):
    dy = dy_in[...]
    early = pl.program_id(0) < 2
    slope = jnp.where(early, d_one[...], d_two[...]).astype(F32)
    du = (dot_cols(dy, w_two[...]) * slope).astype(BF)
    du_out[...] = du
    db_out[...] = row_sum(du.astype(F32))
    split_cores(
        dot_rows(jnp.where(early, g_one[...], g_two[...]), dy), rows, spot[3], own_out, sent_out
    )


def fc1_back_kernel(rows, spot, du_in, w_one, h_in, dh_out, own_out, sent_out, turned):
    step = pl.program_id(0)

    @pl.when(step == 0)
    def _():
        turned[...] = h_in[...].T
        dh_out[...] = jnp.zeros_like(dh_out)

    du = du_in[...]
    split_cores(dot(turned[...], du), rows, spot[3], own_out, sent_out)
    dh_out[...] += dot_cols(du, w_one[...])


def out_back_kernel(rows, parts, spot, dh_one, dh_two, r_in, dy_in, vecs, w_out, *refs):
    o_in = refs[:parts]
    dr_out, do_out, own_out, sent_out, sums, total = refs[parts:]
    step = pl.program_id(0)
    unit, scale = normalised(r_in[...])
    grad = dh_one[...] + dh_two[...]
    dr = dy_in[...].astype(F32) + norm_back(unit, scale, vecs[5:6, :], grad)
    dr_out[...] = dr
    da = dr.astype(BF)
    do_out[...] = dot_cols(da, w_out[...]).astype(BF)

    @pl.when(step == 0)
    def _():
        sums[...] = jnp.zeros_like(sums)
        total[...] = jnp.zeros_like(total)

    sums[0:1, :] += row_sum(grad * unit)
    sums[1:2, :] += row_sum(grad)
    sums[2:3, :] += row_sum(da.astype(F32))
    width = o_in[0].shape[1]
    for i, o in enumerate(o_in):
        total[i * width : (i + 1) * width, :] += dot_rows(o[...], da)

    @pl.when(step == pl.num_programs(0) - 1)
    def _():
        split_cores(total[...], rows, spot[3], own_out, sent_out)


def attention_back_kernel(rows_dev, lay, chunk, head_dim, spot, h_in, q_in, k_in, v_in, pl_in, ps_in, do_in,
                          dq_out, dk_out, dv_out, own_out, sent_out, sums, scores, ds_big):
    big, small = lay.large_pad, lay.small_pad
    lane = lax.broadcasted_iota(jnp.int32, (1, 2 * head_dim), 1)
    low = lane < head_dim
    halves = (jnp.where(low, 1.0, 0.0).astype(BF), jnp.where(low, 0.0, 1.0).astype(BF))

    def back_rows(weights, grad):
        p = weights.astype(F32)
        inner = jnp.sum(grad * p, axis=1, keepdims=True)
        return (p * (grad - inner)).astype(BF)

    for pair in range(q_in.shape[1] // (2 * head_dim)):
        cols = slice(pair * 2 * head_dim, (pair + 1) * 2 * head_dim)
        spans = [(0, big)] + [(s, small) for s in lay.starts]
        first = []
        for half in range(2):
            head = 2 * pair + half
            found = []
            for i, (start, size) in enumerate(spans):
                rows = slice(start, start + size)
                grad_o = do_in[rows, cols] * halves[half]
                if i == 0:
                    scores[...] = dot_cols(grad_o, v_in[rows, cols])
                    for s in range(0, big, chunk):
                        ds_big[s : s + chunk, :] = back_rows(
                            pl_in[head, s : s + chunk, :], scores[s : s + chunk, :]
                        )
                    weights, ds = pl_in[head], ds_big[...]
                else:
                    weights = ps_in[head, i - 1]
                    ds = back_rows(weights, dot_cols(grad_o, v_in[rows, cols]))
                found.append(
                    (
                        dot(ds, k_in[rows, cols]),
                        dot_rows(ds, q_in[rows, cols]),
                        dot_rows(weights, do_in[rows, cols]),
                    )
                )
            if half == 0:
                first = found
        for (start, size), left, right in zip(spans, first, found):
            rows = slice(start, start + size)
            dq_out[rows, cols] = (
                jnp.where(low, left[0], right[0]) * (head_dim**-0.5)
            ).astype(BF)
            dk_out[rows, cols] = jnp.where(low, left[1], right[1]).astype(BF)
            dv_out[rows, cols] = jnp.where(low, left[2], right[2]).astype(BF)
    turned = h_in[...].T
    width = dq_out.shape[1]
    for i, grad in enumerate((dq_out, dk_out, dv_out)):
        cols = slice(i * width, (i + 1) * width)
        split_cores(
            dot(turned, grad[...]), rows_dev, spot[3], own_out.at[:, :, cols], sent_out.at[:, :, cols]
        )
    sums[0:1, :] = row_sum(dq_out[...].astype(F32))
    sums[1:2, :] = row_sum(dv_out[...].astype(F32))


def first_back_kernel(lay, parts, meta, *refs):
    grads, more = refs[: 3 * parts], refs[3 * parts : 4 * parts]
    w_qkv, x_in, dr_in, vecs, sums_two, db_two, out, sums, kept = refs[4 * parts :]
    step = pl.program_id(0)
    rows = x_in.shape[0]
    width = grads[0].shape[1]
    grad = dot_cols(grads[0][...], w_qkv[:, :width])
    for i in range(1, 3 * parts):
        grad += dot_cols(grads[i][...], w_qkv[:, i * width : (i + 1) * width])
    unit, scale = normalised(x_in[...].astype(F32))
    moved = dr_in[...] + norm_back(unit, scale, vecs[0:1, :], grad)
    kept[pl.ds(pl.multiple_of(step * rows, rows), rows), :] = moved.astype(BF)

    @pl.when(step == 0)
    def _():
        sums[...] = jnp.zeros_like(sums)
        for i, part in enumerate(more):
            sums[2:4, i * width : (i + 1) * width] = part[0:2, :]
        sums[4:5, :] = sums_two[2:3, :]
        sums[5:7, :] = sums_two[0:2, :]
        sums[7:8, :] = db_two[...]

    sums[0:1, :] += row_sum(grad * unit)
    sums[1:2, :] += row_sum(grad)

    @pl.when(step == pl.num_programs(0) - 1)
    def _():
        slot = lax.broadcasted_iota(jnp.int32, (out.shape[0], 1), 0)
        row = lax.broadcasted_iota(jnp.int32, (1, lay.rows), 1)
        out[...] = dot(one_hot(slot, lay.source(row, meta[BIG])), kept[...]).astype(BF)


def owner_rank(owner_vec):
    window_ids = jnp.arange(owner_vec.shape[0], dtype=jnp.int32)
    earlier = (owner_vec[:, None] == owner_vec[None, :]) & (
        window_ids[None, :] < window_ids[:, None]
    )
    return jnp.sum(earlier.astype(jnp.int32), axis=1)


def spec(shape, index):
    return pl.BlockSpec(shape, index)


def local(tokens, ln1_gain, ln1_bias, qkv_weight, query_bias, value_bias, out_weight, out_bias,
          ln2_gain, ln2_bias, fc1_weight, fc1_bias, fc2_weight, fc2_bias, dec_weight, dec_bias,
          mask_token, kept_offsets, kept_count, res_id, dec_owner, dec_cot):
    count = lax.axis_size("dp")
    dev = Slice(count)
    vis, D = tokens.shape
    dec_width = dec_cot.shape[1]
    windows, slots = kept_offsets.shape
    images = res_id.shape[0]
    hidden = fc1_weight.shape[1]
    head_dim = D // HEADS
    per_peer = (windows + count - 1) // count
    total = count * per_peer
    lay = Layout(images, slots)
    R = lay.rows
    sd = jax.ShapeDtypeStruct

    ga, gc = Gather(dev, [qkv_weight]), Gather(dev, [fc2_weight])
    za = ga.along_z()
    rest = lax.all_gather(
        jnp.concatenate([fc1_weight, out_weight, dec_weight], axis=1), "dp", axis=0, tiled=True
    )
    image_ids = jnp.arange(images, dtype=jnp.int32)
    big = jnp.sum(image_ids * res_id)
    kept_big = jnp.sum(res_id * kept_count)
    kept_small = jnp.where(image_ids[:-1] < big, kept_count[:-1], kept_count[1:])
    meta = jnp.concatenate(
        [jnp.stack([dev.coord(axis) for axis in "zyxc"] + [big, kept_big]), kept_small]
    ).astype(jnp.int32)
    bucket = dec_owner * per_peer + owner_rank(dec_owner)
    place_row = lay.place(big, kept_count, bucket, LANE_SLOTS)[None, :]
    win = jnp.arange(windows, dtype=jnp.int32)
    big_start = GRID * big
    in_big = (win >= big_start) & (win < big_start + 4 * GRID)
    after = win >= big_start + 4 * GRID
    image_win = jnp.where(in_big, big, jnp.where(after, win // GRID - 3, win // GRID))
    in_image = jnp.where(in_big, win - big_start, win % GRID)
    kept_win = jnp.sum(
        jnp.where(image_win[:, None] == image_ids[None, :], kept_count[None, :], 0), axis=1
    )
    side_win = jnp.where(in_big, 2 * GRID, GRID)
    info = jnp.concatenate(
        [jnp.stack([jnp.ones_like(win), kept_win, in_image, side_win], axis=1), kept_offsets], axis=1
    )
    xa = ga.first(bucket)
    bucket = held(bucket, *ga.sent)
    slot_of = jnp.arange(total, dtype=jnp.int32)
    info_send = jnp.sum(
        jnp.where((slot_of[:, None] == bucket[None, :])[:, :, None], info[None, :, :], 0), axis=1
    )
    eight = [ln1_gain, ln1_bias, query_bias, value_bias, out_bias, ln2_gain, ln2_bias, fc2_bias]
    vectors = eight + [fc1_bias, dec_bias, mask_token]
    wide = max(fc1_bias.shape[0], 128)
    line = lambda v: jnp.pad(v, (0, wide - v.shape[0]))[None, :]
    sheet = jnp.concatenate([line(v) for v in vectors], axis=0)
    fields = info_send.shape[1]
    info_block = jnp.pad(info_send.astype(BF), ((0, 0), (0, wide - fields)))
    packed = jnp.concatenate(
        [
            jnp.broadcast_to(sheet[None], (count,) + sheet.shape),
            info_block.reshape(count, per_peer, wide),
        ],
        axis=1,
    )
    ya = ga.second(packed)
    packed = lax.all_to_all(packed, "dp", 0, 0, tiled=True)
    n_vec = eight[0].shape[0]
    vecs = packed[:, :8, :n_vec].transpose(1, 0, 2).reshape(8, D).astype(F32)
    bf1 = packed[:, 8, : fc1_bias.shape[0]].reshape(1, hidden).astype(F32)
    vec_dec = packed[:, 9:11, : dec_bias.shape[0]].transpose(1, 0, 2).reshape(2, dec_width).astype(F32)
    info_got = packed[:, 11:, :fields].reshape(total, fields)

    w_out_spec = spec((D, D), lambda *_: (0, hidden // D))
    first_dec, dec_half = 2 * (hidden + D) // dec_width, dec_width // 2
    w_dec_specs = [spec((D, dec_half), lambda *_, i=i: (0, first_dec + i)) for i in range(2)]
    tile = R // 3
    rows_of = lambda width: spec((tile, width), lambda i: (i, 0))
    x_rows, h_one = pl.pallas_call(
        functools.partial(first_norm_kernel, lay),
        name="first_norm",
        grid=(3,),
        in_specs=[SMEM, whole((vis, D)), whole((8, D))],
        out_specs=[rows_of(D), rows_of(D)],
        out_shape=[sd((R, D), BF), sd((R, D), BF)],
        compiler_params=params(),
        cost_estimate=cost(2 * R * vis * D, 4e6),
    )(meta, held(tokens, za), vecs)

    wins = 16
    steps = total // wins
    cells_w, rows_w = wins * GRID, wins * LANE_SLOTS
    by_step = lambda height, width: spec((height, width), lambda i: (i, 0))
    info_spec = by_step(wins, info_got.shape[1])
    de_send, base, owner_sums = pl.pallas_call(
        functools.partial(owner_kernel, slots, wins),
        name="owner_side",
        grid=(steps,),
        in_specs=[by_step(cells_w, dec_width), info_spec, whole((2, dec_width))],
        out_specs=[by_step(rows_w, dec_width), by_step(cells_w, dec_width), whole((8, dec_width))],
        out_shape=[sd((total * LANE_SLOTS, dec_width), BF), sd((total * GRID, dec_width), F32),
                   sd((8, dec_width), F32)],
        compiler_params=params(),
        cost_estimate=cost(4e9, 8e6, 1e5),
    )(dec_cot, held(info_got, h_one, *xa), vec_dec)

    from_a = ga.swap(de_send, h_one)
    zc = gc.along_z(*ya)
    (w_qkv,) = ga.result(meta)
    de_got = lax.all_to_all(
        held(de_send, *from_a).reshape(count, per_peer * LANE_SLOTS, dec_width), "dp", 0, 0, tiled=True
    ).reshape(total * LANE_SLOTS, dec_width)

    group = 4
    parts = HEADS // group
    gw = group * head_dim
    chunk = lay.large_pad // 5
    p_big_t = sd((group, lay.large_pad, lay.large_pad), BF)
    p_small_t = sd((group, images - 1, lay.small_pad, lay.small_pad), BF)

    def attend(i, h_rows):
        col_of = lambda base_: spec((D, gw), lambda _: (0, base_ * parts + i))
        return pl.pallas_call(
            functools.partial(attention_kernel, lay, chunk, head_dim),
            name="attention",
            grid=(1,),
            in_specs=[SMEM, whole((R, D)), col_of(0), col_of(1), col_of(2),
                      spec((8, gw), lambda _: (0, i))],
            out_specs=[whole((R, gw))] * 3 + [whole(p_big_t.shape), whole(p_small_t.shape), whole((R, gw))],
            out_shape=[sd((R, gw), BF)] * 3 + [p_big_t, p_small_t, sd((R, gw), BF)],
            scratch_shapes=[pltpu.VMEM((lay.large_pad, lay.large_pad), F32)],
            compiler_params=params(),
            cost_estimate=cost(2 * R * D * D + 2e9, 8e6, 1e6),
        )(meta, h_rows, w_qkv, w_qkv, w_qkv, vecs)

    attn = [attend(0, h_one)]
    attn.append(attend(1, held(h_one, attn[0][5])))
    gc.first(attn[1][5])
    attn.append(attend(2, held(h_one, attn[1][5], *gc.sent)))
    gc.second(attn[2][5])
    att = [a[5] for a in attn]

    r_one, h_two = pl.pallas_call(
        functools.partial(out_kernel, parts),
        name="out_projection",
        grid=(3,),
        in_specs=[rows_of(gw)] * parts
        + [w_out_spec, whole((8, D)), rows_of(D)],
        out_specs=[rows_of(D), rows_of(D)],
        out_shape=[sd((R, D), F32), sd((R, D), BF)],
        compiler_params=params(),
        cost_estimate=cost(2 * R * D * D, 9e6),
    )(*att, rest, vecs, held(x_rows, *gc.sent))

    ht = hidden // 6

    def feed(i, h_rows):
        return pl.pallas_call(
            functools.partial(fc1_kernel, R // 24),
            name="fc1",
            grid=(3,),
            in_specs=[whole((R, D)), spec((D, ht), lambda j: (0, 3 * i + j)),
                      spec((1, ht), lambda j: (0, 3 * i + j))],
            out_specs=[spec((R, ht), lambda j: (0, j))] * 2,
            out_shape=[sd((R, hidden // 2), BF)] * 2,
            scratch_shapes=[pltpu.VMEM((R, ht), F32)],
            compiler_params=params(),
            cost_estimate=cost(R * D * hidden, 1e7, 3e6),
        )(h_rows, rest, bf1)

    act_0, gelu_0 = feed(0, h_two)
    gc.swap(act_0)
    act_1, gelu_1 = feed(1, held(h_two, act_0, de_got, *gc.sent))
    (w_two,) = gc.result(meta)

    y_rows, e_send = pl.pallas_call(
        fc2_kernel,
        name="fc2_and_embed",
        grid=(3,),
        in_specs=[rows_of(hidden // 2), rows_of(hidden // 2), whole((hidden, D)), whole((8, D)),
                  rows_of(D), *w_dec_specs, whole((2, dec_width)), whole((1, R))],
        out_specs=[rows_of(D), whole((total * LANE_SLOTS, dec_width))],
        out_shape=[sd((R, D), BF), sd((total * LANE_SLOTS, dec_width), BF)],
        scratch_shapes=[pltpu.VMEM((R, dec_width), BF)],
        compiler_params=params(),
        cost_estimate=cost(2 * R * D * hidden + 4 * R * D * dec_width, 2e7),
    )(act_0, act_1, w_two, vecs, r_one, rest, rest, vec_dec, place_row)

    e_got = lax.all_to_all(
        e_send.reshape(count, per_peer * LANE_SLOTS, dec_width), "dp", 0, 0, tiled=True
    ).reshape(total * LANE_SLOTS, dec_width)

    row_dev, row_two = D // count, hidden // count
    chips = count // 2
    dy, own_dec, sent_dec, db_two = pl.pallas_call(
        functools.partial(dec_back_kernel, row_dev),
        name="embed_back",
        grid=(1,),
        in_specs=[SMEM, whole((total * LANE_SLOTS, dec_width)), whole((1, R)), *w_dec_specs, whole((R, D))],
        out_specs=[whole((R, D)), whole((chips, row_dev, dec_width)),
                   whole((chips, row_dev, dec_width)), whole((1, D))],
        out_shape=[sd((R, D), BF), sd((chips, row_dev, dec_width), BF),
                   sd((chips, row_dev, dec_width), BF), sd((1, D), F32)],
        compiler_params=params(),
        cost_estimate=cost(6 * R * D * dec_width, 7e6, weight=20),
    )(meta, de_got, place_row, rest, rest, y_rows)

    ht = hidden // 4
    held_chips = ht // (2 * row_two)
    grad_spec = spec((held_chips, row_two, D), lambda j: (j, 0, 0))
    half_tile = lambda k: spec((R, ht), lambda j: (0, jnp.clip(j - 2 * k, 0, 1)))
    du, own_two, sent_two, db_one = pl.pallas_call(
        functools.partial(fc2_back_kernel, row_two),
        name="fc2_back",
        grid=(4,),
        in_specs=[SMEM, whole((R, D)), spec((ht, D), lambda j: (j, 0)), half_tile(0), half_tile(0),
                  half_tile(1), half_tile(1)],
        out_specs=[spec((R, ht), lambda j: (0, j)), grad_spec, grad_spec,
                   spec((1, ht), lambda j: (0, j))],
        out_shape=[sd((R, hidden), BF), sd((chips, row_two, D), BF), sd((chips, row_two, D), BF),
                   sd((1, hidden), F32)],
        compiler_params=params(),
        cost_estimate=cost(4 * R * D * hidden, 3e7, weight=20),
    )(meta, dy, w_two, act_0, gelu_0, act_1, gelu_1)
    s_two = Scatter(dev, [(own_two, sent_two)], meta)
    c_two = s_two.swap()

    grad_spec = spec((chips, row_dev, ht), lambda j: (0, 0, j))

    def fc1_back(i, du_rows):
        return pl.pallas_call(
            functools.partial(fc1_back_kernel, row_dev),
            name="fc1_back",
            grid=(2,),
            in_specs=[SMEM, spec((R, ht), lambda j: (0, 2 * i + j)),
                      spec((D, ht), lambda j: (0, 2 * i + j)), whole((R, D))],
            out_specs=[whole((R, D)), grad_spec, grad_spec],
            out_shape=[sd((R, D), F32)] + [sd((chips, row_dev, hidden // 2), BF)] * 2,
            scratch_shapes=[pltpu.VMEM((D, R), BF)],
            compiler_params=params(),
            cost_estimate=cost(2 * R * D * hidden, 1.5e7, weight=20),
        )(meta, du_rows, rest, h_two)

    dh_0, own_f0, sent_f0 = fc1_back(0, du)
    s_two.add(dh_0, *c_two)
    near = s_two.near()
    dh_1, own_f1, sent_f1 = fc1_back(1, held(du, dh_0, s_two.blocks[0]))
    s_one = Scatter(dev, [(own_f0, sent_f0), (own_f1, sent_f1), (own_dec, sent_dec)], meta)
    far = s_two.far(dh_1, *near)
    c_one = s_one.swap(dh_1, *near)

    grad_spec = whole((chips, row_dev, D))
    dr, d_att, own_out, sent_out, sums_two = pl.pallas_call(
        functools.partial(out_back_kernel, row_dev, parts),
        name="out_back",
        grid=(3,),
        in_specs=[SMEM, rows_of(D), rows_of(D), rows_of(D), rows_of(D), whole((8, D)), w_out_spec]
        + [rows_of(gw)] * parts,
        out_specs=[rows_of(D), rows_of(D), grad_spec, grad_spec, whole((8, D))],
        out_shape=[sd((R, D), F32), sd((R, D), BF)] + [sd((chips, row_dev, D), BF)] * 2
        + [sd((8, D), F32)],
        scratch_shapes=[pltpu.VMEM((D, D), F32)],
        compiler_params=params(),
        cost_estimate=cost(4 * R * D * D, 2e7, weight=20),
    )(meta, dh_0, held(dh_1, *near), r_one, dy, vecs, rest, *att)
    s_one.add(dr, *far, *c_one)
    near = s_one.near()

    def attend_back(i, d_att_rows):
        q_rows, k_rows, v_rows, prob_l, prob_s, _ = attn[i]
        grad_shape = (chips, row_dev, 3 * gw)
        return pl.pallas_call(
            functools.partial(attention_back_kernel, row_dev, lay, chunk, head_dim),
            name="attention_back",
            grid=(1,),
            in_specs=[SMEM, whole((R, D))] + [whole((R, gw))] * 3
            + [whole(p_big_t.shape), whole(p_small_t.shape), spec((R, gw), lambda _: (0, i))],
            out_specs=[whole((R, gw))] * 3 + [whole(grad_shape)] * 2 + [whole((8, gw))],
            out_shape=[sd((R, gw), BF)] * 3 + [sd(grad_shape, BF)] * 2 + [sd((8, gw), F32)],
            scratch_shapes=[pltpu.VMEM((lay.large_pad, lay.large_pad), F32),
                            pltpu.VMEM((lay.large_pad, lay.large_pad), BF)],
            compiler_params=params(),
            cost_estimate=cost(2 * R * D * D + 3e9, 1e7, weight=20),
        )(meta, h_one, q_rows, k_rows, v_rows, prob_l, prob_s, d_att_rows)

    back = [attend_back(0, held(d_att, s_one.blocks[0], *far))]
    far = s_one.far(back[0][0], *near)
    s_mid = Scatter(dev, [(own_out, sent_out), back[0][3:5]], meta)
    c_mid = s_mid.swap(back[0][0], *near)
    back.append(attend_back(1, held(d_att, back[0][0], *near)))
    s_mid.add(back[1][0], *far, *c_mid)
    near = s_mid.near()
    lines_early, z_early = finish(dev, meta, [s_two, s_one], True, back[1][0], s_mid.blocks[0])
    s_last = Scatter(dev, [back[1][3:5]], meta)
    c_last = s_last.swap(back[1][0], *far)
    back.append(attend_back(2, held(d_att, back[1][0], s_mid.blocks[0], lines_early[0])))
    s_last.more(*back[2][3:5])
    c_last += s_last.swap(back[2][0], *near, *c_last)
    far = s_mid.far(back[2][0], *near)

    decoded = pl.pallas_call(
        functools.partial(decode_kernel, slots, wins),
        name="decode",
        grid=(steps,),
        in_specs=[by_step(rows_w, dec_width), info_spec, by_step(cells_w, dec_width)],
        out_specs=by_step(cells_w, dec_width),
        out_shape=sd((total * GRID, dec_width), BF),
        compiler_params=params(),
        cost_estimate=cost(1e9, 7e6, weight=20),
    )(held(e_got, back[2][0], *near), info_got, base)
    s_last.add(decoded, *far, *c_last)
    near = s_last.near() + s_last.far()

    dqkv = [b[i] for i in range(3) for b in back]
    grad_tokens, sums = pl.pallas_call(
        functools.partial(first_back_kernel, lay, parts),
        name="first_back",
        grid=(3,),
        in_specs=[SMEM] + [rows_of(gw)] * (3 * parts) + [whole((8, gw))] * parts
        + [whole((D, 3 * D)), rows_of(D), rows_of(D), whole((8, D)), whole((8, D)), whole((1, D))],
        out_specs=[whole((vis, D)), whole((8, D))],
        out_shape=[sd((vis, D), BF), sd((8, D), F32)],
        scratch_shapes=[pltpu.VMEM((R, D), BF)],
        compiler_params=params(),
        cost_estimate=cost(2 * R * D * 3 * D + 2 * R * vis * D, 2e7, weight=20),
    )(meta, *dqkv, *[b[5] for b in back], w_qkv, x_rows, held(dr, s_last.blocks[0], z_early), vecs, sums_two,
      db_two)

    rows = jnp.concatenate(
        [
            sums.reshape(8, count, -1).transpose(1, 0, 2).reshape(count, -1),
            db_one.reshape(count, -1),
            owner_sums[:2].reshape(2, count, -1).transpose(1, 0, 2).reshape(count, -1),
        ],
        axis=1,
    )
    lines_late, z_late = finish(dev, meta, [s_mid, s_last], False, grad_tokens, *near)
    rows = lax.all_to_all(held(rows, lines_late[0]), "dp", 0, 0, tiled=True)
    rows = jnp.sum(rows, axis=0)
    grad_two, grad_f0, grad_f1, grad_dec = totals(z_early, [s_two, s_one])
    grad_one = jnp.concatenate([grad_f0, grad_f1], axis=1)
    grad_out, *grads_qkv = totals(z_late, [s_mid, s_last])
    grad_qkv = jnp.concatenate(
        [g[:, i * gw : (i + 1) * gw] for i in range(3) for g in grads_qkv], axis=1
    )
    vec_grads, start = [], 0
    for v in vectors:
        vec_grads.append(rows[start : start + v.shape[0]])
        start += v.shape[0]
    (gg1, gb1, gbq, gbv, gbo, gg2, gb2, gbf2, gbf1, gbdec, gmask) = vec_grads
    return (decoded, grad_tokens, gg1, gb1, grad_qkv, gbq, gbv, grad_out, gbo, gg2, gb2, grad_one,
            gbf1, grad_two, gbf2, grad_dec, gbdec, gmask)


def solution(mesh):
    mat, vec = P("dp", None), P("dp")
    in_specs = (mat, vec, vec, mat, vec, vec, mat, vec, vec, vec, mat, vec, mat, vec, mat, vec, vec,
                mat, vec, vec, vec, mat)
    out_specs = (mat, mat, vec, vec, mat, vec, vec, mat, vec, vec, vec, mat, vec, mat, vec, mat, vec,
                 vec)
    return jax.shard_map(local, mesh=mesh, in_specs=in_specs, out_specs=out_specs, check_vma=False)
```

```python
import functools

import jax
import jax.numpy as jnp
from jax import lax
from jax.experimental import pallas as pl
from jax.experimental.pallas import tpu as pltpu
from jax.sharding import PartitionSpec as P

HEADS = 12
GRID = 14
NORM_EPS = 1e-06
MASK_FILL = -1e30
BF = jnp.bfloat16
F32 = jnp.float32
MIB = 1 << 20


class Slice:
    def __init__(self, count):
        chips = count // 2
        side = 2 if chips <= 16 else 4
        self.count = count
        self.size = {"c": 2, "x": side, "y": side, "z": chips // (side * side)}
        self.stride = {"c": 1, "x": 2, "y": 2 * side, "z": 2 * side * side}

    def coord(self, axis):
        return (lax.axis_index("dp") // self.stride[axis]) % self.size[axis]

    def shift(self, values, axis, steps):
        stride, size = self.stride[axis], self.size[axis]
        pairs = []
        for source in range(self.count):
            place = (source // stride) % size
            pairs.append((source, source + ((place + steps) % size - place) * stride))
        return lax.ppermute(values, "dp", pairs)

    def copies(self, values, axis):
        return [values] + [self.shift(values, axis, k) for k in range(1, self.size[axis])]

    def shift_plane(self, values, ky, kx):
        pairs = []
        for source in range(self.count):
            target = source
            for axis, steps in (("y", ky), ("x", kx)):
                stride, size = self.stride[axis], self.size[axis]
                place = (source // stride) % size
                target += ((place + steps) % size - place) * stride
            pairs.append((source, target))
        return lax.ppermute(values, "dp", pairs)

    def groups(self, axes):
        seen, found = set(), []
        for first in range(self.count):
            if first in seen:
                continue
            members = [first]
            for axis in axes:
                members = [
                    m + k * self.stride[axis] for m in members for k in range(self.size[axis])
                ]
            found.append(members)
            seen.update(members)
        return found


def cost(flops, moved, trans=0, weight=1):
    return pl.CostEstimate(
        flops=int(weight * flops), bytes_accessed=int(weight * moved), transcendentals=int(trans)
    )


def params():
    return pltpu.CompilerParams(vmem_limit_bytes=60 * MIB)


def whole(shape):
    zeros = (0,) * len(shape)
    return pl.BlockSpec(shape, lambda *_: zeros)


SMEM = pl.BlockSpec(memory_space=pltpu.SMEM)
VMEM = pl.BlockSpec(memory_space=pltpu.VMEM)


def assemble_kernel(sizes, widths, place, part_a, part_b, from_a, from_b, *outs):
    _, ny, nx = sizes
    own_y, own_x, own_c = place[1], place[2], place[3]
    for ky in range(ny):
        at_y = lax.rem(own_y - ky + ny, ny)
        for kx in range(nx):
            at_x = lax.rem(own_x - kx + nx, nx)
            chip = at_y * nx + at_x
            for core, left, right in ((own_c, part_a, part_b), (1 - own_c, from_a, from_b)):
                row, start = chip * 2 + core, 0
                for out, width in zip(outs, widths):
                    half = width // 2
                    out[0, row, :, :half] = left[ky, kx, 0, :, start : start + half]
                    out[0, row, :, half:] = right[kx, ky, 0, :, start : start + half]
                    start += half


def held(values, *others):
    others = [o for o in others if o is not None]
    return lax.optimization_barrier((values, others))[0] if others else values


class Gather:
    def __init__(self, dev, shards):
        self.dev = dev
        self.rows = shards[0].shape[0]
        self.widths = [s.shape[1] for s in shards]
        self.half = sum(self.widths) // 2
        if len(shards) == 1:
            self.local = shards[0]
        else:
            halves = [s.shape[1] // 2 for s in shards]
            self.local = jnp.concatenate(
                [s[:, :h] for s, h in zip(shards, halves)]
                + [s[:, h:] for s, h in zip(shards, halves)],
                axis=1,
            )

    def along_z(self, *after):
        self.arrived = self.dev.copies(held(self.local, *after), "z")
        return self.arrived

    def first(self, *after):
        line = jnp.stack(held(self.arrived, *after))
        part_a, part_b = line[:, :, : self.half], line[:, :, self.half :]
        self.sent = [part_a, part_b]
        self.arrived = self.dev.copies(part_a, "x"), self.dev.copies(part_b, "y")
        return self.arrived[0] + self.arrived[1]

    def second(self, *after):
        part_a, part_b = (jnp.stack(v) for v in held(self.arrived, *after))
        self.sent = [part_a, part_b]
        self.arrived = self.dev.copies(part_a, "y"), self.dev.copies(part_b, "x")
        return self.arrived[0] + self.arrived[1]

    def swap(self, *after):
        self.part_a, self.part_b = (jnp.stack(v) for v in held(self.arrived, *after))
        self.sent = [self.part_a, self.part_b]
        self.from_a = self.dev.shift(self.part_a, "c", 1)
        self.from_b = self.dev.shift(self.part_b, "c", 1)
        return [self.from_a, self.from_b]

    def result(self, place, *after):
        dev, rows = self.dev, self.rows
        nz, ny, nx = sizes = (dev.size["z"], dev.size["y"], dev.size["x"])
        kind = self.local.dtype
        from_a, from_b = held((self.from_a, self.from_b), *after)
        part = pl.BlockSpec((ny, nx, 1, rows, self.half), lambda k, _: (0, 0, k, 0, 0))
        outs = pl.pallas_call(
            functools.partial(assemble_kernel, sizes, self.widths),
            name="assemble",
            grid_spec=pltpu.PrefetchScalarGridSpec(
                num_scalar_prefetch=1,
                grid=(nz,),
                in_specs=[part] * 4,
                out_specs=[
                    pl.BlockSpec(
                        (1, 2 * ny * nx, rows, w), lambda k, at: (lax.rem(at[0] - k + nz, nz), 0, 0, 0)
                    )
                    for w in self.widths
                ],
            ),
            out_shape=[jax.ShapeDtypeStruct((nz, 2 * ny * nx, rows, w), kind) for w in self.widths],
            compiler_params=params(),
            cost_estimate=cost(0, 4 * dev.count * rows * sum(self.widths)),
        )(place, self.part_a, self.part_b, from_a, from_b)
        return [o.reshape(dev.count * rows, w) for o, w in zip(outs, self.widths)]


def chip_sum_kernel(sizes, pairs, place, *refs):
    nz, ny, nx = sizes
    owns, gots, outs = refs[:pairs], refs[pairs : 2 * pairs], refs[2 * pairs :]
    own_y, own_x = place[1], place[2]
    for ky in range(ny):
        for kx in range(nx):
            at = lax.rem(own_y + ky, ny) * nx + lax.rem(own_x + kx, nx)
            for z in range(nz):
                start = 0
                for own, got in zip(owns, gots):
                    width = own.shape[-1]
                    chip = z * ny * nx + at
                    outs[ky * nx + kx][z, :, start : start + width] = own[chip] + got[chip]
                    start += width


class Scatter:
    def __init__(self, dev, pairs, place):
        self.dev, self.place = dev, place
        self.own = [p[0] for p in pairs]
        self.sent = [p[1] for p in pairs]
        self.rows = self.own[0].shape[1]
        self.widths = [p[0].shape[2] for p in pairs]
        self.got = []

    def swap(self, *after):
        waiting = held(self.sent[len(self.got) :], *after)
        found = [self.dev.shift(v, "c", 1) for v in waiting]
        self.got = self.got + found
        return found

    def more(self, own, sent):
        self.own, self.sent = self.own + [own], self.sent + [sent]
        self.widths = self.widths + [own.shape[2]]

    def add(self, *after):
        self.got = held(self.got, *after)
        dev, rows = self.dev, self.rows
        sizes = (dev.size["z"], dev.size["y"], dev.size["x"])
        plane, width = sizes[1] * sizes[2], sum(self.widths)
        pairs, chips = len(self.own), dev.count // 2
        self.steps = next(n for n in (4, 3, 2, 1) if all(w % (128 * n) == 0 for w in self.widths))
        tiles = [w // self.steps for w in self.widths]
        halves = [pl.BlockSpec((chips, rows, t), lambda i: (0, 0, i)) for t in tiles]
        out_tile = pl.BlockSpec((sizes[0], rows, sum(tiles)), lambda i: (0, 0, i))
        self.blocks = pl.pallas_call(
            functools.partial(chip_sum_kernel, sizes, pairs),
            name="chip_sum",
            grid=(self.steps,),
            out_shape=[jax.ShapeDtypeStruct((sizes[0], rows, width), BF)] * plane,
            in_specs=[SMEM] + halves + halves,
            out_specs=[out_tile] * plane,
            compiler_params=params(),
            cost_estimate=cost(0, 6 * dev.count // 2 * rows * width),
        )(self.place, *self.own, *self.got)
        self.terms = [self.blocks[0]]
        return self.blocks

    def near(self, *after):
        return self._plane(lambda ky, kx: ky == 0 or kx == 0, after)

    def far(self, *after):
        return self._plane(lambda ky, kx: ky > 0 and kx > 0, after)

    def _plane(self, chosen, after):
        dev, ny, nx = self.dev, self.dev.size["y"], self.dev.size["x"]
        blocks = held(self.blocks, *after)
        found = [
            dev.shift_plane(blocks[ky * nx + kx], ky, kx)
            for ky in range(ny)
            for kx in range(nx)
            if (ky or kx) and chosen(ky, kx)
        ]
        self.terms += found
        return found


def line_kernel(nz, counts, place, *refs):
    terms, outs = refs[: sum(counts)], refs[sum(counts) :]
    joined = len(outs) == 1
    rows = outs[0].shape[-2]
    for k in range(nz):
        at, first, start = k if joined else lax.rem(place[0] + k, nz), 0, 0
        out = outs[0].at[k] if joined else outs[k]
        for count in counts:
            group = terms[first : first + count]
            total = group[0][at].astype(F32)
            for term in group[1:]:
                total += term[at].astype(F32)
            first, width = first + count, total.shape[1]
            for piece in range(total.shape[0] // rows):
                out[:, start : start + width] = total[piece * rows : (piece + 1) * rows].astype(BF)
                start += width


def finish(dev, place, scatters, joined, *after):
    nz, rows = dev.size["z"], min(s.rows for s in scatters)
    width = sum(w * (s.rows // rows) for s in scatters for w in s.widths)
    terms = held([t for s in scatters for t in s.terms], *after)
    blocks = pl.pallas_call(
        functools.partial(line_kernel, nz, [len(s.terms) for s in scatters]),
        name="plane_sum",
        out_shape=[jax.ShapeDtypeStruct((nz, rows, width), BF)]
        if joined
        else [jax.ShapeDtypeStruct((rows, width), BF)] * nz,
        in_specs=[SMEM] + [VMEM] * len(terms),
        out_specs=[VMEM] * (1 if joined else nz),
        compiler_params=params(),
        cost_estimate=cost(0, 8 * nz * rows * width),
    )(place, *terms)
    if joined:
        line = lax.all_to_all(
            blocks[0], "dp", 0, 0, axis_index_groups=dev.groups("z"), tiled=True
        )
        return blocks, line
    return blocks, [blocks[0]] + [dev.shift(blocks[k], "z", k) for k in range(1, nz)]


def totals(arrived, scatters):
    if isinstance(arrived, list):
        total = sum(v.astype(F32) for v in arrived)
    else:
        total = jnp.sum(arrived.astype(F32), axis=0)
    rows, start, out = total.shape[0], 0, []
    for s in scatters:
        pieces, width = s.rows // rows, sum(s.widths)
        parts = [total[:, start + i * width : start + (i + 1) * width] for i in range(pieces)]
        whole_rows = parts[0] if pieces == 1 else jnp.concatenate(parts, axis=0)
        start += pieces * width
        tiles, span = [w // s.steps for w in s.widths], width // s.steps
        for t, tile in enumerate(tiles):
            at = sum(tiles[:t])
            found = [whole_rows[:, i * span + at : i * span + at + tile] for i in range(s.steps)]
            out.append(found[0] if len(found) == 1 else jnp.concatenate(found, axis=1))
    return out


def last_sums_kernel(moves, *refs):
    terms, outs = refs[:-2], refs[-2:]
    for start, width, out, at in moves:
        total = terms[0][:, start : start + width].astype(F32)
        for term in terms[1:]:
            total += term[:, start : start + width].astype(F32)
        outs[out][:, at : at + width] = total


def last_sums(arrived, scatters, model, head_cols):
    rows, width = arrived[0].shape
    moves, start, first = [], 0, True
    part = -1
    for s in scatters:
        tiles, span = [w // s.steps for w in s.widths], sum(s.widths) // s.steps
        for t, tile in enumerate(tiles):
            part = part if first else part + 1
            for i in range(s.steps):
                source = start + i * span + sum(tiles[:t])
                if first:
                    moves.append((source, tile, 0, i * tile))
                    continue
                piece = min(tile, head_cols)
                for k in range(0, tile, piece):
                    block, inside = divmod(i * tile + k, head_cols)
                    moves.append((source + k, piece, 1, block * model + part * head_cols + inside))
            if first:
                part, first = -1, False
        start += sum(s.widths)
    shapes = [(rows, model), (rows, 3 * model)]
    return pl.pallas_call(
        functools.partial(last_sums_kernel, moves),
        name="last_sums",
        grid=(1,),
        in_specs=[whole((rows, width))] * len(arrived),
        out_specs=[whole(v) for v in shapes],
        out_shape=[jax.ShapeDtypeStruct(v, F32) for v in shapes],
        compiler_params=params(),
    )(*arrived)


def split_cores(value, rows, core, own, sent):
    if rows % 8 == 0:
        parts = value.reshape(-1, 2, rows, value.shape[1])
        own[...] = jnp.where(core == 0, parts[:, 0], parts[:, 1]).astype(BF)
        sent[...] = jnp.where(core == 0, parts[:, 1], parts[:, 0]).astype(BF)
        return
    for chip in range(value.shape[0] // (2 * rows)):
        first = value[2 * chip * rows : (2 * chip + 1) * rows]
        second = value[(2 * chip + 1) * rows : (2 * chip + 2) * rows]
        own[chip] = jnp.where(core == 0, first, second).astype(BF)
        sent[chip] = jnp.where(core == 0, second, first).astype(BF)


def dot(left, right):
    return jnp.dot(left, right, preferred_element_type=F32)


def dot_rows(left, right):
    return lax.dot_general(left, right, (((0,), (0,)), ((), ())), preferred_element_type=F32)


def dot_cols(left, right):
    return lax.dot_general(left, right, (((1,), (1,)), ((), ())), preferred_element_type=F32)


def one_hot(column, row):
    return jnp.where(column == row, 1.0, 0.0).astype(BF)


def row_sum(values):
    return jnp.sum(values, axis=0, keepdims=True)


def normalised(values):
    mean = jnp.mean(values, axis=1, keepdims=True)
    centered = values - mean
    variance = jnp.mean(centered * centered, axis=1, keepdims=True)
    scale = lax.rsqrt(variance + NORM_EPS)
    return centered * scale, scale


def norm_back(unit, scale, gain, grad):
    weighted = grad * gain
    first = jnp.mean(weighted, axis=1, keepdims=True)
    second = jnp.mean(weighted * unit, axis=1, keepdims=True)
    return scale * (weighted - first - unit * second)


class Layout:
    def __init__(self, images, slots):
        self.images, self.slots = images, slots
        self.small, self.large = GRID * slots, 4 * GRID * slots
        self.small_pad = -(-self.small // 16) * 16
        self.large_pad = -(-self.large // 16) * 16
        self.starts = [self.large_pad + i * self.small_pad for i in range(images - 1)]
        self.rows = self.large_pad + (images - 1) * self.small_pad

    def rows_of(self, row, big):
        small_id = jnp.maximum(row - self.large_pad, 0) // self.small_pad
        in_large = row < self.large_pad
        offset = jnp.where(in_large, row, row - self.large_pad - small_id * self.small_pad)
        real = offset < jnp.where(in_large, self.large, self.small)
        image = jnp.where(in_large, big, small_id + jnp.where(small_id >= big, 1, 0))
        window = (
            GRID * image + jnp.where(image > big, 3 * GRID, 0) + offset // self.slots
        )
        return window, offset % self.slots, real

    def source(self, row, big):
        window, slot, real = self.rows_of(row, big)
        return jnp.where(real, window * self.slots + slot, -1)

    def key_mask(self, size, real, kept):
        lane = lax.broadcasted_iota(jnp.int32, (1, size), 1)
        live = (lane < real) & (lane % self.slots < kept)
        return jnp.where(live, 0.0, MASK_FILL)


LANE_SLOTS = 8
BIG, KEPT = 4, 5
FIELDS = 4


def describe_kernel(lay, dims, per_peer, index, counts, sides, owner_in, offsets_in,
                    meta, place_out, info_out, owners, cells):
    images, slots = lay.images, lay.slots
    windows, padded = offsets_in.shape[0], owners.shape[1]
    _, ny, nx = dims
    me = index[0]
    meta[0] = me // (2 * nx * ny)
    meta[1] = (me // (2 * nx)) % ny
    meta[2] = (me // 2) % nx
    meta[3] = me % 2
    big, kept_big = jnp.int32(0), jnp.int32(0)
    for i in range(images):
        big += i * sides[i]
        kept_big += sides[i] * counts[i]
    meta[BIG] = big
    meta[KEPT] = kept_big
    for i in range(images - 1):
        meta[KEPT + 1 + i] = jnp.where(i < big, counts[i], counts[i + 1])

    owners[...] = jnp.full(owners.shape, -1.0, F32)
    owners[:, :windows] = jnp.broadcast_to(owner_in[...], (8, windows)).astype(F32)
    row = owners[0:1, :]
    col = owners[...].T[:, 0:1]
    before = lax.broadcasted_iota(jnp.int32, (padded, padded), 0)
    after = lax.broadcasted_iota(jnp.int32, (padded, padded), 1)
    same = jnp.where(col == row, 1.0, 0.0)
    rank_row = jnp.sum(jnp.where(before < after, same, 0.0), axis=0, keepdims=True)
    rank_col = jnp.sum(jnp.where(after < before, same, 0.0), axis=1, keepdims=True)
    bucket_row = jnp.where(row >= 0, row * per_peer + rank_row, -1.0)
    bucket_col = jnp.where(col >= 0, col * per_peer + rank_col, -1.0)

    win = lax.broadcasted_iota(jnp.int32, (padded, 1), 0)
    start = GRID * big
    in_big = (win >= start) & (win < start + 4 * GRID)
    image = jnp.where(in_big, big, win // GRID - jnp.where(win >= start + 4 * GRID, 3, 0))
    kept = jnp.zeros((padded, 1), jnp.int32)
    for i in range(images):
        kept = jnp.where(image == i, counts[i], kept)
    cells[...] = jnp.zeros_like(cells)
    cells[:windows, FIELDS : FIELDS + slots] = offsets_in[...].astype(F32)
    lane = lax.broadcasted_iota(jnp.int32, cells.shape, 1)
    turn = jnp.where(in_big, win - start, win % GRID)
    values = jnp.where(lane == 0, 1.0, cells[...])
    values = jnp.where(lane == 1, kept.astype(F32), values)
    values = jnp.where(lane == 2, turn.astype(F32), values)
    values = jnp.where(lane == 3, jnp.where(in_big, 2.0 * GRID, 1.0 * GRID), values)
    target = lax.broadcasted_iota(jnp.int32, (info_out.shape[0], padded), 0).astype(F32)
    info_out[...] = dot(one_hot(target, bucket_row), values.astype(BF)).astype(BF)

    place = lax.broadcasted_iota(jnp.int32, (1, lay.rows), 1)
    window, slot, real = lay.rows_of(place, big)
    found = jnp.sum(
        jnp.where(win == window, bucket_col * LANE_SLOTS, 0.0), axis=0, keepdims=True
    ).astype(jnp.int32)
    bound = jnp.sum(jnp.where(win == window, kept.astype(F32), 0.0), axis=0, keepdims=True)
    live = real & (slot.astype(F32) < bound)
    place_out[...] = jnp.where(live, found + slot, -1)


def slot_targets(info, slots, wins, axis):
    rows = wins * LANE_SLOTS
    shape = (rows, 1) if axis == 0 else (1, rows)
    spread = (rows, wins) if axis == 0 else (wins, rows)
    owner = lax.broadcasted_iota(jnp.int32, spread, axis) // LANE_SLOTS
    window = lax.broadcasted_iota(jnp.int32, spread, 1 - axis)
    pick = jnp.where(owner == window, 1.0, 0.0).astype(BF)
    fields = dot(pick, info) if axis == 0 else dot_rows(info, pick)
    slot = lax.broadcasted_iota(jnp.int32, shape, axis) % LANE_SLOTS
    field = (lambda i: fields[:, i : i + 1]) if axis == 0 else (lambda i: fields[i : i + 1, :])
    cell = jnp.zeros(shape, F32)
    for j in range(slots):
        cell = cell + jnp.where(slot == j, field(4 + j), 0.0)
    first = (lax.broadcasted_iota(jnp.int32, shape, axis) // LANE_SLOTS) * GRID
    live = slot.astype(F32) < field(1)
    return jnp.where(live, first + cell.astype(jnp.int32), -1)


def owner_kernel(slots, wins, cot, info_in, de_out, sums_out):
    step = pl.program_id(0)
    cells = wins * GRID
    grads = cot[...]
    info = info_in[...]
    cell_lane = lax.broadcasted_iota(jnp.int32, (1, cells), 1)
    want = slot_targets(info, slots, wins, 0)
    pick = one_hot(want, cell_lane)
    picked = dot(pick, grads)
    de_out[...] = picked.astype(BF)
    taken = jnp.sum(jnp.where(want == cell_lane, 1.0, 0.0), axis=0, keepdims=True)
    window = lax.broadcasted_iota(jnp.int32, (wins, cells), 0)
    inside = jnp.where(
        window == lax.broadcasted_iota(jnp.int32, (wins, cells), 1) // GRID, 1.0, 0.0
    ).astype(BF)
    present_row = dot_rows(info, inside)[0:1, :]
    mask_sum = dot(jnp.broadcast_to(present_row - taken, (8, cells)).astype(BF), grads)[:1]

    @pl.when(step == 0)
    def _():
        sums_out[...] = jnp.zeros_like(sums_out)

    sums_out[0:1, :] += row_sum(picked)
    sums_out[1:2, :] += mask_sum


def decode_kernel(slots, wins, got, info_in, vec_dec, out, stacked):
    cells = wins * GRID
    quarter = out.shape[1] // 4
    info = info_in[...]
    depth = stacked.shape[0] // 3

    @pl.when(pl.program_id(0) == 0)
    def _():
        place = lax.broadcasted_iota(jnp.int32, (depth, quarter), 0).astype(F32)
        index = lax.broadcasted_iota(jnp.int32, (depth, quarter), 1).astype(F32) / quarter
        angle = place * (1.0 / jnp.exp(index * jnp.log(F32(10000.0))))
        table = jnp.concatenate([jnp.sin(angle), jnp.cos(angle)], axis=1)
        high = table.astype(BF)
        rest = table - high.astype(F32)
        middle = rest.astype(BF)
        stacked[:depth] = high
        stacked[depth : 2 * depth] = middle
        stacked[2 * depth :] = (rest - middle.astype(F32)).astype(BF)

    cell_row = lax.broadcasted_iota(jnp.int32, (cells, 1), 0)
    chosen = one_hot(cell_row, slot_targets(info, slots, wins, 1))
    filled = jnp.sum(chosen.astype(F32), axis=1, keepdims=True)
    placed = dot(chosen, got[...])
    owner = lax.broadcasted_iota(jnp.int32, (cells, wins), 0) // GRID
    fields = dot(one_hot(owner, lax.broadcasted_iota(jnp.int32, (cells, wins), 1)), info)
    present = fields[:, 0:1]
    turn = fields[:, 2:3].astype(jnp.int32)
    wide = fields[:, 3:4] > GRID
    cell = cell_row % GRID
    along = jnp.where(wide, (turn % 2) * GRID + cell, cell)
    across = jnp.where(wide, turn // 2, turn)
    lane = lax.broadcasted_iota(jnp.int32, (1, 3 * depth), 1) % depth
    shown = present > 0.5
    first = dot(one_hot(jnp.where(shown, along, -1), lane), stacked[...])
    second = dot(one_hot(jnp.where(shown, across, -1), lane), stacked[...])
    bare = present - filled
    half = 2 * quarter
    out[:, :half] = (placed[:, :half] + first + bare * vec_dec[1:2, :half]).astype(BF)
    out[:, half:] = (placed[:, half:] + second + bare * vec_dec[1:2, half:]).astype(BF)


def first_norm_kernel(lay, meta, tokens, vecs, x_out, h_out):
    rows = x_out.shape[0]
    row = lax.broadcasted_iota(jnp.int32, (rows, 1), 0) + pl.program_id(0) * rows
    lane = lax.broadcasted_iota(jnp.int32, (1, tokens.shape[0]), 1)
    moved = dot(one_hot(lay.source(row, meta[BIG]), lane), tokens[...])
    x_out[...] = moved.astype(BF)
    unit, _ = normalised(moved)
    h_out[...] = (unit * vecs[0:1, :] + vecs[1:2, :]).astype(BF)


def softmax_rows(scores):
    top = jnp.max(scores, axis=1, keepdims=True)
    expo = jnp.exp(scores - top)
    return (expo * (1.0 / jnp.sum(expo, axis=1, keepdims=True))).astype(BF)


def attention_kernel(lay, chunk, head_dim, meta, h_in, w_q, w_k, w_v, vecs,
                     q_out, k_out, v_out, pl_out, ps_out, o_out, scores):
    big, small = lay.large_pad, lay.small_pad
    normed = h_in[...]
    q_out[...] = ((dot(normed, w_q[...]) + vecs[2:3, :]) * (head_dim**-0.5)).astype(BF)
    k_out[...] = dot(normed, w_k[...]).astype(BF)
    v_out[...] = (dot(normed, w_v[...]) + vecs[3:4, :]).astype(BF)
    lane = lax.broadcasted_iota(jnp.int32, (1, 2 * head_dim), 1)
    low = lane < head_dim
    halves = (jnp.where(low, 1.0, 0.0).astype(BF), jnp.where(low, 0.0, 1.0).astype(BF))
    mask_l = lay.key_mask(big, lay.large, meta[KEPT])
    masks = [lay.key_mask(small, lay.small, meta[KEPT + 1 + i]) for i in range(lay.images - 1)]
    for pair in range(q_out.shape[1] // (2 * head_dim)):
        cols = slice(pair * 2 * head_dim, (pair + 1) * 2 * head_dim)
        both = jnp.concatenate([q_out[:big, cols] * h for h in halves], axis=0)
        scores[...] = dot_cols(both, k_out[:big, cols])
        for half in range(2):
            for start in range(0, big, chunk):
                part = scores[half * big + start : half * big + start + chunk, :] + mask_l
                pl_out[2 * pair + half, start : start + chunk, :] = softmax_rows(part)
        outs = dot(pl_out[2 * pair : 2 * pair + 2].reshape(2 * big, big), v_out[:big, cols])
        o_out[:big, cols] = jnp.where(low, outs[:big], outs[big:]).astype(BF)
        for i, start in enumerate(lay.starts):
            rows = slice(start, start + small)
            both = jnp.concatenate([q_out[rows, cols] * h for h in halves], axis=0)
            weights = softmax_rows(dot_cols(both, k_out[rows, cols]) + masks[i])
            ps_out[2 * pair, i] = weights[:small]
            ps_out[2 * pair + 1, i] = weights[small:]
            outs = dot(weights, v_out[rows, cols])
            o_out[rows, cols] = jnp.where(low, outs[:small], outs[small:]).astype(BF)


def feed_kernel(parts, chunk, *refs):
    o_in = refs[:parts]
    w_out, vecs, x_in, weight, bias, r_out, h_out, g_out, d_out, hidden = refs[parts:]
    rows_all, width = x_in.shape[0], o_in[0].shape[1]

    @pl.when(pl.program_id(0) == 0)
    def _():
        for start in range(0, rows_all, rows_all // 3):
            rows = slice(start, start + rows_all // 3)
            residual = x_in[rows, :].astype(F32) + vecs[4:5, :]
            for i, o in enumerate(o_in):
                residual += dot(o[rows, :], w_out[i * width : (i + 1) * width, :])
            r_out[rows, :] = residual
            unit, _ = normalised(residual)
            h_out[rows, :] = (unit * vecs[5:6, :] + vecs[6:7, :]).astype(BF)

    hidden[...] = dot(h_out[...], weight[...])
    for start in range(0, rows_all, chunk):
        rows = slice(start, start + chunk)
        u = hidden[rows, :] + bias[...]
        half = 0.5 + 0.5 * lax.erf(u * (0.5**0.5))
        g_out[rows, :] = (u * half).astype(BF)
        density = jnp.exp(u * u * -0.5) * 0.3989422804014327
        d_out[rows, :] = (half + u * density).astype(BF)


def join_kernel(rows_dev, sizes, spot, g_in, part_a, part_b, from_a, from_b, vecs, r_in, w_dec, w_dec_more, vec_dec, place, got,
                w_out, e_out, dy_out, own_out, sent_out, db_out, total):
    step = pl.program_id(0)

    @pl.when(step == 0)
    def _():
        total[...] = r_in[...] + vecs[7:8, :]

    _, ny, nx = sizes
    for ky in range(ny):
        for kx in range(nx):
            chip = lax.rem(spot[1] - ky + ny, ny) * nx + lax.rem(spot[2] - kx + nx, nx)
            for core, left, right in ((spot[3], part_a, part_b), (1 - spot[3], from_a, from_b)):
                half = left.shape[-1]
                w_out[chip * 2 + core, :, :half] = left[ky, kx, 0]
                w_out[chip * 2 + core, :, half:] = right[kx, ky, 0]
    total[...] += dot(g_in[...], w_out[...].reshape(g_in.shape[1], total.shape[1]))

    @pl.when(step == pl.num_programs(0) - 1)
    def _():
        half = w_dec.shape[1]
        y = total[...].astype(BF)
        target = lax.broadcasted_iota(jnp.int32, (e_out.shape[0], 1), 0)
        pick = one_hot(target, place[...])
        grad = dot_rows(pick, got[...]).astype(BF)
        for i, w in enumerate((w_dec, w_dec_more)):
            cols = slice(i * half, (i + 1) * half)
            embedded = (dot(y, w[...]) + vec_dec[0:1, cols]).astype(BF)
            e_out[:, cols] = dot(pick, embedded).astype(BF)
        dy = dot_cols(grad[:, :half], w_dec[...]) + dot_cols(grad[:, half:], w_dec_more[...])
        dy = dy.astype(BF)
        dy_out[...] = dy
        split_cores(dot_rows(y, grad), rows_dev, spot[3], own_out, sent_out)
        db_out[...] = row_sum(dy.astype(F32))


def feed_back_kernel(rows_one, rows_two, spot, dy_in, w_two, g_in, d_in, w_one, h_in,
                     dh_out, own_two, sent_two, own_one, sent_one, db_out, turned):
    step = pl.program_id(0)

    @pl.when(step == 0)
    def _():
        turned[...] = h_in[...].T

    dy = dy_in[...]
    du = (dot_cols(dy, w_two[...]) * d_in[...].astype(F32)).astype(BF)
    db_out[...] = row_sum(du.astype(F32))
    split_cores(dot_rows(g_in[...], dy), rows_two, spot[3], own_two, sent_two)
    split_cores(dot(turned[...], du), rows_one, spot[3], own_one, sent_one)
    part = dot_cols(du, w_one[...])

    @pl.when(step == 0)
    def _():
        dh_out[...] = part

    @pl.when(step > 0)
    def _():
        dh_out[...] += part


def out_back_kernel(rows, parts, spot, dh_in, r_in, dy_in, vecs, w_out, *refs):
    o_in = refs[:parts]
    dr_out, do_out, own_out, sent_out, sums, total = refs[parts:]
    step = pl.program_id(0)
    unit, scale = normalised(r_in[...])
    grad = dh_in[...]
    dr = dy_in[...].astype(F32) + norm_back(unit, scale, vecs[5:6, :], grad)
    dr_out[...] = dr
    da = dr.astype(BF)
    do_out[...] = dot_cols(da, w_out[...]).astype(BF)

    @pl.when(step == 0)
    def _():
        sums[...] = jnp.zeros_like(sums)
        total[...] = jnp.zeros_like(total)

    sums[0:1, :] += row_sum(grad * unit)
    sums[1:2, :] += row_sum(grad)
    sums[2:3, :] += row_sum(da.astype(F32))
    width = o_in[0].shape[1]
    for i, o in enumerate(o_in):
        total[i * width : (i + 1) * width, :] += dot_rows(o[...], da)

    @pl.when(step == pl.num_programs(0) - 1)
    def _():
        split_cores(total[...], rows, spot[3], own_out, sent_out)


def attention_back_kernel(rows_dev, lay, chunk, head_dim, spot, h_in, q_in, k_in, v_in, pl_in, ps_in, do_in,
                          dq_out, dk_out, dv_out, own_out, sent_out, sums, scores, ds_big):
    big, small = lay.large_pad, lay.small_pad
    lane = lax.broadcasted_iota(jnp.int32, (1, 2 * head_dim), 1)
    low = lane < head_dim
    halves = (jnp.where(low, 1.0, 0.0).astype(BF), jnp.where(low, 0.0, 1.0).astype(BF))

    def back_rows(weights, grad):
        p = weights.astype(F32)
        inner = jnp.sum(grad * p, axis=1, keepdims=True)
        return (p * (grad - inner)).astype(BF)

    for pair in range(q_in.shape[1] // (2 * head_dim)):
        cols = slice(pair * 2 * head_dim, (pair + 1) * 2 * head_dim)
        both = jnp.concatenate([do_in[:big, cols] * h for h in halves], axis=0)
        scores[...] = dot_cols(both, v_in[:big, cols])
        for half in range(2):
            for at in range(0, big, chunk):
                rows = slice(half * big + at, half * big + at + chunk)
                ds_big[rows, :] = back_rows(pl_in[2 * pair + half, at : at + chunk, :], scores[rows, :])
        spans = [(slice(0, big), None)] + [
            (slice(start, start + small), i) for i, start in enumerate(lay.starts)
        ]
        for rows, i in spans:
            if i is None:
                size, ds = big, ds_big[...]
                weights = (pl_in[2 * pair], pl_in[2 * pair + 1])
            else:
                size = small
                weights = (ps_in[2 * pair, i], ps_in[2 * pair + 1, i])
                both = jnp.concatenate([do_in[rows, cols] * h for h in halves], axis=0)
                ds = back_rows(jnp.concatenate(weights, axis=0), dot_cols(both, v_in[rows, cols]))
            grad = dot(ds, k_in[rows, cols])
            grad = jnp.where(low, grad[:size], grad[size:]) * (head_dim**-0.5)
            dq_out[rows, cols] = grad.astype(BF)
            left, right = dot_rows(ds[:size], q_in[rows, cols]), dot_rows(ds[size:], q_in[rows, cols])
            dk_out[rows, cols] = jnp.where(low, left, right).astype(BF)
            left, right = (dot_rows(w, do_in[rows, cols]) for w in weights)
            dv_out[rows, cols] = jnp.where(low, left, right).astype(BF)
    turned = h_in[...].T
    width = dq_out.shape[1]
    for i, grad in enumerate((dq_out, dk_out, dv_out)):
        cols = slice(i * width, (i + 1) * width)
        split_cores(
            dot(turned, grad[...]), rows_dev, spot[3], own_out.at[:, :, cols], sent_out.at[:, :, cols]
        )
    sums[0:1, :] = row_sum(dq_out[...].astype(F32))
    sums[1:2, :] = row_sum(dv_out[...].astype(F32))


def first_back_kernel(lay, parts, meta, *refs):
    grads, more = refs[: 3 * parts], refs[3 * parts : 4 * parts]
    w_qkv, x_in, dr_in, vecs, sums_two, db_two, out, sums, kept = refs[4 * parts :]
    step = pl.program_id(0)
    rows = x_in.shape[0]
    width = grads[0].shape[1]
    grad = dot_cols(grads[0][...], w_qkv[:, :width])
    for i in range(1, 3 * parts):
        grad += dot_cols(grads[i][...], w_qkv[:, i * width : (i + 1) * width])
    unit, scale = normalised(x_in[...].astype(F32))
    moved = dr_in[...] + norm_back(unit, scale, vecs[0:1, :], grad)
    kept[pl.ds(pl.multiple_of(step * rows, rows), rows), :] = moved.astype(BF)

    @pl.when(step == 0)
    def _():
        sums[...] = jnp.zeros_like(sums)
        for i, part in enumerate(more):
            sums[2:4, i * width : (i + 1) * width] = part[0:2, :]
        sums[4:5, :] = sums_two[2:3, :]
        sums[5:7, :] = sums_two[0:2, :]
        sums[7:8, :] = db_two[...]

    sums[0:1, :] += row_sum(grad * unit)
    sums[1:2, :] += row_sum(grad)

    @pl.when(step == pl.num_programs(0) - 1)
    def _():
        slot = lax.broadcasted_iota(jnp.int32, (out.shape[0], 1), 0)
        row = lax.broadcasted_iota(jnp.int32, (1, lay.rows), 1)
        out[...] = dot(one_hot(slot, lay.source(row, meta[BIG])), kept[...]).astype(BF)


def owner_rank(owner_vec):
    window_ids = jnp.arange(owner_vec.shape[0], dtype=jnp.int32)
    earlier = (owner_vec[:, None] == owner_vec[None, :]) & (
        window_ids[None, :] < window_ids[:, None]
    )
    return jnp.sum(earlier.astype(jnp.int32), axis=1)


def spec(shape, index):
    return pl.BlockSpec(shape, index)


def local(tokens, ln1_gain, ln1_bias, qkv_weight, query_bias, value_bias, out_weight, out_bias,
          ln2_gain, ln2_bias, fc1_weight, fc1_bias, fc2_weight, fc2_bias, dec_weight, dec_bias,
          mask_token, kept_offsets, kept_count, res_id, dec_owner, dec_cot):
    count = lax.axis_size("dp")
    dev = Slice(count)
    vis, D = tokens.shape
    dec_width = dec_cot.shape[1]
    windows, slots = kept_offsets.shape
    images = res_id.shape[0]
    hidden = fc1_weight.shape[1]
    head_dim = D // HEADS
    per_peer = (windows + count - 1) // count
    total = count * per_peer
    lay = Layout(images, slots)
    R = lay.rows
    sd = jax.ShapeDtypeStruct

    ga, gc = Gather(dev, [qkv_weight]), Gather(dev, [fc2_weight])
    za = ga.along_z()
    xa = ga.first()
    kept_offsets, kept_count, dec_owner, ln1_gain, dec_bias, fc1_bias = held(
        (kept_offsets, kept_count, dec_owner, ln1_gain, dec_bias, fc1_bias), *ga.sent
    )
    wide = max(fc1_bias.shape[0], 128)
    sizes = (dev.size["z"], dev.size["y"], dev.size["x"])
    lanes = -(-windows // 128) * 128
    meta, place_row, info_send = pl.pallas_call(
        functools.partial(describe_kernel, lay, sizes, per_peer),
        name="describe",
        in_specs=[SMEM, SMEM, SMEM, VMEM, VMEM],
        out_specs=[SMEM, VMEM, VMEM],
        out_shape=[sd((16,), jnp.int32), sd((1, R), jnp.int32), sd((total, wide), BF)],
        scratch_shapes=[pltpu.VMEM((8, lanes), F32), pltpu.VMEM((lanes, wide), F32)],
        compiler_params=params(),
    )(lax.axis_index("dp").astype(jnp.int32).reshape(1), kept_count, res_id, dec_owner.reshape(1, windows),
      kept_offsets)
    eight = [ln1_gain, ln1_bias, query_bias, value_bias, out_bias, ln2_gain, ln2_bias, fc2_bias]
    vectors = eight + [fc1_bias, dec_bias, mask_token]
    line = lambda v: jnp.pad(v, ((0, 0), (0, wide - v.shape[1])))
    sheet = jnp.concatenate(
        [line(jnp.stack(eight)), line(fc1_bias[None, :]), line(jnp.stack([dec_bias, mask_token]))], axis=0
    )
    packed = jnp.concatenate(
        [jnp.broadcast_to(sheet[None], (count,) + sheet.shape), info_send.reshape(count, per_peer, wide)],
        axis=1,
    )
    ya = ga.second(packed)
    rest = lax.all_gather(
        held(jnp.concatenate([fc1_weight, out_weight, dec_weight], axis=1), *za),
        "dp",
        axis=0,
        tiled=True,
    )
    packed = lax.all_to_all(packed, "dp", 0, 0, tiled=True)
    n_vec = eight[0].shape[0]
    vecs = packed[:, :8, :n_vec].transpose(1, 0, 2).reshape(8, D).astype(F32)
    bf1 = packed[:, 8, : fc1_bias.shape[0]].reshape(1, hidden).astype(F32)
    vec_dec = packed[:, 9:11, : dec_bias.shape[0]].transpose(1, 0, 2).reshape(2, dec_width).astype(F32)
    info_got = packed[:, 11:].reshape(total, wide)

    w_out_spec = spec((D, D), lambda *_: (0, hidden // D))
    first_dec, dec_half = 2 * (hidden + D) // dec_width, dec_width // 2
    w_dec_specs = [spec((D, dec_half), lambda *_, i=i: (0, first_dec + i)) for i in range(2)]
    tile = R // 3
    rows_of = lambda width: spec((tile, width), lambda i: (i, 0))
    x_rows, h_one = pl.pallas_call(
        functools.partial(first_norm_kernel, lay),
        name="first_norm",
        grid=(3,),
        in_specs=[SMEM, whole((vis, D)), whole((8, D))],
        out_specs=[rows_of(D), rows_of(D)],
        out_shape=[sd((R, D), BF), sd((R, D), BF)],
        compiler_params=params(),
        cost_estimate=cost(2 * R * vis * D, 4e6, weight=0.02),
    )(meta, held(tokens, za), vecs)

    from_a = ga.swap(h_one)

    wins = 16
    steps = total // wins
    cells_w, rows_w = wins * GRID, wins * LANE_SLOTS
    by_step = lambda height, width: spec((height, width), lambda i: (i, 0))
    info_spec = by_step(wins, info_got.shape[1])
    de_send, owner_sums = pl.pallas_call(
        functools.partial(owner_kernel, slots, wins),
        name="owner_side",
        grid=(steps,),
        in_specs=[by_step(cells_w, dec_width), info_spec],
        out_specs=[by_step(rows_w, dec_width), whole((8, dec_width))],
        out_shape=[sd((total * LANE_SLOTS, dec_width), BF), sd((8, dec_width), F32)],
        compiler_params=params(),
        cost_estimate=cost(1e9, 3e6, weight=0.02),
    )(dec_cot, held(info_got, h_one, *ga.sent))

    zc = gc.along_z(*from_a)
    (w_qkv,) = ga.result(meta, de_send)
    group = 4
    parts = HEADS // group
    gw = group * head_dim
    chunk = lay.large_pad // 5
    p_big_t = sd((group, lay.large_pad, lay.large_pad), BF)
    p_small_t = sd((group, images - 1, lay.small_pad, lay.small_pad), BF)

    def attend(i, h_rows):
        col_of = lambda base_: spec((D, gw), lambda _: (0, base_ * parts + i))
        return pl.pallas_call(
            functools.partial(attention_kernel, lay, chunk, head_dim),
            name="attention",
            grid=(1,),
            in_specs=[SMEM, whole((R, D)), col_of(0), col_of(1), col_of(2),
                      spec((8, gw), lambda _: (0, i))],
            out_specs=[whole((R, gw))] * 3 + [whole(p_big_t.shape), whole(p_small_t.shape), whole((R, gw))],
            out_shape=[sd((R, gw), BF)] * 3 + [p_big_t, p_small_t, sd((R, gw), BF)],
            scratch_shapes=[pltpu.VMEM((2 * lay.large_pad, lay.large_pad), F32)],
            compiler_params=params(),
            cost_estimate=cost(2 * R * D * D + 2e9, 8e6, 1e6),
        )(meta, h_rows, w_qkv, w_qkv, w_qkv, vecs)

    attn = [attend(0, h_one)]
    gc.first(attn[0][5])
    attn.append(attend(1, held(h_one, attn[0][5], *gc.sent)))
    gc.second(attn[1][5])
    attn.append(attend(2, held(h_one, attn[1][5], *gc.sent)))
    swapped = gc.swap(attn[2][5])
    de_got = lax.all_to_all(
        held(de_send, attn[1][5]).reshape(count, per_peer * LANE_SLOTS, dec_width), "dp", 0, 0, tiled=True
    ).reshape(total * LANE_SLOTS, dec_width)

    att = [a[5] for a in attn]

    ht = hidden // 6
    row_dev, row_two = D // count, hidden // count
    chips = count // 2
    r_one, h_two, act_h, d_gelu = pl.pallas_call(
        functools.partial(feed_kernel, parts, R // 24),
        name="feed",
        grid=(6,),
        in_specs=[whole((R, gw))] * parts
        + [w_out_spec, whole((8, D)), whole((R, D)), spec((D, ht), lambda j: (0, j)),
           spec((1, ht), lambda j: (0, j))],
        out_specs=[whole((R, D)), whole((R, D))] + [spec((R, ht), lambda j: (0, j))] * 2,
        out_shape=[sd((R, D), F32), sd((R, D), BF), sd((R, hidden), BF), sd((R, hidden), BF)],
        scratch_shapes=[pltpu.VMEM((R, ht), F32)],
        compiler_params=params(),
        cost_estimate=cost(2 * R * D * (hidden + D), 2.5e7, 6e6),
    )(*att, rest, vecs, held(x_rows, *gc.sent), rest, bf1)

    ht = hidden // 4
    nz, ny, nx = sizes
    part = pl.BlockSpec(
        (ny, nx, 1, row_two, D // 2), lambda j, at: (0, 0, lax.rem(at[0] - j + nz, nz), 0, 0)
    )
    ht = hidden // nz
    w_two, e_send, dy, own_dec, sent_dec, db_two = pl.pallas_call(
        functools.partial(join_kernel, row_dev, sizes),
        name="join",
        grid_spec=pltpu.PrefetchScalarGridSpec(
            num_scalar_prefetch=1,
            grid=(nz,),
            in_specs=[spec((R, ht), lambda j, _: (0, j)), part, part, part, part, whole((8, D)),
                      whole((R, D)), *w_dec_specs, whole((2, dec_width)), whole((1, R)),
                      whole((total * LANE_SLOTS, dec_width))],
            out_specs=[spec((2 * ny * nx, row_two, D), lambda j, _: (j, 0, 0)),
                       whole((total * LANE_SLOTS, dec_width)), whole((R, D)),
                       whole((chips, row_dev, dec_width)), whole((chips, row_dev, dec_width)), whole((1, D))],
            scratch_shapes=[pltpu.VMEM((R, D), F32)],
        ),
        out_shape=[sd((count, row_two, D), BF), sd((total * LANE_SLOTS, dec_width), BF), sd((R, D), BF),
                   sd((chips, row_dev, dec_width), BF), sd((chips, row_dev, dec_width), BF), sd((1, D), F32)],
        compiler_params=params(),
        cost_estimate=cost(2 * R * D * hidden + 10 * R * D * dec_width, 2e7),
    )(meta, act_h, gc.part_a, gc.part_b, gc.from_a, gc.from_b, vecs, r_one, rest, rest, vec_dec, place_row,
      de_got)
    w_two = w_two.reshape(hidden, D)
    ht = hidden // 4

    e_got = lax.all_to_all(
        e_send.reshape(count, per_peer * LANE_SLOTS, dec_width), "dp", 0, 0, tiled=True
    ).reshape(total * LANE_SLOTS, dec_width)

    held_chips = ht // (2 * row_two)
    tile_two = spec((held_chips, row_two, D), lambda j: (j, 0, 0))
    tile_one = spec((chips, row_dev, ht), lambda j: (0, 0, j))
    dh, own_two, sent_two, own_one, sent_one, db_one = pl.pallas_call(
        functools.partial(feed_back_kernel, row_dev, row_two),
        name="feed_back",
        grid=(4,),
        in_specs=[SMEM, whole((R, D)), spec((ht, D), lambda j: (j, 0)), spec((R, ht), lambda j: (0, j)),
                  spec((R, ht), lambda j: (0, j)), spec((D, ht), lambda j: (0, j)), whole((R, D))],
        out_specs=[whole((R, D)), tile_two, tile_two, tile_one, tile_one, spec((1, ht), lambda j: (0, j))],
        out_shape=[sd((R, D), F32)] + [sd((chips, row_two, D), BF)] * 2
        + [sd((chips, row_dev, hidden), BF)] * 2 + [sd((1, hidden), F32)],
        scratch_shapes=[pltpu.VMEM((D, R), BF)],
        compiler_params=params(),
        cost_estimate=cost(8 * R * D * hidden, 4e7, weight=20),
    )(meta, dy, w_two, act_h, d_gelu, rest, h_two)
    s_two = Scatter(dev, [(own_two, sent_two)], meta)
    s_one = Scatter(dev, [(own_one, sent_one), (own_dec, sent_dec)], meta)
    c_two, c_one = s_two.swap(), s_one.swap()

    grad_spec = whole((chips, row_dev, D))
    dr, d_att, own_out, sent_out, sums_two = pl.pallas_call(
        functools.partial(out_back_kernel, row_dev, parts),
        name="out_back",
        grid=(3,),
        in_specs=[SMEM, rows_of(D), rows_of(D), rows_of(D), whole((8, D)), w_out_spec]
        + [rows_of(gw)] * parts,
        out_specs=[rows_of(D), rows_of(D), grad_spec, grad_spec, whole((8, D))],
        out_shape=[sd((R, D), F32), sd((R, D), BF)] + [sd((chips, row_dev, D), BF)] * 2
        + [sd((8, D), F32)],
        scratch_shapes=[pltpu.VMEM((D, D), F32)],
        compiler_params=params(),
        cost_estimate=cost(4 * R * D * D, 2e7, weight=20),
    )(meta, dh, r_one, dy, vecs, rest, *att)
    s_two.add(dr, *c_two)
    near = s_two.near()

    def attend_back(i, d_att_rows):
        q_rows, k_rows, v_rows, prob_l, prob_s, _ = attn[i]
        grad_shape = (chips, row_dev, 3 * gw)
        return pl.pallas_call(
            functools.partial(attention_back_kernel, row_dev, lay, chunk, head_dim),
            name="attention_back",
            grid=(1,),
            in_specs=[SMEM, whole((R, D))] + [whole((R, gw))] * 3
            + [whole(p_big_t.shape), whole(p_small_t.shape), spec((R, gw), lambda _: (0, i))],
            out_specs=[whole((R, gw))] * 3 + [whole(grad_shape)] * 2 + [whole((8, gw))],
            out_shape=[sd((R, gw), BF)] * 3 + [sd(grad_shape, BF)] * 2 + [sd((8, gw), F32)],
            scratch_shapes=[pltpu.VMEM((2 * lay.large_pad, lay.large_pad), F32),
                            pltpu.VMEM((2 * lay.large_pad, lay.large_pad), BF)],
            compiler_params=params(),
            cost_estimate=cost(2 * R * D * D + 3e9, 1e7, weight=20),
        )(meta, h_one, q_rows, k_rows, v_rows, prob_l, prob_s, d_att_rows)

    back = [attend_back(0, held(d_att, s_two.blocks[0], e_got, *c_one))]
    far = s_two.far(back[0][0], *near)
    s_one.add(back[0][0], *near)
    near = s_one.near()
    s_mid = Scatter(dev, [(own_out, sent_out), back[0][3:5]], meta)
    c_mid = s_mid.swap(back[0][0])
    back.append(attend_back(1, held(d_att, back[0][0], s_one.blocks[0])))
    s_mid.add(back[1][0], *far, *c_mid)
    lines_two, z_two = finish(dev, meta, [s_two], True, back[1][0])
    far = s_one.far(back[1][0], *near)
    s_last = Scatter(dev, [back[1][3:5]], meta)
    c_last = s_last.swap(back[1][0])
    back.append(attend_back(2, held(d_att, back[1][0], s_mid.blocks[0], lines_two[0], *near)))
    s_last.more(*back[2][3:5])
    near = s_mid.near(back[2][0], *far) + s_mid.far(back[2][0], *far)
    c_last += s_last.swap(back[2][0], *c_last)
    lines_one, z_one = finish(dev, meta, [s_one], True, back[2][0], *far, z_two)

    dqkv = [b[i] for i in range(3) for b in back]
    grad_tokens, sums = pl.pallas_call(
        functools.partial(first_back_kernel, lay, parts),
        name="first_back",
        grid=(3,),
        in_specs=[SMEM] + [rows_of(gw)] * (3 * parts) + [whole((8, gw))] * parts
        + [whole((D, 3 * D)), rows_of(D), rows_of(D), whole((8, D)), whole((8, D)), whole((1, D))],
        out_specs=[whole((vis, D)), whole((8, D))],
        out_shape=[sd((vis, D), BF), sd((8, D), F32)],
        scratch_shapes=[pltpu.VMEM((R, D), BF)],
        compiler_params=params(),
        cost_estimate=cost(2 * R * D * 3 * D + 2 * R * vis * D, 2e7, weight=20),
    )(meta, *dqkv, *[b[5] for b in back], w_qkv, x_rows, held(dr, *lines_one), vecs, sums_two,
      db_two)
    s_last.add(grad_tokens, *near, *c_last)
    near = s_last.near() + s_last.far()

    rows_sent = jnp.concatenate(
        [
            sums.reshape(8, count, -1).transpose(1, 0, 2).reshape(count, -1),
            db_one.reshape(count, -1),
            owner_sums[:2].reshape(2, count, -1).transpose(1, 0, 2).reshape(count, -1),
        ],
        axis=1,
    )
    rows = lax.all_to_all(held(rows_sent, s_last.blocks[0], z_one), "dp", 0, 0, tiled=True)
    decoded = pl.pallas_call(
        functools.partial(decode_kernel, slots, wins),
        name="decode",
        grid=(steps,),
        in_specs=[by_step(rows_w, dec_width), info_spec, whole((2, dec_width))],
        out_specs=by_step(cells_w, dec_width),
        out_shape=sd((total * GRID, dec_width), BF),
        scratch_shapes=[pltpu.VMEM((3 * 32, dec_width // 2), BF)],
        compiler_params=params(),
        cost_estimate=cost(1e9, 7e6, weight=20),
    )(held(e_got, s_last.blocks[0], z_one, rows_sent), info_got, vec_dec)


    lines_late, z_late = finish(dev, meta, [s_mid, s_last], False, decoded, rows, *near)
    rows = jnp.sum(rows, axis=0)
    (grad_two,) = totals(z_two, [s_two])
    grad_one, grad_dec = totals(z_one, [s_one])
    grad_out, grad_qkv = last_sums(z_late, [s_mid, s_last], D, gw)
    vec_grads, start = [], 0
    for v in vectors:
        vec_grads.append(rows[start : start + v.shape[0]])
        start += v.shape[0]
    (gg1, gb1, gbq, gbv, gbo, gg2, gb2, gbf2, gbf1, gbdec, gmask) = vec_grads
    return (decoded, grad_tokens, gg1, gb1, grad_qkv, gbq, gbv, grad_out, gbo, gg2, gb2, grad_one,
            gbf1, grad_two, gbf2, grad_dec, gbdec, gmask)


def solution(mesh):
    mat, vec = P("dp", None), P("dp")
    in_specs = (mat, vec, vec, mat, vec, vec, mat, vec, vec, vec, mat, vec, mat, vec, mat, vec, vec,
                mat, vec, vec, vec, mat)
    out_specs = (mat, mat, vec, vec, mat, vec, vec, mat, vec, vec, vec, mat, vec, mat, vec, mat, vec,
                 vec)
    return jax.shard_map(local, mesh=mesh, in_specs=in_specs, out_specs=out_specs, check_vma=False)
```

```python
import functools

import jax
import jax.numpy as jnp
from jax import lax
from jax.experimental import pallas as pl
from jax.experimental.pallas import tpu as pltpu
from jax.sharding import PartitionSpec as P

HEADS = 12
GRID = 14
NORM_EPS = 1e-06
MASK_FILL = -1e30
BF = jnp.bfloat16
F32 = jnp.float32
MIB = 1 << 20


class Slice:
    def __init__(self, count):
        chips = count // 2
        side = 2 if chips <= 16 else 4
        self.count = count
        self.size = {"c": 2, "x": side, "y": side, "z": chips // (side * side)}
        self.stride = {"c": 1, "x": 2, "y": 2 * side, "z": 2 * side * side}

    def coord(self, axis):
        return (lax.axis_index("dp") // self.stride[axis]) % self.size[axis]

    def shift(self, values, axis, steps):
        stride, size = self.stride[axis], self.size[axis]
        pairs = []
        for source in range(self.count):
            place = (source // stride) % size
            pairs.append((source, source + ((place + steps) % size - place) * stride))
        return lax.ppermute(values, "dp", pairs)

    def copies(self, values, axis):
        return [values] + [self.shift(values, axis, k) for k in range(1, self.size[axis])]

    def shift_plane(self, values, ky, kx):
        pairs = []
        for source in range(self.count):
            target = source
            for axis, steps in (("y", ky), ("x", kx)):
                stride, size = self.stride[axis], self.size[axis]
                place = (source // stride) % size
                target += ((place + steps) % size - place) * stride
            pairs.append((source, target))
        return lax.ppermute(values, "dp", pairs)

    def groups(self, axes):
        seen, found = set(), []
        for first in range(self.count):
            if first in seen:
                continue
            members = [first]
            for axis in axes:
                members = [
                    m + k * self.stride[axis] for m in members for k in range(self.size[axis])
                ]
            found.append(members)
            seen.update(members)
        return found


def cost(flops, moved, trans=0, weight=1):
    return pl.CostEstimate(
        flops=int(weight * flops), bytes_accessed=int(weight * moved), transcendentals=int(trans)
    )


def params():
    return pltpu.CompilerParams(vmem_limit_bytes=60 * MIB)


def whole(shape):
    zeros = (0,) * len(shape)
    return pl.BlockSpec(shape, lambda *_: zeros)


SMEM = pl.BlockSpec(memory_space=pltpu.SMEM)
VMEM = pl.BlockSpec(memory_space=pltpu.VMEM)


def assemble_kernel(sizes, widths, place, part_a, part_b, from_a, from_b, *outs):
    _, ny, nx = sizes
    own_y, own_x, own_c = place[1], place[2], place[3]
    for ky in range(ny):
        at_y = lax.rem(own_y - ky + ny, ny)
        for kx in range(nx):
            at_x = lax.rem(own_x - kx + nx, nx)
            chip = at_y * nx + at_x
            for core, left, right in ((own_c, part_a, part_b), (1 - own_c, from_a, from_b)):
                row, start = chip * 2 + core, 0
                for out, width in zip(outs, widths):
                    half = width // 2
                    out[0, row, :, :half] = left[ky, kx, 0, :, start : start + half]
                    out[0, row, :, half:] = right[kx, ky, 0, :, start : start + half]
                    start += half


def held(values, *others):
    others = [o for o in others if o is not None]
    return lax.optimization_barrier((values, others))[0] if others else values


class Gather:
    def __init__(self, dev, shards):
        self.dev = dev
        self.rows = shards[0].shape[0]
        self.widths = [s.shape[1] for s in shards]
        self.half = sum(self.widths) // 2
        if len(shards) == 1:
            self.local = shards[0]
        else:
            halves = [s.shape[1] // 2 for s in shards]
            self.local = jnp.concatenate(
                [s[:, :h] for s, h in zip(shards, halves)]
                + [s[:, h:] for s, h in zip(shards, halves)],
                axis=1,
            )

    def along_z(self, *after):
        self.arrived = self.dev.copies(held(self.local, *after), "z")
        return self.arrived

    def first(self, *after):
        line = jnp.stack(held(self.arrived, *after))
        part_a, part_b = line[:, :, : self.half], line[:, :, self.half :]
        self.sent = [part_a, part_b]
        self.arrived = self.dev.copies(part_a, "x"), self.dev.copies(part_b, "y")
        return self.arrived[0] + self.arrived[1]

    def second(self, *after):
        part_a, part_b = (jnp.stack(v) for v in held(self.arrived, *after))
        self.sent = [part_a, part_b]
        self.arrived = self.dev.copies(part_a, "y"), self.dev.copies(part_b, "x")
        return self.arrived[0] + self.arrived[1]

    def swap(self, *after):
        self.part_a, self.part_b = (jnp.stack(v) for v in held(self.arrived, *after))
        self.sent = [self.part_a, self.part_b]
        self.from_a = self.dev.shift(self.part_a, "c", 1)
        self.from_b = self.dev.shift(self.part_b, "c", 1)
        return [self.from_a, self.from_b]

    def result(self, place, *after):
        dev, rows = self.dev, self.rows
        nz, ny, nx = sizes = (dev.size["z"], dev.size["y"], dev.size["x"])
        kind = self.local.dtype
        from_a, from_b = held((self.from_a, self.from_b), *after)
        part = pl.BlockSpec((ny, nx, 1, rows, self.half), lambda k, _: (0, 0, k, 0, 0))
        outs = pl.pallas_call(
            functools.partial(assemble_kernel, sizes, self.widths),
            name="assemble",
            grid_spec=pltpu.PrefetchScalarGridSpec(
                num_scalar_prefetch=1,
                grid=(nz,),
                in_specs=[part] * 4,
                out_specs=[
                    pl.BlockSpec(
                        (1, 2 * ny * nx, rows, w), lambda k, at: (lax.rem(at[0] - k + nz, nz), 0, 0, 0)
                    )
                    for w in self.widths
                ],
            ),
            out_shape=[jax.ShapeDtypeStruct((nz, 2 * ny * nx, rows, w), kind) for w in self.widths],
            compiler_params=params(),
            cost_estimate=cost(0, 4 * dev.count * rows * sum(self.widths)),
        )(place, self.part_a, self.part_b, from_a, from_b)
        return [o.reshape(dev.count * rows, w) for o, w in zip(outs, self.widths)]


def chip_sum_kernel(sizes, pairs, place, *refs):
    nz, ny, nx = sizes
    owns, gots, outs = refs[:pairs], refs[pairs : 2 * pairs], refs[2 * pairs :]
    own_y, own_x = place[1], place[2]
    for ky in range(ny):
        for kx in range(nx):
            at = lax.rem(own_y + ky, ny) * nx + lax.rem(own_x + kx, nx)
            for z in range(nz):
                start = 0
                for own, got in zip(owns, gots):
                    width = own.shape[-1]
                    chip = z * ny * nx + at
                    outs[ky * nx + kx][z, :, start : start + width] = own[chip] + got[chip]
                    start += width


class Scatter:
    def __init__(self, dev, pairs, place):
        self.dev, self.place = dev, place
        self.own = [p[0] for p in pairs]
        self.sent = [p[1] for p in pairs]
        self.rows = self.own[0].shape[1]
        self.widths = [p[0].shape[2] for p in pairs]
        self.got = []

    def swap(self, *after):
        waiting = held(self.sent[len(self.got) :], *after)
        found = [self.dev.shift(v, "c", 1) for v in waiting]
        self.got = self.got + found
        return found

    def more(self, own, sent):
        self.own, self.sent = self.own + [own], self.sent + [sent]
        self.widths = self.widths + [own.shape[2]]

    def add(self, *after):
        self.got = held(self.got, *after)
        dev, rows = self.dev, self.rows
        sizes = (dev.size["z"], dev.size["y"], dev.size["x"])
        plane, width = sizes[1] * sizes[2], sum(self.widths)
        pairs, chips = len(self.own), dev.count // 2
        self.steps = next(n for n in (4, 3, 2, 1) if all(w % (128 * n) == 0 for w in self.widths))
        tiles = [w // self.steps for w in self.widths]
        halves = [pl.BlockSpec((chips, rows, t), lambda i: (0, 0, i)) for t in tiles]
        out_tile = pl.BlockSpec((sizes[0], rows, sum(tiles)), lambda i: (0, 0, i))
        self.blocks = pl.pallas_call(
            functools.partial(chip_sum_kernel, sizes, pairs),
            name="chip_sum",
            grid=(self.steps,),
            out_shape=[jax.ShapeDtypeStruct((sizes[0], rows, width), BF)] * plane,
            in_specs=[SMEM] + halves + halves,
            out_specs=[out_tile] * plane,
            compiler_params=params(),
            cost_estimate=cost(0, 6 * dev.count // 2 * rows * width),
        )(self.place, *self.own, *self.got)
        self.terms = [self.blocks[0]]
        return self.blocks

    def near(self, *after):
        return self._plane(lambda ky, kx: ky == 0 or kx == 0, after)

    def far(self, *after):
        return self._plane(lambda ky, kx: ky > 0 and kx > 0, after)

    def _plane(self, chosen, after):
        dev, ny, nx = self.dev, self.dev.size["y"], self.dev.size["x"]
        blocks = held(self.blocks, *after)
        found = [
            dev.shift_plane(blocks[ky * nx + kx], ky, kx)
            for ky in range(ny)
            for kx in range(nx)
            if (ky or kx) and chosen(ky, kx)
        ]
        self.terms += found
        return found


def line_kernel(nz, counts, place, *refs):
    terms, outs = refs[: sum(counts)], refs[sum(counts) :]
    joined = len(outs) == 1
    rows = outs[0].shape[-2]
    for k in range(nz):
        at, first, start = k if joined else lax.rem(place[0] + k, nz), 0, 0
        out = outs[0].at[k] if joined else outs[k]
        for count in counts:
            group = terms[first : first + count]
            total = group[0][at].astype(F32)
            for term in group[1:]:
                total += term[at].astype(F32)
            first, width = first + count, total.shape[1]
            for piece in range(total.shape[0] // rows):
                out[:, start : start + width] = total[piece * rows : (piece + 1) * rows].astype(BF)
                start += width


def finish(dev, place, scatters, joined, *after):
    nz, rows = dev.size["z"], min(s.rows for s in scatters)
    width = sum(w * (s.rows // rows) for s in scatters for w in s.widths)
    terms = held([t for s in scatters for t in s.terms], *after)
    blocks = pl.pallas_call(
        functools.partial(line_kernel, nz, [len(s.terms) for s in scatters]),
        name="plane_sum",
        out_shape=[jax.ShapeDtypeStruct((nz, rows, width), BF)]
        if joined
        else [jax.ShapeDtypeStruct((rows, width), BF)] * nz,
        in_specs=[SMEM] + [VMEM] * len(terms),
        out_specs=[VMEM] * (1 if joined else nz),
        compiler_params=params(),
        cost_estimate=cost(0, 8 * nz * rows * width),
    )(place, *terms)
    if joined:
        line = lax.all_to_all(
            blocks[0], "dp", 0, 0, axis_index_groups=dev.groups("z"), tiled=True
        )
        return blocks, line
    return blocks, [blocks[0]] + [dev.shift(blocks[k], "z", k) for k in range(1, nz)]


def totals(arrived, scatters):
    if isinstance(arrived, list):
        total = sum(v.astype(F32) for v in arrived)
    else:
        total = jnp.sum(arrived.astype(F32), axis=0)
    rows, start, out = total.shape[0], 0, []
    for s in scatters:
        pieces, width = s.rows // rows, sum(s.widths)
        parts = [total[:, start + i * width : start + (i + 1) * width] for i in range(pieces)]
        whole_rows = parts[0] if pieces == 1 else jnp.concatenate(parts, axis=0)
        start += pieces * width
        tiles, span = [w // s.steps for w in s.widths], width // s.steps
        for t, tile in enumerate(tiles):
            at = sum(tiles[:t])
            found = [whole_rows[:, i * span + at : i * span + at + tile] for i in range(s.steps)]
            out.append(found[0] if len(found) == 1 else jnp.concatenate(found, axis=1))
    return out


def last_sums_kernel(count, moves, vectors_at, *refs):
    terms, outs = refs[:count], refs[count:]
    for start, width, out, at in moves:
        total = terms[0][:, start : start + width].astype(F32)
        for term in terms[1:]:
            total += term[:, start : start + width].astype(F32)
        outs[out][:, at : at + width] = total
    for out, (row, lane) in zip(outs[2:], vectors_at):
        lanes = slice(lane, lane + out.shape[1])
        total = terms[0][:, lanes].astype(F32)
        for term in terms[1:]:
            total += term[:, lanes].astype(F32)
        out[...] = total[row : row + 1]


def last_sums(arrived, scatters, model, head_cols, lengths):
    rows, width = arrived[0].shape
    moves, rides, start, first = [], [], 0, True
    part = -1
    for s in scatters:
        tiles, span = [w // s.steps for w in s.widths], sum(s.widths) // s.steps
        for t, tile in enumerate(tiles):
            part = part if first else part + 1
            for i in range(s.steps):
                source = start + i * span + sum(tiles[:t])
                if first:
                    moves.append((source, tile, 0, i * tile))
                    continue
                if s is scatters[-1] and t == len(tiles) - 1:
                    rides.append(source)
                    continue
                piece = min(tile, head_cols)
                for k in range(0, tile, piece):
                    block, inside = divmod(i * tile + k, head_cols)
                    moves.append((source + k, piece, 1, block * model + part * head_cols + inside))
            if first:
                part, first = -1, False
        start += sum(s.widths)
    ride_tile = scatters[-1].widths[-1] // scatters[-1].steps
    vectors_at = []
    for i in range(len(lengths)):
        step, inside = divmod(128 * (i // rows), ride_tile)
        vectors_at.append((i % rows, rides[step] + inside))
    shapes = [(rows, model), (rows, 3 * model)] + [(1, n) for n in lengths]
    return pl.pallas_call(
        functools.partial(last_sums_kernel, len(arrived), moves, vectors_at),
        name="last_sums",
        grid=(1,),
        in_specs=[whole((rows, width))] * len(arrived),
        out_specs=[whole(v) for v in shapes],
        out_shape=[jax.ShapeDtypeStruct(v, F32) for v in shapes],
        compiler_params=params(),
    )(*arrived)


def split_cores(value, rows, core, own, sent):
    if rows % 8 == 0:
        parts = value.reshape(-1, 2, rows, value.shape[1])
        own[...] = jnp.where(core == 0, parts[:, 0], parts[:, 1]).astype(BF)
        sent[...] = jnp.where(core == 0, parts[:, 1], parts[:, 0]).astype(BF)
        return
    for chip in range(value.shape[0] // (2 * rows)):
        first = value[2 * chip * rows : (2 * chip + 1) * rows]
        second = value[(2 * chip + 1) * rows : (2 * chip + 2) * rows]
        own[chip] = jnp.where(core == 0, first, second).astype(BF)
        sent[chip] = jnp.where(core == 0, second, first).astype(BF)


def dot(left, right):
    return jnp.dot(left, right, preferred_element_type=F32)


def dot_rows(left, right):
    return lax.dot_general(left, right, (((0,), (0,)), ((), ())), preferred_element_type=F32)


def dot_cols(left, right):
    return lax.dot_general(left, right, (((1,), (1,)), ((), ())), preferred_element_type=F32)


def one_hot(column, row):
    return jnp.where(column == row, 1.0, 0.0).astype(BF)


def row_sum(values):
    return jnp.sum(values, axis=0, keepdims=True)


def normalised(values):
    mean = jnp.mean(values, axis=1, keepdims=True)
    centered = values - mean
    variance = jnp.mean(centered * centered, axis=1, keepdims=True)
    scale = lax.rsqrt(variance + NORM_EPS)
    return centered * scale, scale


def norm_back(unit, scale, gain, grad):
    weighted = grad * gain
    first = jnp.mean(weighted, axis=1, keepdims=True)
    second = jnp.mean(weighted * unit, axis=1, keepdims=True)
    return scale * (weighted - first - unit * second)


class Layout:
    def __init__(self, images, slots):
        self.images, self.slots = images, slots
        self.small, self.large = GRID * slots, 4 * GRID * slots
        self.small_pad = -(-self.small // 16) * 16
        self.large_pad = -(-self.large // 16) * 16
        self.starts = [self.large_pad + i * self.small_pad for i in range(images - 1)]
        self.rows = self.large_pad + (images - 1) * self.small_pad

    def rows_of(self, row, big):
        small_id = jnp.maximum(row - self.large_pad, 0) // self.small_pad
        in_large = row < self.large_pad
        offset = jnp.where(in_large, row, row - self.large_pad - small_id * self.small_pad)
        real = offset < jnp.where(in_large, self.large, self.small)
        image = jnp.where(in_large, big, small_id + jnp.where(small_id >= big, 1, 0))
        window = (
            GRID * image + jnp.where(image > big, 3 * GRID, 0) + offset // self.slots
        )
        return window, offset % self.slots, real

    def source(self, row, big):
        window, slot, real = self.rows_of(row, big)
        return jnp.where(real, window * self.slots + slot, -1)

    def key_mask(self, size, real, kept):
        lane = lax.broadcasted_iota(jnp.int32, (1, size), 1)
        live = (lane < real) & (lane % self.slots < kept)
        return jnp.where(live, 0.0, MASK_FILL)


def spread_lanes(width, full):
    lane = lax.broadcasted_iota(jnp.int32, (1, full), 1) % width
    return lax.broadcasted_iota(jnp.int32, (128, 1), 0) == lane


def own_lanes(count, width, full):
    lane = lax.broadcasted_iota(jnp.int32, (1, full), 1) // width
    return lax.broadcasted_iota(jnp.int32, (count, 1), 0) == lane


def pack_rows(count, width, joined, out, first):
    vectors, full = joined.shape
    mask = own_lanes(count, width, full)
    split = jnp.concatenate(
        [jnp.where(mask, joined[v : v + 1, :], 0.0) for v in range(vectors)], axis=0
    )
    high = split.astype(BF)
    rest = split - high.astype(F32)
    middle = rest.astype(BF)
    low = (rest - middle.astype(F32)).astype(BF)
    lanes = jnp.where(spread_lanes(width, full), 1.0, 0.0).astype(BF)
    found = dot_cols(jnp.concatenate([high, middle, low], axis=0), lanes)
    size = vectors * count
    total = found[:size] + found[size : 2 * size] + found[2 * size :]
    for v in range(vectors):
        out[first + v] = total[v * count : (v + 1) * count]


LANE_SLOTS = 8
BIG, KEPT = 4, 5
FIELDS = 4


def describe_kernel(lay, dims, per_peer, index, counts, sides, owner_in, offsets_in,
                    meta, place_out, info_out, owners, cells):
    images, slots = lay.images, lay.slots
    windows, padded = offsets_in.shape[0], owners.shape[1]
    _, ny, nx = dims
    me = index[0]
    meta[0] = me // (2 * nx * ny)
    meta[1] = (me // (2 * nx)) % ny
    meta[2] = (me // 2) % nx
    meta[3] = me % 2
    big, kept_big = jnp.int32(0), jnp.int32(0)
    for i in range(images):
        big += i * sides[i]
        kept_big += sides[i] * counts[i]
    meta[BIG] = big
    meta[KEPT] = kept_big
    for i in range(images - 1):
        meta[KEPT + 1 + i] = jnp.where(i < big, counts[i], counts[i + 1])

    owners[...] = jnp.full(owners.shape, -1.0, F32)
    owners[:, :windows] = jnp.broadcast_to(owner_in[...], (8, windows)).astype(F32)
    row = owners[0:1, :]
    col = owners[...].T[:, 0:1]
    before = lax.broadcasted_iota(jnp.int32, (padded, padded), 0)
    after = lax.broadcasted_iota(jnp.int32, (padded, padded), 1)
    same = jnp.where(col == row, 1.0, 0.0)
    rank_row = jnp.sum(jnp.where(before < after, same, 0.0), axis=0, keepdims=True)
    rank_col = jnp.sum(jnp.where(after < before, same, 0.0), axis=1, keepdims=True)
    bucket_row = jnp.where(row >= 0, row * per_peer + rank_row, -1.0)
    bucket_col = jnp.where(col >= 0, col * per_peer + rank_col, -1.0)

    win = lax.broadcasted_iota(jnp.int32, (padded, 1), 0)
    start = GRID * big
    in_big = (win >= start) & (win < start + 4 * GRID)
    image = jnp.where(in_big, big, win // GRID - jnp.where(win >= start + 4 * GRID, 3, 0))
    kept = jnp.zeros((padded, 1), jnp.int32)
    for i in range(images):
        kept = jnp.where(image == i, counts[i], kept)
    cells[...] = jnp.zeros_like(cells)
    cells[:windows, FIELDS : FIELDS + slots] = offsets_in[...].astype(F32)
    lane = lax.broadcasted_iota(jnp.int32, cells.shape, 1)
    turn = jnp.where(in_big, win - start, win % GRID)
    values = jnp.where(lane == 0, 1.0, cells[...])
    values = jnp.where(lane == 1, kept.astype(F32), values)
    values = jnp.where(lane == 2, turn.astype(F32), values)
    values = jnp.where(lane == 3, jnp.where(in_big, 2.0 * GRID, 1.0 * GRID), values)
    target = lax.broadcasted_iota(jnp.int32, (info_out.shape[0], padded), 0).astype(F32)
    info_out[...] = dot(one_hot(target, bucket_row), values.astype(BF)).astype(BF)

    place = lax.broadcasted_iota(jnp.int32, (1, lay.rows), 1)
    window, slot, real = lay.rows_of(place, big)
    found = jnp.sum(
        jnp.where(win == window, bucket_col * LANE_SLOTS, 0.0), axis=0, keepdims=True
    ).astype(jnp.int32)
    bound = jnp.sum(jnp.where(win == window, kept.astype(F32), 0.0), axis=0, keepdims=True)
    live = real & (slot.astype(F32) < bound)
    place_out[...] = jnp.where(live, found + slot, -1)


def slot_targets(info, slots, wins, axis):
    rows = wins * LANE_SLOTS
    shape = (rows, 1) if axis == 0 else (1, rows)
    spread = (rows, wins) if axis == 0 else (wins, rows)
    owner = lax.broadcasted_iota(jnp.int32, spread, axis) // LANE_SLOTS
    window = lax.broadcasted_iota(jnp.int32, spread, 1 - axis)
    pick = jnp.where(owner == window, 1.0, 0.0).astype(BF)
    fields = dot(pick, info) if axis == 0 else dot_rows(info, pick)
    slot = lax.broadcasted_iota(jnp.int32, shape, axis) % LANE_SLOTS
    field = (lambda i: fields[:, i : i + 1]) if axis == 0 else (lambda i: fields[i : i + 1, :])
    cell = jnp.zeros(shape, F32)
    for j in range(slots):
        cell = cell + jnp.where(slot == j, field(4 + j), 0.0)
    first = (lax.broadcasted_iota(jnp.int32, shape, axis) // LANE_SLOTS) * GRID
    live = slot.astype(F32) < field(1)
    return jnp.where(live, first + cell.astype(jnp.int32), -1)


def owner_kernel(slots, wins, cot, info_in, de_out, sums_out):
    step = pl.program_id(0)
    cells = wins * GRID
    grads = cot[...]
    info = info_in[...]
    cell_lane = lax.broadcasted_iota(jnp.int32, (1, cells), 1)
    want = slot_targets(info, slots, wins, 0)
    pick = one_hot(want, cell_lane)
    picked = dot(pick, grads)
    de_out[...] = picked.astype(BF)
    taken = jnp.sum(jnp.where(want == cell_lane, 1.0, 0.0), axis=0, keepdims=True)
    window = lax.broadcasted_iota(jnp.int32, (wins, cells), 0)
    inside = jnp.where(
        window == lax.broadcasted_iota(jnp.int32, (wins, cells), 1) // GRID, 1.0, 0.0
    ).astype(BF)
    present_row = dot_rows(info, inside)[0:1, :]
    mask_sum = dot(jnp.broadcast_to(present_row - taken, (8, cells)).astype(BF), grads)[:1]

    @pl.when(step == 0)
    def _():
        sums_out[...] = jnp.zeros_like(sums_out)

    sums_out[0:1, :] += row_sum(picked)
    sums_out[1:2, :] += mask_sum


def decode_kernel(slots, wins, got, info_in, vec_dec, out, stacked):
    cells = wins * GRID
    quarter = out.shape[1] // 4
    info = info_in[...]
    depth = stacked.shape[0] // 3

    @pl.when(pl.program_id(0) == 0)
    def _():
        place = lax.broadcasted_iota(jnp.int32, (depth, quarter), 0).astype(F32)
        index = lax.broadcasted_iota(jnp.int32, (depth, quarter), 1).astype(F32) / quarter
        angle = place * (1.0 / jnp.exp(index * jnp.log(F32(10000.0))))
        table = jnp.concatenate([jnp.sin(angle), jnp.cos(angle)], axis=1)
        high = table.astype(BF)
        rest = table - high.astype(F32)
        middle = rest.astype(BF)
        stacked[:depth] = high
        stacked[depth : 2 * depth] = middle
        stacked[2 * depth :] = (rest - middle.astype(F32)).astype(BF)

    cell_row = lax.broadcasted_iota(jnp.int32, (cells, 1), 0)
    chosen = one_hot(cell_row, slot_targets(info, slots, wins, 1))
    filled = jnp.sum(chosen.astype(F32), axis=1, keepdims=True)
    placed = dot(chosen, got[...])
    owner = lax.broadcasted_iota(jnp.int32, (cells, wins), 0) // GRID
    fields = dot(one_hot(owner, lax.broadcasted_iota(jnp.int32, (cells, wins), 1)), info)
    present = fields[:, 0:1]
    turn = fields[:, 2:3].astype(jnp.int32)
    wide = fields[:, 3:4] > GRID
    cell = cell_row % GRID
    along = jnp.where(wide, (turn % 2) * GRID + cell, cell)
    across = jnp.where(wide, turn // 2, turn)
    lane = lax.broadcasted_iota(jnp.int32, (1, 3 * depth), 1) % depth
    shown = present > 0.5
    first = dot(one_hot(jnp.where(shown, along, -1), lane), stacked[...])
    second = dot(one_hot(jnp.where(shown, across, -1), lane), stacked[...])
    bare = present - filled
    half = 2 * quarter
    out[:, :half] = (placed[:, :half] + first + bare * vec_dec[1:2, :half]).astype(BF)
    out[:, half:] = (placed[:, half:] + second + bare * vec_dec[1:2, half:]).astype(BF)


def first_norm_kernel(lay, meta, tokens, vecs, x_out, h_out):
    rows = x_out.shape[0]
    row = lax.broadcasted_iota(jnp.int32, (rows, 1), 0) + pl.program_id(0) * rows
    lane = lax.broadcasted_iota(jnp.int32, (1, tokens.shape[0]), 1)
    moved = dot(one_hot(lay.source(row, meta[BIG]), lane), tokens[...])
    x_out[...] = moved.astype(BF)
    unit, _ = normalised(moved)
    h_out[...] = (unit * vecs[0:1, :] + vecs[1:2, :]).astype(BF)


def softmax_rows(scores):
    top = jnp.max(scores, axis=1, keepdims=True)
    expo = jnp.exp(scores - top)
    return (expo * (1.0 / jnp.sum(expo, axis=1, keepdims=True))).astype(BF)


def attention_kernel(lay, chunk, head_dim, meta, h_in, w_q, w_k, w_v, vecs,
                     q_out, k_out, v_out, pl_out, ps_out, o_out, scores):
    big, small = lay.large_pad, lay.small_pad
    normed = h_in[...]
    q_out[...] = ((dot(normed, w_q[...]) + vecs[2:3, :]) * (head_dim**-0.5)).astype(BF)
    k_out[...] = dot(normed, w_k[...]).astype(BF)
    v_out[...] = (dot(normed, w_v[...]) + vecs[3:4, :]).astype(BF)
    lane = lax.broadcasted_iota(jnp.int32, (1, 2 * head_dim), 1)
    low = lane < head_dim
    halves = (jnp.where(low, 1.0, 0.0).astype(BF), jnp.where(low, 0.0, 1.0).astype(BF))
    mask_l = lay.key_mask(big, lay.large, meta[KEPT])
    masks = [lay.key_mask(small, lay.small, meta[KEPT + 1 + i]) for i in range(lay.images - 1)]
    for pair in range(q_out.shape[1] // (2 * head_dim)):
        cols = slice(pair * 2 * head_dim, (pair + 1) * 2 * head_dim)
        both = jnp.concatenate([q_out[:big, cols] * h for h in halves], axis=0)
        scores[...] = dot_cols(both, k_out[:big, cols])
        for half in range(2):
            for start in range(0, big, chunk):
                part = scores[half * big + start : half * big + start + chunk, :] + mask_l
                pl_out[2 * pair + half, start : start + chunk, :] = softmax_rows(part)
        outs = dot(pl_out[2 * pair : 2 * pair + 2].reshape(2 * big, big), v_out[:big, cols])
        o_out[:big, cols] = jnp.where(low, outs[:big], outs[big:]).astype(BF)
        for i, start in enumerate(lay.starts):
            rows = slice(start, start + small)
            both = jnp.concatenate([q_out[rows, cols] * h for h in halves], axis=0)
            weights = softmax_rows(dot_cols(both, k_out[rows, cols]) + masks[i])
            ps_out[2 * pair, i] = weights[:small]
            ps_out[2 * pair + 1, i] = weights[small:]
            outs = dot(weights, v_out[rows, cols])
            o_out[rows, cols] = jnp.where(low, outs[:small], outs[small:]).astype(BF)


def feed_kernel(parts, chunk, *refs):
    o_in = refs[:parts]
    w_out, vecs, x_in, weight, bias, r_out, h_out, g_out, d_out, hidden = refs[parts:]
    rows_all, width = x_in.shape[0], o_in[0].shape[1]

    @pl.when(pl.program_id(0) == 0)
    def _():
        for start in range(0, rows_all, rows_all // 3):
            rows = slice(start, start + rows_all // 3)
            residual = x_in[rows, :].astype(F32) + vecs[4:5, :]
            for i, o in enumerate(o_in):
                residual += dot(o[rows, :], w_out[i * width : (i + 1) * width, :])
            r_out[rows, :] = residual
            unit, _ = normalised(residual)
            h_out[rows, :] = (unit * vecs[5:6, :] + vecs[6:7, :]).astype(BF)

    hidden[...] = dot(h_out[...], weight[...])
    for start in range(0, rows_all, chunk):
        rows = slice(start, start + chunk)
        u = hidden[rows, :] + bias[...]
        half = 0.5 + 0.5 * lax.erf(u * (0.5**0.5))
        g_out[rows, :] = (u * half).astype(BF)
        density = jnp.exp(u * u * -0.5) * 0.3989422804014327
        d_out[rows, :] = (half + u * density).astype(BF)


def join_kernel(rows_dev, sizes, spot, g_in, part_a, part_b, from_a, from_b, vecs, r_in, w_dec, w_dec_more, vec_dec, place, got,
                w_out, e_out, dy_out, own_out, sent_out, db_out, total):
    step = pl.program_id(0)

    @pl.when(step == 0)
    def _():
        total[...] = r_in[...] + vecs[7:8, :]

    _, ny, nx = sizes
    for ky in range(ny):
        for kx in range(nx):
            chip = lax.rem(spot[1] - ky + ny, ny) * nx + lax.rem(spot[2] - kx + nx, nx)
            for core, left, right in ((spot[3], part_a, part_b), (1 - spot[3], from_a, from_b)):
                half = left.shape[-1]
                w_out[chip * 2 + core, :, :half] = left[ky, kx, 0]
                w_out[chip * 2 + core, :, half:] = right[kx, ky, 0]
    total[...] += dot(g_in[...], w_out[...].reshape(g_in.shape[1], total.shape[1]))

    @pl.when(step == pl.num_programs(0) - 1)
    def _():
        half = w_dec.shape[1]
        y = total[...].astype(BF)
        target = lax.broadcasted_iota(jnp.int32, (e_out.shape[0], 1), 0)
        pick = one_hot(target, place[...])
        grad = dot_rows(pick, got[...]).astype(BF)
        for i, w in enumerate((w_dec, w_dec_more)):
            cols = slice(i * half, (i + 1) * half)
            embedded = (dot(y, w[...]) + vec_dec[0:1, cols]).astype(BF)
            e_out[:, cols] = dot(pick, embedded).astype(BF)
        dy = dot_cols(grad[:, :half], w_dec[...]) + dot_cols(grad[:, half:], w_dec_more[...])
        dy = dy.astype(BF)
        dy_out[...] = dy
        split_cores(dot_rows(y, grad), rows_dev, spot[3], own_out, sent_out)
        db_out[...] = row_sum(dy.astype(F32))


def feed_back_kernel(rows_one, rows_two, spot, dy_in, w_two, g_in, d_in, w_one, h_in,
                     dh_out, own_two, sent_two, own_one, sent_one, db_out, turned):
    step = pl.program_id(0)

    @pl.when(step == 0)
    def _():
        turned[...] = h_in[...].T

    dy = dy_in[...]
    du = (dot_cols(dy, w_two[...]) * d_in[...].astype(F32)).astype(BF)
    db_out[...] = row_sum(du.astype(F32))
    split_cores(dot_rows(g_in[...], dy), rows_two, spot[3], own_two, sent_two)
    split_cores(dot(turned[...], du), rows_one, spot[3], own_one, sent_one)
    part = dot_cols(du, w_one[...])

    @pl.when(step == 0)
    def _():
        dh_out[...] = part

    @pl.when(step > 0)
    def _():
        dh_out[...] += part


def out_back_kernel(rows, parts, spot, dh_in, r_in, dy_in, vecs, w_out, *refs):
    o_in = refs[:parts]
    dr_out, do_out, own_out, sent_out, sums, total = refs[parts:]
    step = pl.program_id(0)
    unit, scale = normalised(r_in[...])
    grad = dh_in[...]
    dr = dy_in[...].astype(F32) + norm_back(unit, scale, vecs[5:6, :], grad)
    dr_out[...] = dr
    da = dr.astype(BF)
    do_out[...] = dot_cols(da, w_out[...]).astype(BF)

    @pl.when(step == 0)
    def _():
        sums[...] = jnp.zeros_like(sums)
        total[...] = jnp.zeros_like(total)

    sums[0:1, :] += row_sum(grad * unit)
    sums[1:2, :] += row_sum(grad)
    sums[2:3, :] += row_sum(da.astype(F32))
    width = o_in[0].shape[1]
    for i, o in enumerate(o_in):
        total[i * width : (i + 1) * width, :] += dot_rows(o[...], da)

    @pl.when(step == pl.num_programs(0) - 1)
    def _():
        split_cores(total[...], rows, spot[3], own_out, sent_out)


def attention_back_kernel(rows_dev, lay, chunk, head_dim, spot, h_in, q_in, k_in, v_in, pl_in, ps_in, do_in,
                          dq_out, dk_out, dv_out, own_out, sent_out, sums, scores, ds_big):
    big, small = lay.large_pad, lay.small_pad
    lane = lax.broadcasted_iota(jnp.int32, (1, 2 * head_dim), 1)
    low = lane < head_dim
    halves = (jnp.where(low, 1.0, 0.0).astype(BF), jnp.where(low, 0.0, 1.0).astype(BF))

    def back_rows(weights, grad):
        p = weights.astype(F32)
        inner = jnp.sum(grad * p, axis=1, keepdims=True)
        return (p * (grad - inner)).astype(BF)

    for pair in range(q_in.shape[1] // (2 * head_dim)):
        cols = slice(pair * 2 * head_dim, (pair + 1) * 2 * head_dim)
        both = jnp.concatenate([do_in[:big, cols] * h for h in halves], axis=0)
        scores[...] = dot_cols(both, v_in[:big, cols])
        for half in range(2):
            for at in range(0, big, chunk):
                rows = slice(half * big + at, half * big + at + chunk)
                ds_big[rows, :] = back_rows(pl_in[2 * pair + half, at : at + chunk, :], scores[rows, :])
        spans = [(slice(0, big), None)] + [
            (slice(start, start + small), i) for i, start in enumerate(lay.starts)
        ]
        for rows, i in spans:
            if i is None:
                size, ds = big, ds_big[...]
                weights = (pl_in[2 * pair], pl_in[2 * pair + 1])
            else:
                size = small
                weights = (ps_in[2 * pair, i], ps_in[2 * pair + 1, i])
                both = jnp.concatenate([do_in[rows, cols] * h for h in halves], axis=0)
                ds = back_rows(jnp.concatenate(weights, axis=0), dot_cols(both, v_in[rows, cols]))
            grad = dot(ds, k_in[rows, cols])
            grad = jnp.where(low, grad[:size], grad[size:]) * (head_dim**-0.5)
            dq_out[rows, cols] = grad.astype(BF)
            left, right = dot_rows(ds[:size], q_in[rows, cols]), dot_rows(ds[size:], q_in[rows, cols])
            dk_out[rows, cols] = jnp.where(low, left, right).astype(BF)
            left, right = (dot_rows(w, do_in[rows, cols]) for w in weights)
            dv_out[rows, cols] = jnp.where(low, left, right).astype(BF)
    turned = h_in[...].T
    width = dq_out.shape[1]
    for i, grad in enumerate((dq_out, dk_out, dv_out)):
        cols = slice(i * width, (i + 1) * width)
        split_cores(
            dot(turned, grad[...]), rows_dev, spot[3], own_out.at[:, :, cols], sent_out.at[:, :, cols]
        )
    sums[0:1, :] = row_sum(dq_out[...].astype(F32))
    sums[1:2, :] = row_sum(dv_out[...].astype(F32))


def first_back_kernel(lay, parts, count, widths, meta, *refs):
    grads, more = refs[: 3 * parts], refs[3 * parts : 4 * parts]
    w_qkv, x_in, dr_in, vecs, sums_two, db_two, db_one, sums_dec, out, sheet, sums, kept = refs[4 * parts :]
    step = pl.program_id(0)
    rows = x_in.shape[0]
    width = grads[0].shape[1]
    grad = dot_cols(grads[0][...], w_qkv[:, :width])
    for i in range(1, 3 * parts):
        grad += dot_cols(grads[i][...], w_qkv[:, i * width : (i + 1) * width])
    unit, scale = normalised(x_in[...].astype(F32))
    moved = dr_in[...] + norm_back(unit, scale, vecs[0:1, :], grad)
    kept[pl.ds(pl.multiple_of(step * rows, rows), rows), :] = moved.astype(BF)

    @pl.when(step == 0)
    def _():
        sums[...] = jnp.zeros_like(sums)
        for i, part in enumerate(more):
            sums[2:4, i * width : (i + 1) * width] = part[0:2, :]
        sums[4:5, :] = sums_two[2:3, :]
        sums[5:7, :] = sums_two[0:2, :]
        sums[7:8, :] = db_two[...]

    sums[0:1, :] += row_sum(grad * unit)
    sums[1:2, :] += row_sum(grad)

    @pl.when(step == pl.num_programs(0) - 1)
    def _():
        slot = lax.broadcasted_iota(jnp.int32, (out.shape[0], 1), 0)
        row = lax.broadcasted_iota(jnp.int32, (1, lay.rows), 1)
        out[...] = dot(one_hot(slot, lay.source(row, meta[BIG])), kept[...]).astype(BF)
        pack_rows(count, widths[0], sums[...], sheet, 0)
        pack_rows(count, widths[1], db_one[...], sheet, 8)
        pack_rows(count, widths[2], sums_dec[0:2, :], sheet, 9)


def owner_rank(owner_vec):
    window_ids = jnp.arange(owner_vec.shape[0], dtype=jnp.int32)
    earlier = (owner_vec[:, None] == owner_vec[None, :]) & (
        window_ids[None, :] < window_ids[:, None]
    )
    return jnp.sum(earlier.astype(jnp.int32), axis=1)


def spec(shape, index):
    return pl.BlockSpec(shape, index)


def local(tokens, ln1_gain, ln1_bias, qkv_weight, query_bias, value_bias, out_weight, out_bias,
          ln2_gain, ln2_bias, fc1_weight, fc1_bias, fc2_weight, fc2_bias, dec_weight, dec_bias,
          mask_token, kept_offsets, kept_count, res_id, dec_owner, dec_cot):
    count = lax.axis_size("dp")
    dev = Slice(count)
    vis, D = tokens.shape
    dec_width = dec_cot.shape[1]
    windows, slots = kept_offsets.shape
    images = res_id.shape[0]
    hidden = fc1_weight.shape[1]
    head_dim = D // HEADS
    per_peer = (windows + count - 1) // count
    total = count * per_peer
    lay = Layout(images, slots)
    R = lay.rows
    sd = jax.ShapeDtypeStruct

    ga, gc = Gather(dev, [qkv_weight]), Gather(dev, [fc2_weight])
    za = ga.along_z()
    xa = ga.first()
    kept_offsets, kept_count, dec_owner, ln1_gain, dec_bias, fc1_bias = held(
        (kept_offsets, kept_count, dec_owner, ln1_gain, dec_bias, fc1_bias), *ga.sent
    )
    wide = max(fc1_bias.shape[0], 128)
    sizes = (dev.size["z"], dev.size["y"], dev.size["x"])
    lanes = -(-windows // 128) * 128
    meta, place_row, info_send = pl.pallas_call(
        functools.partial(describe_kernel, lay, sizes, per_peer),
        name="describe",
        in_specs=[SMEM, SMEM, SMEM, VMEM, VMEM],
        out_specs=[SMEM, VMEM, VMEM],
        out_shape=[sd((16,), jnp.int32), sd((1, R), jnp.int32), sd((total, wide), BF)],
        scratch_shapes=[pltpu.VMEM((8, lanes), F32), pltpu.VMEM((lanes, wide), F32)],
        compiler_params=params(),
    )(lax.axis_index("dp").astype(jnp.int32).reshape(1), kept_count, res_id, dec_owner.reshape(1, windows),
      kept_offsets)
    eight = [ln1_gain, ln1_bias, query_bias, value_bias, out_bias, ln2_gain, ln2_bias, fc2_bias]
    vectors = eight + [fc1_bias, dec_bias, mask_token]
    line = lambda v: jnp.pad(v, ((0, 0), (0, wide - v.shape[1])))
    sheet = jnp.concatenate(
        [line(jnp.stack(eight)), line(fc1_bias[None, :]), line(jnp.stack([dec_bias, mask_token]))], axis=0
    )
    packed = jnp.concatenate(
        [jnp.broadcast_to(sheet[None], (count,) + sheet.shape), info_send.reshape(count, per_peer, wide)],
        axis=1,
    )
    ya = ga.second(packed)
    rest = lax.all_gather(
        held(jnp.concatenate([fc1_weight, out_weight, dec_weight], axis=1), *za),
        "dp",
        axis=0,
        tiled=True,
    )
    packed = lax.all_to_all(packed, "dp", 0, 0, tiled=True)
    n_vec = eight[0].shape[0]
    vecs = packed[:, :8, :n_vec].transpose(1, 0, 2).reshape(8, D).astype(F32)
    bf1 = packed[:, 8, : fc1_bias.shape[0]].reshape(1, hidden).astype(F32)
    vec_dec = packed[:, 9:11, : dec_bias.shape[0]].transpose(1, 0, 2).reshape(2, dec_width).astype(F32)
    info_got = packed[:, 11:].reshape(total, wide)

    w_out_spec = spec((D, D), lambda *_: (0, hidden // D))
    first_dec, dec_half = 2 * (hidden + D) // dec_width, dec_width // 2
    w_dec_specs = [spec((D, dec_half), lambda *_, i=i: (0, first_dec + i)) for i in range(2)]
    tile = R // 3
    rows_of = lambda width: spec((tile, width), lambda i: (i, 0))
    x_rows, h_one = pl.pallas_call(
        functools.partial(first_norm_kernel, lay),
        name="first_norm",
        grid=(3,),
        in_specs=[SMEM, whole((vis, D)), whole((8, D))],
        out_specs=[rows_of(D), rows_of(D)],
        out_shape=[sd((R, D), BF), sd((R, D), BF)],
        compiler_params=params(),
        cost_estimate=cost(2 * R * vis * D, 4e6, weight=0.02),
    )(meta, held(tokens, za), vecs)

    from_a = ga.swap(h_one)

    wins = 16
    steps = total // wins
    cells_w, rows_w = wins * GRID, wins * LANE_SLOTS
    by_step = lambda height, width: spec((height, width), lambda i: (i, 0))
    info_spec = by_step(wins, info_got.shape[1])
    de_send, owner_sums = pl.pallas_call(
        functools.partial(owner_kernel, slots, wins),
        name="owner_side",
        grid=(steps,),
        in_specs=[by_step(cells_w, dec_width), info_spec],
        out_specs=[by_step(rows_w, dec_width), whole((8, dec_width))],
        out_shape=[sd((total * LANE_SLOTS, dec_width), BF), sd((8, dec_width), F32)],
        compiler_params=params(),
        cost_estimate=cost(1e9, 3e6, weight=0.02),
    )(dec_cot, held(info_got, h_one, *ga.sent))

    zc = gc.along_z(*from_a)
    (w_qkv,) = ga.result(meta, de_send)
    group = 4
    parts = HEADS // group
    gw = group * head_dim
    chunk = lay.large_pad // 5
    p_big_t = sd((group, lay.large_pad, lay.large_pad), BF)
    p_small_t = sd((group, images - 1, lay.small_pad, lay.small_pad), BF)

    def attend(i, h_rows):
        col_of = lambda base_: spec((D, gw), lambda _: (0, base_ * parts + i))
        return pl.pallas_call(
            functools.partial(attention_kernel, lay, chunk, head_dim),
            name="attention",
            grid=(1,),
            in_specs=[SMEM, whole((R, D)), col_of(0), col_of(1), col_of(2),
                      spec((8, gw), lambda _: (0, i))],
            out_specs=[whole((R, gw))] * 3 + [whole(p_big_t.shape), whole(p_small_t.shape), whole((R, gw))],
            out_shape=[sd((R, gw), BF)] * 3 + [p_big_t, p_small_t, sd((R, gw), BF)],
            scratch_shapes=[pltpu.VMEM((2 * lay.large_pad, lay.large_pad), F32)],
            compiler_params=params(),
            cost_estimate=cost(2 * R * D * D + 2e9, 8e6, 1e6),
        )(meta, h_rows, w_qkv, w_qkv, w_qkv, vecs)

    attn = [attend(0, h_one)]
    gc.first(attn[0][5])
    attn.append(attend(1, held(h_one, attn[0][5], *gc.sent)))
    gc.second(attn[1][5])
    attn.append(attend(2, held(h_one, attn[1][5], *gc.sent)))
    swapped = gc.swap(attn[2][5])
    de_got = lax.all_to_all(
        held(de_send, attn[1][5]).reshape(count, per_peer * LANE_SLOTS, dec_width), "dp", 0, 0, tiled=True
    ).reshape(total * LANE_SLOTS, dec_width)

    att = [a[5] for a in attn]

    ht = hidden // 6
    row_dev, row_two = D // count, hidden // count
    chips = count // 2
    r_one, h_two, act_h, d_gelu = pl.pallas_call(
        functools.partial(feed_kernel, parts, R // 24),
        name="feed",
        grid=(6,),
        in_specs=[whole((R, gw))] * parts
        + [w_out_spec, whole((8, D)), whole((R, D)), spec((D, ht), lambda j: (0, j)),
           spec((1, ht), lambda j: (0, j))],
        out_specs=[whole((R, D)), whole((R, D))] + [spec((R, ht), lambda j: (0, j))] * 2,
        out_shape=[sd((R, D), F32), sd((R, D), BF), sd((R, hidden), BF), sd((R, hidden), BF)],
        scratch_shapes=[pltpu.VMEM((R, ht), F32)],
        compiler_params=params(),
        cost_estimate=cost(2 * R * D * (hidden + D), 2.5e7, 6e6),
    )(*att, rest, vecs, held(x_rows, *gc.sent), rest, bf1)

    ht = hidden // 4
    nz, ny, nx = sizes
    part = pl.BlockSpec(
        (ny, nx, 1, row_two, D // 2), lambda j, at: (0, 0, lax.rem(at[0] - j + nz, nz), 0, 0)
    )
    ht = hidden // nz
    w_two, e_send, dy, own_dec, sent_dec, db_two = pl.pallas_call(
        functools.partial(join_kernel, row_dev, sizes),
        name="join",
        grid_spec=pltpu.PrefetchScalarGridSpec(
            num_scalar_prefetch=1,
            grid=(nz,),
            in_specs=[spec((R, ht), lambda j, _: (0, j)), part, part, part, part, whole((8, D)),
                      whole((R, D)), *w_dec_specs, whole((2, dec_width)), whole((1, R)),
                      whole((total * LANE_SLOTS, dec_width))],
            out_specs=[spec((2 * ny * nx, row_two, D), lambda j, _: (j, 0, 0)),
                       whole((total * LANE_SLOTS, dec_width)), whole((R, D)),
                       whole((chips, row_dev, dec_width)), whole((chips, row_dev, dec_width)), whole((1, D))],
            scratch_shapes=[pltpu.VMEM((R, D), F32)],
        ),
        out_shape=[sd((count, row_two, D), BF), sd((total * LANE_SLOTS, dec_width), BF), sd((R, D), BF),
                   sd((chips, row_dev, dec_width), BF), sd((chips, row_dev, dec_width), BF), sd((1, D), F32)],
        compiler_params=params(),
        cost_estimate=cost(2 * R * D * hidden + 10 * R * D * dec_width, 2e7),
    )(meta, act_h, gc.part_a, gc.part_b, gc.from_a, gc.from_b, vecs, r_one, rest, rest, vec_dec, place_row,
      de_got)
    w_two = w_two.reshape(hidden, D)
    ht = hidden // 4

    e_got = lax.all_to_all(
        e_send.reshape(count, per_peer * LANE_SLOTS, dec_width), "dp", 0, 0, tiled=True
    ).reshape(total * LANE_SLOTS, dec_width)

    held_chips = ht // (2 * row_two)
    tile_two = spec((held_chips, row_two, D), lambda j: (j, 0, 0))
    tile_one = spec((chips, row_dev, ht), lambda j: (0, 0, j))
    dh, own_two, sent_two, own_one, sent_one, db_one = pl.pallas_call(
        functools.partial(feed_back_kernel, row_dev, row_two),
        name="feed_back",
        grid=(4,),
        in_specs=[SMEM, whole((R, D)), spec((ht, D), lambda j: (j, 0)), spec((R, ht), lambda j: (0, j)),
                  spec((R, ht), lambda j: (0, j)), spec((D, ht), lambda j: (0, j)), whole((R, D))],
        out_specs=[whole((R, D)), tile_two, tile_two, tile_one, tile_one, spec((1, ht), lambda j: (0, j))],
        out_shape=[sd((R, D), F32)] + [sd((chips, row_two, D), BF)] * 2
        + [sd((chips, row_dev, hidden), BF)] * 2 + [sd((1, hidden), F32)],
        scratch_shapes=[pltpu.VMEM((D, R), BF)],
        compiler_params=params(),
        cost_estimate=cost(8 * R * D * hidden, 4e7, weight=20),
    )(meta, dy, w_two, act_h, d_gelu, rest, h_two)
    s_two = Scatter(dev, [(own_two, sent_two)], meta)
    s_one = Scatter(dev, [(own_one, sent_one), (own_dec, sent_dec)], meta)
    c_two, c_one = s_two.swap(), s_one.swap()

    grad_spec = whole((chips, row_dev, D))
    dr, d_att, own_out, sent_out, sums_two = pl.pallas_call(
        functools.partial(out_back_kernel, row_dev, parts),
        name="out_back",
        grid=(3,),
        in_specs=[SMEM, rows_of(D), rows_of(D), rows_of(D), whole((8, D)), w_out_spec]
        + [rows_of(gw)] * parts,
        out_specs=[rows_of(D), rows_of(D), grad_spec, grad_spec, whole((8, D))],
        out_shape=[sd((R, D), F32), sd((R, D), BF)] + [sd((chips, row_dev, D), BF)] * 2
        + [sd((8, D), F32)],
        scratch_shapes=[pltpu.VMEM((D, D), F32)],
        compiler_params=params(),
        cost_estimate=cost(4 * R * D * D, 2e7, weight=20),
    )(meta, dh, r_one, dy, vecs, rest, *att)
    s_two.add(dr, *c_two)
    near = s_two.near()

    def attend_back(i, d_att_rows):
        q_rows, k_rows, v_rows, prob_l, prob_s, _ = attn[i]
        grad_shape = (chips, row_dev, 3 * gw)
        return pl.pallas_call(
            functools.partial(attention_back_kernel, row_dev, lay, chunk, head_dim),
            name="attention_back",
            grid=(1,),
            in_specs=[SMEM, whole((R, D))] + [whole((R, gw))] * 3
            + [whole(p_big_t.shape), whole(p_small_t.shape), spec((R, gw), lambda _: (0, i))],
            out_specs=[whole((R, gw))] * 3 + [whole(grad_shape)] * 2 + [whole((8, gw))],
            out_shape=[sd((R, gw), BF)] * 3 + [sd(grad_shape, BF)] * 2 + [sd((8, gw), F32)],
            scratch_shapes=[pltpu.VMEM((2 * lay.large_pad, lay.large_pad), F32),
                            pltpu.VMEM((2 * lay.large_pad, lay.large_pad), BF)],
            compiler_params=params(),
            cost_estimate=cost(2 * R * D * D + 3e9, 1e7, weight=20),
        )(meta, h_one, q_rows, k_rows, v_rows, prob_l, prob_s, d_att_rows)

    back = [attend_back(0, held(d_att, s_two.blocks[0], e_got, *c_one))]
    far = s_two.far(back[0][0], *near)
    s_one.add(back[0][0], *near)
    near = s_one.near()
    s_mid = Scatter(dev, [(own_out, sent_out), back[0][3:5]], meta)
    c_mid = s_mid.swap(back[0][0])
    back.append(attend_back(1, held(d_att, back[0][0], s_one.blocks[0])))
    lines_two, z_two = finish(dev, meta, [s_two], True, back[1][0], *far)
    far = s_one.far(back[1][0], *near)
    s_mid.more(*back[1][3:5])
    c_mid += s_mid.swap(back[1][0])
    back.append(attend_back(2, held(d_att, back[1][0], lines_two[0], *near)))
    s_last = Scatter(dev, [back[2][3:5]], meta)
    c_last = s_last.swap(back[2][0])
    s_mid.add(back[2][0], *c_mid)
    near = s_mid.near() + s_mid.far()
    lines_one, z_one = finish(dev, meta, [s_one], True, back[2][0], *far, z_two, s_mid.blocks[0])

    dqkv = [b[i] for i in range(3) for b in back]
    widths = (ln1_gain.shape[0], fc1_bias.shape[0], dec_bias.shape[0])
    grad_tokens, sheet = pl.pallas_call(
        functools.partial(first_back_kernel, lay, parts, count, widths),
        name="first_back",
        grid=(3,),
        in_specs=[SMEM] + [rows_of(gw)] * (3 * parts) + [whole((8, gw))] * parts
        + [whole((D, 3 * D)), rows_of(D), rows_of(D), whole((8, D)), whole((8, D)), whole((1, D)), whole((1, hidden)),
           whole((8, dec_width))],
        out_specs=[whole((vis, D)), whole((11, count, 128))],
        out_shape=[sd((vis, D), BF), sd((11, count, 128), F32)],
        scratch_shapes=[pltpu.VMEM((8, D), F32), pltpu.VMEM((R, D), BF)],
        compiler_params=params(),
        cost_estimate=cost(2 * R * D * 3 * D + 2 * R * vis * D, 2e7, weight=20),
    )(meta, *dqkv, *[b[5] for b in back], w_qkv, x_rows, held(dr, s_mid.blocks[0], *lines_one), vecs, sums_two,
      db_two, db_one, owner_sums)
    blocks = -(-11 // row_dev)
    vec_width = -(-128 * blocks // 384) * 384
    ride = jnp.pad(sheet, ((0, blocks * row_dev - 11), (0, 0), (0, 0)))
    ride = ride.reshape(blocks, row_dev, count, 128).transpose(2, 1, 0, 3).reshape(count, row_dev, -1)
    ride = jnp.pad(ride, ((0, 0), (0, 0), (0, vec_width - 128 * blocks))).astype(BF)
    ride = ride.reshape(chips, 2, row_dev, vec_width)
    even = dev.coord("c") == 0
    s_last.more(
        jnp.where(even, ride[:, 0], ride[:, 1]), jnp.where(even, ride[:, 1], ride[:, 0])
    )
    c_last += s_last.swap(grad_tokens)
    s_last.add(grad_tokens, *near, *c_last)
    near = s_last.near() + s_last.far()

    decoded = pl.pallas_call(
        functools.partial(decode_kernel, slots, wins),
        name="decode",
        grid=(steps,),
        in_specs=[by_step(rows_w, dec_width), info_spec, whole((2, dec_width))],
        out_specs=by_step(cells_w, dec_width),
        out_shape=sd((total * GRID, dec_width), BF),
        scratch_shapes=[pltpu.VMEM((3 * 32, dec_width // 2), BF)],
        compiler_params=params(),
        cost_estimate=cost(1e9, 7e6, weight=20),
    )(held(e_got, s_last.blocks[0], z_one), info_got, vec_dec)


    lines_late, z_late = finish(dev, meta, [s_mid, s_last], False, decoded, *near)
    (grad_two,) = totals(z_two, [s_two])
    grad_one, grad_dec = totals(z_one, [s_one])
    grad_out, grad_qkv, *vec_grads = last_sums(
        z_late, [s_mid, s_last], D, gw, [v.shape[0] for v in vectors]
    )
    vec_grads = [v.reshape(-1) for v in vec_grads]
    (gg1, gb1, gbq, gbv, gbo, gg2, gb2, gbf2, gbf1, gbdec, gmask) = vec_grads
    return (decoded, grad_tokens, gg1, gb1, grad_qkv, gbq, gbv, grad_out, gbo, gg2, gb2, grad_one,
            gbf1, grad_two, gbf2, grad_dec, gbdec, gmask)


def solution(mesh):
    mat, vec = P("dp", None), P("dp")
    in_specs = (mat, vec, vec, mat, vec, vec, mat, vec, vec, vec, mat, vec, mat, vec, mat, vec, vec,
                mat, vec, vec, vec, mat)
    out_specs = (mat, mat, vec, vec, mat, vec, vec, mat, vec, vec, vec, mat, vec, mat, vec, mat, vec,
                 vec)
    return jax.shard_map(local, mesh=mesh, in_specs=in_specs, out_specs=out_specs, check_vma=False)
```

```python
import functools

import jax
import jax.numpy as jnp
from jax import lax
from jax.experimental import pallas as pl
from jax.experimental.pallas import tpu as pltpu
from jax.sharding import PartitionSpec as P

HEADS = 12
GRID = 14
NORM_EPS = 1e-06
MASK_FILL = -1e30
BF = jnp.bfloat16
F32 = jnp.float32
MIB = 1 << 20


class Slice:
    def __init__(self, count):
        chips = count // 2
        side = 2 if chips <= 16 else 4
        self.count = count
        self.size = {"c": 2, "x": side, "y": side, "z": chips // (side * side)}
        self.stride = {"c": 1, "x": 2, "y": 2 * side, "z": 2 * side * side}

    def coord(self, axis):
        return (lax.axis_index("dp") // self.stride[axis]) % self.size[axis]

    def shift(self, values, axis, steps):
        stride, size = self.stride[axis], self.size[axis]
        pairs = []
        for source in range(self.count):
            place = (source // stride) % size
            pairs.append((source, source + ((place + steps) % size - place) * stride))
        return lax.ppermute(values, "dp", pairs)

    def copies(self, values, axis):
        return [values] + [self.shift(values, axis, k) for k in range(1, self.size[axis])]

    def shift_plane(self, values, ky, kx):
        pairs = []
        for source in range(self.count):
            target = source
            for axis, steps in (("y", ky), ("x", kx)):
                stride, size = self.stride[axis], self.size[axis]
                place = (source // stride) % size
                target += ((place + steps) % size - place) * stride
            pairs.append((source, target))
        return lax.ppermute(values, "dp", pairs)

    def groups(self, axes):
        seen, found = set(), []
        for first in range(self.count):
            if first in seen:
                continue
            members = [first]
            for axis in axes:
                members = [
                    m + k * self.stride[axis] for m in members for k in range(self.size[axis])
                ]
            found.append(members)
            seen.update(members)
        return found


def cost(flops, moved, trans=0, weight=1):
    return pl.CostEstimate(
        flops=int(weight * flops), bytes_accessed=int(weight * moved), transcendentals=int(trans)
    )


def params():
    return pltpu.CompilerParams(vmem_limit_bytes=60 * MIB)


def whole(shape):
    zeros = (0,) * len(shape)
    return pl.BlockSpec(shape, lambda *_: zeros)


SMEM = pl.BlockSpec(memory_space=pltpu.SMEM)
VMEM = pl.BlockSpec(memory_space=pltpu.VMEM)


def assemble_kernel(sizes, widths, place, part_a, part_b, from_a, from_b, *outs):
    _, ny, nx = sizes
    own_y, own_x, own_c = place[1], place[2], place[3]
    for ky in range(ny):
        at_y = lax.rem(own_y - ky + ny, ny)
        for kx in range(nx):
            at_x = lax.rem(own_x - kx + nx, nx)
            chip = at_y * nx + at_x
            for core, left, right in ((own_c, part_a, part_b), (1 - own_c, from_a, from_b)):
                row, start = chip * 2 + core, 0
                for out, width in zip(outs, widths):
                    half = width // 2
                    out[0, row, :, :half] = left[ky, kx, 0, :, start : start + half]
                    out[0, row, :, half:] = right[kx, ky, 0, :, start : start + half]
                    start += half


def held(values, *others):
    others = [o for o in others if o is not None]
    return lax.optimization_barrier((values, others))[0] if others else values


class Gather:
    def __init__(self, dev, shards):
        self.dev = dev
        self.rows = shards[0].shape[0]
        self.widths = [s.shape[1] for s in shards]
        self.half = sum(self.widths) // 2
        if len(shards) == 1:
            self.local = shards[0]
        else:
            halves = [s.shape[1] // 2 for s in shards]
            self.local = jnp.concatenate(
                [s[:, :h] for s, h in zip(shards, halves)]
                + [s[:, h:] for s, h in zip(shards, halves)],
                axis=1,
            )

    def along_z(self, *after):
        self.arrived = self.dev.copies(held(self.local, *after), "z")
        return self.arrived

    def first(self, *after):
        line = jnp.stack(held(self.arrived, *after))
        part_a, part_b = line[:, :, : self.half], line[:, :, self.half :]
        self.sent = [part_a, part_b]
        self.arrived = self.dev.copies(part_a, "x"), self.dev.copies(part_b, "y")
        return self.arrived[0] + self.arrived[1]

    def second(self, *after):
        part_a, part_b = (jnp.stack(v) for v in held(self.arrived, *after))
        self.sent = [part_a, part_b]
        self.arrived = self.dev.copies(part_a, "y"), self.dev.copies(part_b, "x")
        return self.arrived[0] + self.arrived[1]

    def swap(self, *after):
        self.part_a, self.part_b = (jnp.stack(v) for v in held(self.arrived, *after))
        self.sent = [self.part_a, self.part_b]
        self.from_a = self.dev.shift(self.part_a, "c", 1)
        self.from_b = self.dev.shift(self.part_b, "c", 1)
        return [self.from_a, self.from_b]

    def result(self, place, *after):
        dev, rows = self.dev, self.rows
        nz, ny, nx = sizes = (dev.size["z"], dev.size["y"], dev.size["x"])
        kind = self.local.dtype
        from_a, from_b = held((self.from_a, self.from_b), *after)
        part = pl.BlockSpec((ny, nx, 1, rows, self.half), lambda k, _: (0, 0, k, 0, 0))
        outs = pl.pallas_call(
            functools.partial(assemble_kernel, sizes, self.widths),
            name="assemble",
            grid_spec=pltpu.PrefetchScalarGridSpec(
                num_scalar_prefetch=1,
                grid=(nz,),
                in_specs=[part] * 4,
                out_specs=[
                    pl.BlockSpec(
                        (1, 2 * ny * nx, rows, w), lambda k, at: (lax.rem(at[0] - k + nz, nz), 0, 0, 0)
                    )
                    for w in self.widths
                ],
            ),
            out_shape=[jax.ShapeDtypeStruct((nz, 2 * ny * nx, rows, w), kind) for w in self.widths],
            compiler_params=params(),
            cost_estimate=cost(0, 4 * dev.count * rows * sum(self.widths)),
        )(place, self.part_a, self.part_b, from_a, from_b)
        return [o.reshape(dev.count * rows, w) for o, w in zip(outs, self.widths)]


def chip_sum_kernel(sizes, pairs, place, *refs):
    nz, ny, nx = sizes
    owns, gots, outs = refs[:pairs], refs[pairs : 2 * pairs], refs[2 * pairs :]
    own_y, own_x = place[1], place[2]
    for ky in range(ny):
        for kx in range(nx):
            at = lax.rem(own_y + ky, ny) * nx + lax.rem(own_x + kx, nx)
            for z in range(nz):
                start = 0
                for own, got in zip(owns, gots):
                    width = own.shape[-1]
                    chip = z * ny * nx + at
                    outs[ky * nx + kx][z, :, start : start + width] = own[chip] + got[chip]
                    start += width


class Scatter:
    def __init__(self, dev, pairs, place):
        self.dev, self.place = dev, place
        self.own = [p[0] for p in pairs]
        self.sent = [p[1] for p in pairs]
        self.rows = self.own[0].shape[1]
        self.widths = [p[0].shape[2] for p in pairs]
        self.got = []

    def swap(self, *after):
        waiting = held(self.sent[len(self.got) :], *after)
        found = [self.dev.shift(v, "c", 1) for v in waiting]
        self.got = self.got + found
        return found

    def more(self, own, sent):
        self.own, self.sent = self.own + [own], self.sent + [sent]
        self.widths = self.widths + [own.shape[2]]

    def add(self, *after):
        self.got = held(self.got, *after)
        dev, rows = self.dev, self.rows
        sizes = (dev.size["z"], dev.size["y"], dev.size["x"])
        plane, width = sizes[1] * sizes[2], sum(self.widths)
        pairs, chips = len(self.own), dev.count // 2
        self.steps = next(n for n in (4, 3, 2, 1) if all(w % (128 * n) == 0 for w in self.widths))
        tiles = [w // self.steps for w in self.widths]
        halves = [pl.BlockSpec((chips, rows, t), lambda i: (0, 0, i)) for t in tiles]
        out_tile = pl.BlockSpec((sizes[0], rows, sum(tiles)), lambda i: (0, 0, i))
        self.blocks = pl.pallas_call(
            functools.partial(chip_sum_kernel, sizes, pairs),
            name="chip_sum",
            grid=(self.steps,),
            out_shape=[jax.ShapeDtypeStruct((sizes[0], rows, width), BF)] * plane,
            in_specs=[SMEM] + halves + halves,
            out_specs=[out_tile] * plane,
            compiler_params=params(),
            cost_estimate=cost(0, 6 * dev.count // 2 * rows * width),
        )(self.place, *self.own, *self.got)
        self.terms = [self.blocks[0]]
        return self.blocks

    def near(self, *after):
        return self._plane(lambda ky, kx: ky == 0 or kx == 0, after)

    def far(self, *after):
        return self._plane(lambda ky, kx: ky > 0 and kx > 0, after)

    def _plane(self, chosen, after):
        dev, ny, nx = self.dev, self.dev.size["y"], self.dev.size["x"]
        blocks = held(self.blocks, *after)
        found = [
            dev.shift_plane(blocks[ky * nx + kx], ky, kx)
            for ky in range(ny)
            for kx in range(nx)
            if (ky or kx) and chosen(ky, kx)
        ]
        self.terms += found
        return found


def line_kernel(nz, counts, place, *refs):
    terms, outs = refs[: sum(counts)], refs[sum(counts) :]
    joined = len(outs) == 1
    rows = outs[0].shape[-2]
    for k in range(nz):
        at, first, start = k if joined else lax.rem(place[0] + k, nz), 0, 0
        out = outs[0].at[k] if joined else outs[k]
        for count in counts:
            group = terms[first : first + count]
            total = group[0][at].astype(F32)
            for term in group[1:]:
                total += term[at].astype(F32)
            first, width = first + count, total.shape[1]
            for piece in range(total.shape[0] // rows):
                out[:, start : start + width] = total[piece * rows : (piece + 1) * rows].astype(BF)
                start += width


def finish(dev, place, scatters, joined, *after):
    nz, rows = dev.size["z"], min(s.rows for s in scatters)
    width = sum(w * (s.rows // rows) for s in scatters for w in s.widths)
    terms = held([t for s in scatters for t in s.terms], *after)
    blocks = pl.pallas_call(
        functools.partial(line_kernel, nz, [len(s.terms) for s in scatters]),
        name="plane_sum",
        out_shape=[jax.ShapeDtypeStruct((nz, rows, width), BF)]
        if joined
        else [jax.ShapeDtypeStruct((rows, width), BF)] * nz,
        in_specs=[SMEM] + [VMEM] * len(terms),
        out_specs=[VMEM] * (1 if joined else nz),
        compiler_params=params(),
        cost_estimate=cost(0, 8 * nz * rows * width),
    )(place, *terms)
    if joined:
        line = lax.all_to_all(
            blocks[0], "dp", 0, 0, axis_index_groups=dev.groups("z"), tiled=True
        )
        return blocks, line
    return blocks, [blocks[0]] + [dev.shift(blocks[k], "z", k) for k in range(1, nz)]


def totals(arrived, scatters):
    if isinstance(arrived, list):
        total = sum(v.astype(F32) for v in arrived)
    else:
        total = jnp.sum(arrived.astype(F32), axis=0)
    rows, start, out = total.shape[0], 0, []
    for s in scatters:
        pieces, width = s.rows // rows, sum(s.widths)
        parts = [total[:, start + i * width : start + (i + 1) * width] for i in range(pieces)]
        whole_rows = parts[0] if pieces == 1 else jnp.concatenate(parts, axis=0)
        start += pieces * width
        tiles, span = [w // s.steps for w in s.widths], width // s.steps
        for t, tile in enumerate(tiles):
            at = sum(tiles[:t])
            found = [whole_rows[:, i * span + at : i * span + at + tile] for i in range(s.steps)]
            out.append(found[0] if len(found) == 1 else jnp.concatenate(found, axis=1))
    return out


def last_sums_kernel(count, moves, vectors_at, *refs):
    terms, outs = refs[:count], refs[count:]
    for start, width, out, at in moves:
        total = terms[0][:, start : start + width].astype(F32)
        for term in terms[1:]:
            total += term[:, start : start + width].astype(F32)
        outs[out][:, at : at + width] = total
    for out, (row, lane) in zip(outs[2:], vectors_at):
        lanes = slice(lane, lane + out.shape[1])
        total = terms[0][:, lanes].astype(F32)
        for term in terms[1:]:
            total += term[:, lanes].astype(F32)
        out[...] = total[row : row + 1]


def last_sums(arrived, scatters, model, head_cols, lengths):
    rows, width = arrived[0].shape
    moves, rides, start, first = [], [], 0, True
    part = -1
    for s in scatters:
        tiles, span = [w // s.steps for w in s.widths], sum(s.widths) // s.steps
        for t, tile in enumerate(tiles):
            part = part if first else part + 1
            for i in range(s.steps):
                source = start + i * span + sum(tiles[:t])
                if first:
                    moves.append((source, tile, 0, i * tile))
                    continue
                if s is scatters[-1] and t == len(tiles) - 1:
                    rides.append(source)
                    continue
                piece = min(tile, head_cols)
                for k in range(0, tile, piece):
                    block, inside = divmod(i * tile + k, head_cols)
                    moves.append((source + k, piece, 1, block * model + part * head_cols + inside))
            if first:
                part, first = -1, False
        start += sum(s.widths)
    ride_tile = scatters[-1].widths[-1] // scatters[-1].steps
    vectors_at = []
    for i in range(len(lengths)):
        step, inside = divmod(128 * (i // rows), ride_tile)
        vectors_at.append((i % rows, rides[step] + inside))
    shapes = [(rows, model), (rows, 3 * model)] + [(1, n) for n in lengths]
    return pl.pallas_call(
        functools.partial(last_sums_kernel, len(arrived), moves, vectors_at),
        name="last_sums",
        grid=(1,),
        in_specs=[whole((rows, width))] * len(arrived),
        out_specs=[whole(v) for v in shapes],
        out_shape=[jax.ShapeDtypeStruct(v, F32) for v in shapes],
        compiler_params=params(),
    )(*arrived)


def split_cores(value, rows, core, own, sent):
    if rows % 8 == 0:
        parts = value.reshape(-1, 2, rows, value.shape[1])
        own[...] = jnp.where(core == 0, parts[:, 0], parts[:, 1]).astype(BF)
        sent[...] = jnp.where(core == 0, parts[:, 1], parts[:, 0]).astype(BF)
        return
    for chip in range(value.shape[0] // (2 * rows)):
        first = value[2 * chip * rows : (2 * chip + 1) * rows]
        second = value[(2 * chip + 1) * rows : (2 * chip + 2) * rows]
        own[chip] = jnp.where(core == 0, first, second).astype(BF)
        sent[chip] = jnp.where(core == 0, second, first).astype(BF)


def dot(left, right):
    return jnp.dot(left, right, preferred_element_type=F32)


def dot_rows(left, right):
    return lax.dot_general(left, right, (((0,), (0,)), ((), ())), preferred_element_type=F32)


def dot_cols(left, right):
    return lax.dot_general(left, right, (((1,), (1,)), ((), ())), preferred_element_type=F32)


def one_hot(column, row):
    return jnp.where(column == row, 1.0, 0.0).astype(BF)


def row_sum(values):
    return jnp.sum(values, axis=0, keepdims=True)


def normalised(values):
    mean = jnp.mean(values, axis=1, keepdims=True)
    centered = values - mean
    variance = jnp.mean(centered * centered, axis=1, keepdims=True)
    scale = lax.rsqrt(variance + NORM_EPS)
    return centered * scale, scale


def norm_back(unit, scale, gain, grad):
    weighted = grad * gain
    first = jnp.mean(weighted, axis=1, keepdims=True)
    second = jnp.mean(weighted * unit, axis=1, keepdims=True)
    return scale * (weighted - first - unit * second)


class Layout:
    def __init__(self, images, slots):
        self.images, self.slots = images, slots
        self.small, self.large = GRID * slots, 4 * GRID * slots
        self.small_pad = -(-self.small // 16) * 16
        self.large_pad = -(-self.large // 16) * 16
        self.starts = [self.large_pad + i * self.small_pad for i in range(images - 1)]
        self.rows = self.large_pad + (images - 1) * self.small_pad

    def rows_of(self, row, big):
        small_id = jnp.maximum(row - self.large_pad, 0) // self.small_pad
        in_large = row < self.large_pad
        offset = jnp.where(in_large, row, row - self.large_pad - small_id * self.small_pad)
        real = offset < jnp.where(in_large, self.large, self.small)
        image = jnp.where(in_large, big, small_id + jnp.where(small_id >= big, 1, 0))
        window = (
            GRID * image + jnp.where(image > big, 3 * GRID, 0) + offset // self.slots
        )
        return window, offset % self.slots, real

    def source(self, row, big):
        window, slot, real = self.rows_of(row, big)
        return jnp.where(real, window * self.slots + slot, -1)

    def key_mask(self, size, real, kept):
        lane = lax.broadcasted_iota(jnp.int32, (1, size), 1)
        live = (lane < real) & (lane % self.slots < kept)
        return jnp.where(live, 0.0, MASK_FILL)


def spread_lanes(width, full):
    lane = lax.broadcasted_iota(jnp.int32, (1, full), 1) % width
    return lax.broadcasted_iota(jnp.int32, (128, 1), 0) == lane


def own_lanes(count, width, full):
    lane = lax.broadcasted_iota(jnp.int32, (1, full), 1) // width
    return lax.broadcasted_iota(jnp.int32, (count, 1), 0) == lane


def pack_rows(count, width, joined, out, first):
    vectors, full = joined.shape
    mask = own_lanes(count, width, full)
    split = jnp.concatenate(
        [jnp.where(mask, joined[v : v + 1, :], 0.0) for v in range(vectors)], axis=0
    )
    high = split.astype(BF)
    rest = split - high.astype(F32)
    middle = rest.astype(BF)
    low = (rest - middle.astype(F32)).astype(BF)
    lanes = jnp.where(spread_lanes(width, full), 1.0, 0.0).astype(BF)
    found = dot_cols(jnp.concatenate([high, middle, low], axis=0), lanes)
    size = vectors * count
    total = found[:size] + found[size : 2 * size] + found[2 * size :]
    for v in range(vectors):
        out[first + v] = total[v * count : (v + 1) * count]


LANE_SLOTS = 8
BIG, KEPT = 4, 5
FIELDS = 4


def describe_kernel(lay, dims, per_peer, index, counts, sides, owner_in, offsets_in,
                    meta, place_out, info_out, owners, cells):
    images, slots = lay.images, lay.slots
    windows, padded = offsets_in.shape[0], owners.shape[1]
    _, ny, nx = dims
    me = index[0]
    meta[0] = me // (2 * nx * ny)
    meta[1] = (me // (2 * nx)) % ny
    meta[2] = (me // 2) % nx
    meta[3] = me % 2
    big, kept_big = jnp.int32(0), jnp.int32(0)
    for i in range(images):
        big += i * sides[i]
        kept_big += sides[i] * counts[i]
    meta[BIG] = big
    meta[KEPT] = kept_big
    for i in range(images - 1):
        meta[KEPT + 1 + i] = jnp.where(i < big, counts[i], counts[i + 1])

    owners[...] = jnp.full(owners.shape, -1.0, F32)
    owners[:, :windows] = jnp.broadcast_to(owner_in[...], (8, windows)).astype(F32)
    row = owners[0:1, :]
    col = owners[...].T[:, 0:1]
    before = lax.broadcasted_iota(jnp.int32, (padded, padded), 0)
    after = lax.broadcasted_iota(jnp.int32, (padded, padded), 1)
    same = jnp.where(col == row, 1.0, 0.0)
    rank_row = jnp.sum(jnp.where(before < after, same, 0.0), axis=0, keepdims=True)
    rank_col = jnp.sum(jnp.where(after < before, same, 0.0), axis=1, keepdims=True)
    bucket_row = jnp.where(row >= 0, row * per_peer + rank_row, -1.0)
    bucket_col = jnp.where(col >= 0, col * per_peer + rank_col, -1.0)

    win = lax.broadcasted_iota(jnp.int32, (padded, 1), 0)
    start = GRID * big
    in_big = (win >= start) & (win < start + 4 * GRID)
    image = jnp.where(in_big, big, win // GRID - jnp.where(win >= start + 4 * GRID, 3, 0))
    kept = jnp.zeros((padded, 1), jnp.int32)
    for i in range(images):
        kept = jnp.where(image == i, counts[i], kept)
    cells[...] = jnp.zeros_like(cells)
    cells[:windows, FIELDS : FIELDS + slots] = offsets_in[...].astype(F32)
    lane = lax.broadcasted_iota(jnp.int32, cells.shape, 1)
    turn = jnp.where(in_big, win - start, win % GRID)
    values = jnp.where(lane == 0, 1.0, cells[...])
    values = jnp.where(lane == 1, kept.astype(F32), values)
    values = jnp.where(lane == 2, turn.astype(F32), values)
    values = jnp.where(lane == 3, jnp.where(in_big, 2.0 * GRID, 1.0 * GRID), values)
    target = lax.broadcasted_iota(jnp.int32, (info_out.shape[0], padded), 0).astype(F32)
    info_out[...] = dot(one_hot(target, bucket_row), values.astype(BF)).astype(BF)

    place = lax.broadcasted_iota(jnp.int32, (1, lay.rows), 1)
    window, slot, real = lay.rows_of(place, big)
    found = jnp.sum(
        jnp.where(win == window, bucket_col * LANE_SLOTS, 0.0), axis=0, keepdims=True
    ).astype(jnp.int32)
    bound = jnp.sum(jnp.where(win == window, kept.astype(F32), 0.0), axis=0, keepdims=True)
    live = real & (slot.astype(F32) < bound)
    place_out[...] = jnp.where(live, found + slot, -1)


def slot_targets(info, slots, wins, axis):
    rows = wins * LANE_SLOTS
    shape = (rows, 1) if axis == 0 else (1, rows)
    spread = (rows, wins) if axis == 0 else (wins, rows)
    owner = lax.broadcasted_iota(jnp.int32, spread, axis) // LANE_SLOTS
    window = lax.broadcasted_iota(jnp.int32, spread, 1 - axis)
    pick = jnp.where(owner == window, 1.0, 0.0).astype(BF)
    fields = dot(pick, info) if axis == 0 else dot_rows(info, pick)
    slot = lax.broadcasted_iota(jnp.int32, shape, axis) % LANE_SLOTS
    field = (lambda i: fields[:, i : i + 1]) if axis == 0 else (lambda i: fields[i : i + 1, :])
    cell = jnp.zeros(shape, F32)
    for j in range(slots):
        cell = cell + jnp.where(slot == j, field(4 + j), 0.0)
    first = (lax.broadcasted_iota(jnp.int32, shape, axis) // LANE_SLOTS) * GRID
    live = slot.astype(F32) < field(1)
    return jnp.where(live, first + cell.astype(jnp.int32), -1)


def owner_kernel(slots, wins, cot, info_in, de_out, sums_out):
    step = pl.program_id(0)
    cells = wins * GRID
    grads = cot[...]
    info = info_in[...]
    cell_lane = lax.broadcasted_iota(jnp.int32, (1, cells), 1)
    want = slot_targets(info, slots, wins, 0)
    pick = one_hot(want, cell_lane)
    picked = dot(pick, grads)
    de_out[...] = picked.astype(BF)
    taken = jnp.sum(jnp.where(want == cell_lane, 1.0, 0.0), axis=0, keepdims=True)
    window = lax.broadcasted_iota(jnp.int32, (wins, cells), 0)
    inside = jnp.where(
        window == lax.broadcasted_iota(jnp.int32, (wins, cells), 1) // GRID, 1.0, 0.0
    ).astype(BF)
    present_row = dot_rows(info, inside)[0:1, :]
    mask_sum = dot(jnp.broadcast_to(present_row - taken, (8, cells)).astype(BF), grads)[:1]

    @pl.when(step == 0)
    def _():
        sums_out[...] = jnp.zeros_like(sums_out)

    sums_out[0:1, :] += row_sum(picked)
    sums_out[1:2, :] += mask_sum


def decode_kernel(slots, wins, got, info_in, vec_dec, out, stacked):
    cells = wins * GRID
    quarter = out.shape[1] // 4
    info = info_in[...]
    depth = stacked.shape[0] // 3

    @pl.when(pl.program_id(0) == 0)
    def _():
        place = lax.broadcasted_iota(jnp.int32, (depth, quarter), 0).astype(F32)
        index = lax.broadcasted_iota(jnp.int32, (depth, quarter), 1).astype(F32) / quarter
        angle = place * (1.0 / jnp.exp(index * jnp.log(F32(10000.0))))
        table = jnp.concatenate([jnp.sin(angle), jnp.cos(angle)], axis=1)
        high = table.astype(BF)
        rest = table - high.astype(F32)
        middle = rest.astype(BF)
        stacked[:depth] = high
        stacked[depth : 2 * depth] = middle
        stacked[2 * depth :] = (rest - middle.astype(F32)).astype(BF)

    cell_row = lax.broadcasted_iota(jnp.int32, (cells, 1), 0)
    chosen = one_hot(cell_row, slot_targets(info, slots, wins, 1))
    filled = jnp.sum(chosen.astype(F32), axis=1, keepdims=True)
    placed = dot(chosen, got[...])
    owner = lax.broadcasted_iota(jnp.int32, (cells, wins), 0) // GRID
    fields = dot(one_hot(owner, lax.broadcasted_iota(jnp.int32, (cells, wins), 1)), info)
    present = fields[:, 0:1]
    turn = fields[:, 2:3].astype(jnp.int32)
    wide = fields[:, 3:4] > GRID
    cell = cell_row % GRID
    along = jnp.where(wide, (turn % 2) * GRID + cell, cell)
    across = jnp.where(wide, turn // 2, turn)
    lane = lax.broadcasted_iota(jnp.int32, (1, 3 * depth), 1) % depth
    shown = present > 0.5
    first = dot(one_hot(jnp.where(shown, along, -1), lane), stacked[...])
    second = dot(one_hot(jnp.where(shown, across, -1), lane), stacked[...])
    bare = present - filled
    half = 2 * quarter
    out[:, :half] = (placed[:, :half] + first + bare * vec_dec[1:2, :half]).astype(BF)
    out[:, half:] = (placed[:, half:] + second + bare * vec_dec[1:2, half:]).astype(BF)


def first_norm_kernel(lay, meta, tokens, vecs, x_out, h_out):
    rows = x_out.shape[0]
    row = lax.broadcasted_iota(jnp.int32, (rows, 1), 0) + pl.program_id(0) * rows
    lane = lax.broadcasted_iota(jnp.int32, (1, tokens.shape[0]), 1)
    moved = dot(one_hot(lay.source(row, meta[BIG]), lane), tokens[...])
    x_out[...] = moved.astype(BF)
    unit, _ = normalised(moved)
    h_out[...] = (unit * vecs[0:1, :] + vecs[1:2, :]).astype(BF)


def softmax_rows(scores):
    top = jnp.max(scores, axis=1, keepdims=True)
    expo = jnp.exp(scores - top)
    return (expo * (1.0 / jnp.sum(expo, axis=1, keepdims=True))).astype(BF)


def attention_kernel(lay, chunk, head_dim, meta, h_in, w_q, w_k, w_v, vecs,
                     q_out, k_out, v_out, pl_out, ps_out, o_out, scores):
    big, small = lay.large_pad, lay.small_pad
    normed = h_in[...]
    q_out[...] = ((dot(normed, w_q[...]) + vecs[2:3, :]) * (head_dim**-0.5)).astype(BF)
    k_out[...] = dot(normed, w_k[...]).astype(BF)
    v_out[...] = (dot(normed, w_v[...]) + vecs[3:4, :]).astype(BF)
    lane = lax.broadcasted_iota(jnp.int32, (1, 2 * head_dim), 1)
    low = lane < head_dim
    halves = (jnp.where(low, 1.0, 0.0).astype(BF), jnp.where(low, 0.0, 1.0).astype(BF))
    mask_l = lay.key_mask(big, lay.large, meta[KEPT])
    masks = [lay.key_mask(small, lay.small, meta[KEPT + 1 + i]) for i in range(lay.images - 1)]
    for pair in range(q_out.shape[1] // (2 * head_dim)):
        cols = slice(pair * 2 * head_dim, (pair + 1) * 2 * head_dim)
        both = jnp.concatenate([q_out[:big, cols] * h for h in halves], axis=0)
        scores[...] = dot_cols(both, k_out[:big, cols])
        for half in range(2):
            for start in range(0, big, chunk):
                part = scores[half * big + start : half * big + start + chunk, :] + mask_l
                pl_out[2 * pair + half, start : start + chunk, :] = softmax_rows(part)
        outs = dot(pl_out[2 * pair : 2 * pair + 2].reshape(2 * big, big), v_out[:big, cols])
        o_out[:big, cols] = jnp.where(low, outs[:big], outs[big:]).astype(BF)
        for i, start in enumerate(lay.starts):
            rows = slice(start, start + small)
            both = jnp.concatenate([q_out[rows, cols] * h for h in halves], axis=0)
            weights = softmax_rows(dot_cols(both, k_out[rows, cols]) + masks[i])
            ps_out[2 * pair, i] = weights[:small]
            ps_out[2 * pair + 1, i] = weights[small:]
            outs = dot(weights, v_out[rows, cols])
            o_out[rows, cols] = jnp.where(low, outs[:small], outs[small:]).astype(BF)


def feed_kernel(parts, chunk, *refs):
    o_in = refs[:parts]
    w_out, vecs, x_in, weight, bias, r_out, h_out, g_out, d_out, hidden = refs[parts:]
    rows_all, width = x_in.shape[0], o_in[0].shape[1]

    @pl.when(pl.program_id(0) == 0)
    def _():
        for start in range(0, rows_all, rows_all // 3):
            rows = slice(start, start + rows_all // 3)
            residual = x_in[rows, :].astype(F32) + vecs[4:5, :]
            for i, o in enumerate(o_in):
                residual += dot(o[rows, :], w_out[i * width : (i + 1) * width, :])
            r_out[rows, :] = residual
            unit, _ = normalised(residual)
            h_out[rows, :] = (unit * vecs[5:6, :] + vecs[6:7, :]).astype(BF)

    hidden[...] = dot(h_out[...], weight[...])
    for start in range(0, rows_all, chunk):
        rows = slice(start, start + chunk)
        u = hidden[rows, :] + bias[...]
        half = 0.5 + 0.5 * lax.erf(u * (0.5**0.5))
        g_out[rows, :] = (u * half).astype(BF)
        density = jnp.exp(u * u * -0.5) * 0.3989422804014327
        d_out[rows, :] = (half + u * density).astype(BF)


def join_kernel(rows_dev, sizes, spot, g_in, part_a, part_b, from_a, from_b, vecs, r_in, w_dec, w_dec_more, vec_dec, place, got,
                w_out, e_out, dy_out, own_out, sent_out, db_out, total):
    step = pl.program_id(0)

    @pl.when(step == 0)
    def _():
        total[...] = r_in[...] + vecs[7:8, :]

    _, ny, nx = sizes
    for ky in range(ny):
        for kx in range(nx):
            chip = lax.rem(spot[1] - ky + ny, ny) * nx + lax.rem(spot[2] - kx + nx, nx)
            for core, left, right in ((spot[3], part_a, part_b), (1 - spot[3], from_a, from_b)):
                half = left.shape[-1]
                w_out[chip * 2 + core, :, :half] = left[ky, kx, 0]
                w_out[chip * 2 + core, :, half:] = right[kx, ky, 0]
    total[...] += dot(g_in[...], w_out[...].reshape(g_in.shape[1], total.shape[1]))

    @pl.when(step == pl.num_programs(0) - 1)
    def _():
        half = w_dec.shape[1]
        y = total[...].astype(BF)
        target = lax.broadcasted_iota(jnp.int32, (e_out.shape[0], 1), 0)
        pick = one_hot(target, place[...])
        grad = dot_rows(pick, got[...]).astype(BF)
        for i, w in enumerate((w_dec, w_dec_more)):
            cols = slice(i * half, (i + 1) * half)
            embedded = (dot(y, w[...]) + vec_dec[0:1, cols]).astype(BF)
            e_out[:, cols] = dot(pick, embedded).astype(BF)
        dy = dot_cols(grad[:, :half], w_dec[...]) + dot_cols(grad[:, half:], w_dec_more[...])
        dy = dy.astype(BF)
        dy_out[...] = dy
        split_cores(dot_rows(y, grad), rows_dev, spot[3], own_out, sent_out)
        db_out[...] = row_sum(dy.astype(F32))


def feed_back_kernel(rows_one, rows_two, spot, dy_in, w_two, g_in, d_in, w_one, h_in,
                     dh_out, own_two, sent_two, own_one, sent_one, db_out, turned):
    step = pl.program_id(0)

    @pl.when(step == 0)
    def _():
        turned[...] = h_in[...].T

    dy = dy_in[...]
    du = (dot_cols(dy, w_two[...]) * d_in[...].astype(F32)).astype(BF)
    db_out[...] = row_sum(du.astype(F32))
    split_cores(dot_rows(g_in[...], dy), rows_two, spot[3], own_two, sent_two)
    split_cores(dot(turned[...], du), rows_one, spot[3], own_one, sent_one)
    part = dot_cols(du, w_one[...])

    @pl.when(step == 0)
    def _():
        dh_out[...] = part

    @pl.when(step > 0)
    def _():
        dh_out[...] += part


def out_back_kernel(rows, parts, spot, dh_in, r_in, dy_in, vecs, w_out, *refs):
    o_in = refs[:parts]
    dr_out, do_out, own_out, sent_out, sums, total = refs[parts:]
    step = pl.program_id(0)
    unit, scale = normalised(r_in[...])
    grad = dh_in[...]
    dr = dy_in[...].astype(F32) + norm_back(unit, scale, vecs[5:6, :], grad)
    dr_out[...] = dr
    da = dr.astype(BF)
    do_out[...] = dot_cols(da, w_out[...]).astype(BF)

    @pl.when(step == 0)
    def _():
        sums[...] = jnp.zeros_like(sums)
        total[...] = jnp.zeros_like(total)

    sums[0:1, :] += row_sum(grad * unit)
    sums[1:2, :] += row_sum(grad)
    sums[2:3, :] += row_sum(da.astype(F32))
    width = o_in[0].shape[1]
    for i, o in enumerate(o_in):
        total[i * width : (i + 1) * width, :] += dot_rows(o[...], da)

    @pl.when(step == pl.num_programs(0) - 1)
    def _():
        split_cores(total[...], rows, spot[3], own_out, sent_out)


def attention_back_kernel(rows_dev, lay, chunk, head_dim, spot, h_in, q_in, k_in, v_in, pl_in, ps_in, do_in,
                          dq_out, dk_out, dv_out, own_out, sent_out, sums, scores, ds_big):
    big, small = lay.large_pad, lay.small_pad
    lane = lax.broadcasted_iota(jnp.int32, (1, 2 * head_dim), 1)
    low = lane < head_dim
    halves = (jnp.where(low, 1.0, 0.0).astype(BF), jnp.where(low, 0.0, 1.0).astype(BF))

    def back_rows(weights, grad):
        p = weights.astype(F32)
        inner = jnp.sum(grad * p, axis=1, keepdims=True)
        return (p * (grad - inner)).astype(BF)

    for pair in range(q_in.shape[1] // (2 * head_dim)):
        cols = slice(pair * 2 * head_dim, (pair + 1) * 2 * head_dim)
        both = jnp.concatenate([do_in[:big, cols] * h for h in halves], axis=0)
        scores[...] = dot_cols(both, v_in[:big, cols])
        for half in range(2):
            for at in range(0, big, chunk):
                rows = slice(half * big + at, half * big + at + chunk)
                ds_big[rows, :] = back_rows(pl_in[2 * pair + half, at : at + chunk, :], scores[rows, :])
        spans = [(slice(0, big), None)] + [
            (slice(start, start + small), i) for i, start in enumerate(lay.starts)
        ]
        for rows, i in spans:
            if i is None:
                size, ds = big, ds_big[...]
                weights = (pl_in[2 * pair], pl_in[2 * pair + 1])
            else:
                size = small
                weights = (ps_in[2 * pair, i], ps_in[2 * pair + 1, i])
                both = jnp.concatenate([do_in[rows, cols] * h for h in halves], axis=0)
                ds = back_rows(jnp.concatenate(weights, axis=0), dot_cols(both, v_in[rows, cols]))
            grad = dot(ds, k_in[rows, cols])
            grad = jnp.where(low, grad[:size], grad[size:]) * (head_dim**-0.5)
            dq_out[rows, cols] = grad.astype(BF)
            left, right = dot_rows(ds[:size], q_in[rows, cols]), dot_rows(ds[size:], q_in[rows, cols])
            dk_out[rows, cols] = jnp.where(low, left, right).astype(BF)
            left, right = (dot_rows(w, do_in[rows, cols]) for w in weights)
            dv_out[rows, cols] = jnp.where(low, left, right).astype(BF)
    turned = h_in[...].T
    width = dq_out.shape[1]
    for i, grad in enumerate((dq_out, dk_out, dv_out)):
        cols = slice(i * width, (i + 1) * width)
        split_cores(
            dot(turned, grad[...]), rows_dev, spot[3], own_out.at[:, :, cols], sent_out.at[:, :, cols]
        )
    sums[0:1, :] = row_sum(dq_out[...].astype(F32))
    sums[1:2, :] = row_sum(dv_out[...].astype(F32))


def first_back_kernel(lay, parts, count, widths, meta, *refs):
    grads, more = refs[: 3 * parts], refs[3 * parts : 4 * parts]
    w_qkv, x_in, dr_in, vecs, sums_two, db_two, db_one, sums_dec, out, sheet, sums, kept = refs[4 * parts :]
    step = pl.program_id(0)
    rows = x_in.shape[0]
    width = grads[0].shape[1]
    grad = dot_cols(grads[0][...], w_qkv[:, :width])
    for i in range(1, 3 * parts):
        grad += dot_cols(grads[i][...], w_qkv[:, i * width : (i + 1) * width])
    unit, scale = normalised(x_in[...].astype(F32))
    moved = dr_in[...] + norm_back(unit, scale, vecs[0:1, :], grad)
    kept[pl.ds(pl.multiple_of(step * rows, rows), rows), :] = moved.astype(BF)

    @pl.when(step == 0)
    def _():
        sums[...] = jnp.zeros_like(sums)
        for i, part in enumerate(more):
            sums[2:4, i * width : (i + 1) * width] = part[0:2, :]
        sums[4:5, :] = sums_two[2:3, :]
        sums[5:7, :] = sums_two[0:2, :]
        sums[7:8, :] = db_two[...]

    sums[0:1, :] += row_sum(grad * unit)
    sums[1:2, :] += row_sum(grad)

    @pl.when(step == pl.num_programs(0) - 1)
    def _():
        slot = lax.broadcasted_iota(jnp.int32, (out.shape[0], 1), 0)
        row = lax.broadcasted_iota(jnp.int32, (1, lay.rows), 1)
        out[...] = dot(one_hot(slot, lay.source(row, meta[BIG])), kept[...]).astype(BF)
        pack_rows(count, widths[0], sums[...], sheet, 0)
        pack_rows(count, widths[1], db_one[...], sheet, 8)
        pack_rows(count, widths[2], sums_dec[0:2, :], sheet, 9)


def owner_rank(owner_vec):
    window_ids = jnp.arange(owner_vec.shape[0], dtype=jnp.int32)
    earlier = (owner_vec[:, None] == owner_vec[None, :]) & (
        window_ids[None, :] < window_ids[:, None]
    )
    return jnp.sum(earlier.astype(jnp.int32), axis=1)


def spec(shape, index):
    return pl.BlockSpec(shape, index)


def local(tokens, ln1_gain, ln1_bias, qkv_weight, query_bias, value_bias, out_weight, out_bias,
          ln2_gain, ln2_bias, fc1_weight, fc1_bias, fc2_weight, fc2_bias, dec_weight, dec_bias,
          mask_token, kept_offsets, kept_count, res_id, dec_owner, dec_cot):
    count = lax.axis_size("dp")
    dev = Slice(count)
    vis, D = tokens.shape
    dec_width = dec_cot.shape[1]
    windows, slots = kept_offsets.shape
    images = res_id.shape[0]
    hidden = fc1_weight.shape[1]
    head_dim = D // HEADS
    per_peer = (windows + count - 1) // count
    total = count * per_peer
    lay = Layout(images, slots)
    R = lay.rows
    sd = jax.ShapeDtypeStruct

    ga, gc = Gather(dev, [qkv_weight]), Gather(dev, [fc2_weight])
    za = ga.along_z()
    xa = ga.first()
    kept_offsets, kept_count, dec_owner, ln1_gain, dec_bias, fc1_bias = held(
        (kept_offsets, kept_count, dec_owner, ln1_gain, dec_bias, fc1_bias), *ga.sent
    )
    wide = max(fc1_bias.shape[0], 128)
    sizes = (dev.size["z"], dev.size["y"], dev.size["x"])
    lanes = -(-windows // 128) * 128
    meta, place_row, info_send = pl.pallas_call(
        functools.partial(describe_kernel, lay, sizes, per_peer),
        name="describe",
        in_specs=[SMEM, SMEM, SMEM, VMEM, VMEM],
        out_specs=[SMEM, VMEM, VMEM],
        out_shape=[sd((16,), jnp.int32), sd((1, R), jnp.int32), sd((total, wide), BF)],
        scratch_shapes=[pltpu.VMEM((8, lanes), F32), pltpu.VMEM((lanes, wide), F32)],
        compiler_params=params(),
    )(lax.axis_index("dp").astype(jnp.int32).reshape(1), kept_count, res_id, dec_owner.reshape(1, windows),
      kept_offsets)
    eight = [ln1_gain, ln1_bias, query_bias, value_bias, out_bias, ln2_gain, ln2_bias, fc2_bias]
    vectors = eight + [fc1_bias, dec_bias, mask_token]
    line = lambda v: jnp.pad(v, ((0, 0), (0, wide - v.shape[1])))
    sheet = jnp.concatenate(
        [line(jnp.stack(eight)), line(fc1_bias[None, :]), line(jnp.stack([dec_bias, mask_token]))], axis=0
    )
    packed = jnp.concatenate(
        [jnp.broadcast_to(sheet[None], (count,) + sheet.shape), info_send.reshape(count, per_peer, wide)],
        axis=1,
    )
    ya = ga.second(packed)
    rest = lax.all_gather(
        jnp.concatenate([fc1_weight, out_weight, dec_weight], axis=1),
        "dp",
        axis=0,
        tiled=True,
    )
    packed = lax.all_to_all(packed, "dp", 0, 0, tiled=True)
    n_vec = eight[0].shape[0]
    vecs = packed[:, :8, :n_vec].transpose(1, 0, 2).reshape(8, D).astype(F32)
    bf1 = packed[:, 8, : fc1_bias.shape[0]].reshape(1, hidden).astype(F32)
    vec_dec = packed[:, 9:11, : dec_bias.shape[0]].transpose(1, 0, 2).reshape(2, dec_width).astype(F32)
    info_got = packed[:, 11:].reshape(total, wide)

    w_out_spec = spec((D, D), lambda *_: (0, hidden // D))
    first_dec, dec_half = 2 * (hidden + D) // dec_width, dec_width // 2
    w_dec_specs = [spec((D, dec_half), lambda *_, i=i: (0, first_dec + i)) for i in range(2)]
    tile = R // 3
    rows_of = lambda width: spec((tile, width), lambda i: (i, 0))
    x_rows, h_one = pl.pallas_call(
        functools.partial(first_norm_kernel, lay),
        name="first_norm",
        grid=(3,),
        in_specs=[SMEM, whole((vis, D)), whole((8, D))],
        out_specs=[rows_of(D), rows_of(D)],
        out_shape=[sd((R, D), BF), sd((R, D), BF)],
        compiler_params=params(),
        cost_estimate=cost(2 * R * vis * D, 4e6, weight=0.02),
    )(meta, held(tokens, za), vecs)

    from_a = ga.swap(h_one)
    zc = gc.along_z(*ga.sent)

    wins = 16
    steps = total // wins
    cells_w, rows_w = wins * GRID, wins * LANE_SLOTS
    by_step = lambda height, width: spec((height, width), lambda i: (i, 0))
    info_spec = by_step(wins, info_got.shape[1])
    de_send, owner_sums = pl.pallas_call(
        functools.partial(owner_kernel, slots, wins),
        name="owner_side",
        grid=(steps,),
        in_specs=[by_step(cells_w, dec_width), info_spec],
        out_specs=[by_step(rows_w, dec_width), whole((8, dec_width))],
        out_shape=[sd((total * LANE_SLOTS, dec_width), BF), sd((8, dec_width), F32)],
        compiler_params=params(),
        cost_estimate=cost(1e9, 3e6, weight=0.02),
    )(dec_cot, held(info_got, h_one, *ga.sent))

    (w_qkv,) = ga.result(meta, de_send)
    group = 4
    parts = HEADS // group
    gw = group * head_dim
    chunk = lay.large_pad // 5
    p_big_t = sd((group, lay.large_pad, lay.large_pad), BF)
    p_small_t = sd((group, images - 1, lay.small_pad, lay.small_pad), BF)

    def attend(i, h_rows):
        col_of = lambda base_: spec((D, gw), lambda _: (0, base_ * parts + i))
        return pl.pallas_call(
            functools.partial(attention_kernel, lay, chunk, head_dim),
            name="attention",
            grid=(1,),
            in_specs=[SMEM, whole((R, D)), col_of(0), col_of(1), col_of(2),
                      spec((8, gw), lambda _: (0, i))],
            out_specs=[whole((R, gw))] * 3 + [whole(p_big_t.shape), whole(p_small_t.shape), whole((R, gw))],
            out_shape=[sd((R, gw), BF)] * 3 + [p_big_t, p_small_t, sd((R, gw), BF)],
            scratch_shapes=[pltpu.VMEM((2 * lay.large_pad, lay.large_pad), F32)],
            compiler_params=params(),
            cost_estimate=cost(2 * R * D * D + 2e9, 8e6, 1e6),
        )(meta, h_rows, w_qkv, w_qkv, w_qkv, vecs)

    attn = [attend(0, h_one)]
    attn.append(attend(1, held(h_one, attn[0][5])))
    gc.first(attn[1][5])
    attn.append(attend(2, held(h_one, attn[1][5], *gc.sent)))
    gc.second(attn[2][5])
    de_got = lax.all_to_all(
        held(de_send, attn[1][5]).reshape(count, per_peer * LANE_SLOTS, dec_width), "dp", 0, 0, tiled=True
    ).reshape(total * LANE_SLOTS, dec_width)

    att = [a[5] for a in attn]

    ht = hidden // 6
    row_dev, row_two = D // count, hidden // count
    chips = count // 2
    r_one, h_two, act_h, d_gelu = pl.pallas_call(
        functools.partial(feed_kernel, parts, R // 24),
        name="feed",
        grid=(6,),
        in_specs=[whole((R, gw))] * parts
        + [w_out_spec, whole((8, D)), whole((R, D)), spec((D, ht), lambda j: (0, j)),
           spec((1, ht), lambda j: (0, j))],
        out_specs=[whole((R, D)), whole((R, D))] + [spec((R, ht), lambda j: (0, j))] * 2,
        out_shape=[sd((R, D), F32), sd((R, D), BF), sd((R, hidden), BF), sd((R, hidden), BF)],
        scratch_shapes=[pltpu.VMEM((R, ht), F32)],
        compiler_params=params(),
        cost_estimate=cost(2 * R * D * (hidden + D), 2.5e7, 6e6),
    )(*att, rest, vecs, held(x_rows, *gc.sent), rest, bf1)
    gc.swap(h_two)

    ht = hidden // 4
    nz, ny, nx = sizes
    part = pl.BlockSpec(
        (ny, nx, 1, row_two, D // 2), lambda j, at: (0, 0, lax.rem(at[0] - j + nz, nz), 0, 0)
    )
    ht = hidden // nz
    w_two, e_send, dy, own_dec, sent_dec, db_two = pl.pallas_call(
        functools.partial(join_kernel, row_dev, sizes),
        name="join",
        grid_spec=pltpu.PrefetchScalarGridSpec(
            num_scalar_prefetch=1,
            grid=(nz,),
            in_specs=[spec((R, ht), lambda j, _: (0, j)), part, part, part, part, whole((8, D)),
                      whole((R, D)), *w_dec_specs, whole((2, dec_width)), whole((1, R)),
                      whole((total * LANE_SLOTS, dec_width))],
            out_specs=[spec((2 * ny * nx, row_two, D), lambda j, _: (j, 0, 0)),
                       whole((total * LANE_SLOTS, dec_width)), whole((R, D)),
                       whole((chips, row_dev, dec_width)), whole((chips, row_dev, dec_width)), whole((1, D))],
            scratch_shapes=[pltpu.VMEM((R, D), F32)],
        ),
        out_shape=[sd((count, row_two, D), BF), sd((total * LANE_SLOTS, dec_width), BF), sd((R, D), BF),
                   sd((chips, row_dev, dec_width), BF), sd((chips, row_dev, dec_width), BF), sd((1, D), F32)],
        compiler_params=params(),
        cost_estimate=cost(2 * R * D * hidden + 10 * R * D * dec_width, 2e7),
    )(meta, act_h, gc.part_a, gc.part_b, gc.from_a, gc.from_b, vecs, r_one, rest, rest, vec_dec, place_row,
      de_got)
    w_two = w_two.reshape(hidden, D)
    ht = hidden // 4

    e_got = lax.all_to_all(
        e_send.reshape(count, per_peer * LANE_SLOTS, dec_width), "dp", 0, 0, tiled=True
    ).reshape(total * LANE_SLOTS, dec_width)

    held_chips = ht // (2 * row_two)
    tile_two = spec((held_chips, row_two, D), lambda j: (j, 0, 0))
    tile_one = spec((chips, row_dev, ht), lambda j: (0, 0, j))
    dh, own_two, sent_two, own_one, sent_one, db_one = pl.pallas_call(
        functools.partial(feed_back_kernel, row_dev, row_two),
        name="feed_back",
        grid=(4,),
        in_specs=[SMEM, whole((R, D)), spec((ht, D), lambda j: (j, 0)), spec((R, ht), lambda j: (0, j)),
                  spec((R, ht), lambda j: (0, j)), spec((D, ht), lambda j: (0, j)), whole((R, D))],
        out_specs=[whole((R, D)), tile_two, tile_two, tile_one, tile_one, spec((1, ht), lambda j: (0, j))],
        out_shape=[sd((R, D), F32)] + [sd((chips, row_two, D), BF)] * 2
        + [sd((chips, row_dev, hidden), BF)] * 2 + [sd((1, hidden), F32)],
        scratch_shapes=[pltpu.VMEM((D, R), BF)],
        compiler_params=params(),
        cost_estimate=cost(8 * R * D * hidden, 4e7, weight=20),
    )(meta, dy, w_two, act_h, d_gelu, rest, h_two)
    s_two = Scatter(dev, [(own_two, sent_two)], meta)
    s_one = Scatter(dev, [(own_one, sent_one), (own_dec, sent_dec)], meta)
    c_two, c_one = s_two.swap(), s_one.swap()

    grad_spec = whole((chips, row_dev, D))
    dr, d_att, own_out, sent_out, sums_two = pl.pallas_call(
        functools.partial(out_back_kernel, row_dev, parts),
        name="out_back",
        grid=(3,),
        in_specs=[SMEM, rows_of(D), rows_of(D), rows_of(D), whole((8, D)), w_out_spec]
        + [rows_of(gw)] * parts,
        out_specs=[rows_of(D), rows_of(D), grad_spec, grad_spec, whole((8, D))],
        out_shape=[sd((R, D), F32), sd((R, D), BF)] + [sd((chips, row_dev, D), BF)] * 2
        + [sd((8, D), F32)],
        scratch_shapes=[pltpu.VMEM((D, D), F32)],
        compiler_params=params(),
        cost_estimate=cost(4 * R * D * D, 2e7, weight=20),
    )(meta, dh, r_one, dy, vecs, rest, *att)
    s_two.add(dr, *c_two)
    near = s_two.near()

    def attend_back(i, d_att_rows):
        q_rows, k_rows, v_rows, prob_l, prob_s, _ = attn[i]
        grad_shape = (chips, row_dev, 3 * gw)
        return pl.pallas_call(
            functools.partial(attention_back_kernel, row_dev, lay, chunk, head_dim),
            name="attention_back",
            grid=(1,),
            in_specs=[SMEM, whole((R, D))] + [whole((R, gw))] * 3
            + [whole(p_big_t.shape), whole(p_small_t.shape), spec((R, gw), lambda _: (0, i))],
            out_specs=[whole((R, gw))] * 3 + [whole(grad_shape)] * 2 + [whole((8, gw))],
            out_shape=[sd((R, gw), BF)] * 3 + [sd(grad_shape, BF)] * 2 + [sd((8, gw), F32)],
            scratch_shapes=[pltpu.VMEM((2 * lay.large_pad, lay.large_pad), F32),
                            pltpu.VMEM((2 * lay.large_pad, lay.large_pad), BF)],
            compiler_params=params(),
            cost_estimate=cost(2 * R * D * D + 3e9, 1e7, weight=20),
        )(meta, h_one, q_rows, k_rows, v_rows, prob_l, prob_s, d_att_rows)

    back = [attend_back(0, held(d_att, s_two.blocks[0], e_got, *c_one))]
    far = s_two.far(back[0][0], *near)
    s_one.add(back[0][0], *near)
    near = s_one.near()
    s_mid = Scatter(dev, [(own_out, sent_out), back[0][3:5]], meta)
    c_mid = s_mid.swap(back[0][0])
    back.append(attend_back(1, held(d_att, back[0][0], s_one.blocks[0])))
    lines_two, z_two = finish(dev, meta, [s_two], True, back[1][0], *far)
    far = s_one.far(back[1][0], *near)
    s_mid.more(*back[1][3:5])
    c_mid += s_mid.swap(back[1][0])
    back.append(attend_back(2, held(d_att, back[1][0], lines_two[0], *near)))
    s_last = Scatter(dev, [back[2][3:5]], meta)
    c_last = s_last.swap(back[2][0])
    s_mid.add(back[2][0], *c_mid)
    near = s_mid.near() + s_mid.far()
    lines_one, z_one = finish(dev, meta, [s_one], True, back[2][0], *far, z_two, s_mid.blocks[0])

    dqkv = [b[i] for i in range(3) for b in back]
    widths = (ln1_gain.shape[0], fc1_bias.shape[0], dec_bias.shape[0])
    grad_tokens, sheet = pl.pallas_call(
        functools.partial(first_back_kernel, lay, parts, count, widths),
        name="first_back",
        grid=(3,),
        in_specs=[SMEM] + [rows_of(gw)] * (3 * parts) + [whole((8, gw))] * parts
        + [whole((D, 3 * D)), rows_of(D), rows_of(D), whole((8, D)), whole((8, D)), whole((1, D)), whole((1, hidden)),
           whole((8, dec_width))],
        out_specs=[whole((vis, D)), whole((11, count, 128))],
        out_shape=[sd((vis, D), BF), sd((11, count, 128), F32)],
        scratch_shapes=[pltpu.VMEM((8, D), F32), pltpu.VMEM((R, D), BF)],
        compiler_params=params(),
        cost_estimate=cost(2 * R * D * 3 * D + 2 * R * vis * D, 2e7, weight=20),
    )(meta, *dqkv, *[b[5] for b in back], w_qkv, x_rows, held(dr, s_mid.blocks[0], *lines_one), vecs, sums_two,
      db_two, db_one, owner_sums)
    blocks = -(-11 // row_dev)
    vec_width = -(-128 * blocks // 384) * 384
    ride = jnp.pad(sheet, ((0, blocks * row_dev - 11), (0, 0), (0, 0)))
    ride = ride.reshape(blocks, row_dev, count, 128).transpose(2, 1, 0, 3).reshape(count, row_dev, -1)
    ride = jnp.pad(ride, ((0, 0), (0, 0), (0, vec_width - 128 * blocks))).astype(BF)
    ride = ride.reshape(chips, 2, row_dev, vec_width)
    even = dev.coord("c") == 0
    s_last.more(
        jnp.where(even, ride[:, 0], ride[:, 1]), jnp.where(even, ride[:, 1], ride[:, 0])
    )
    c_last += s_last.swap(grad_tokens)
    s_last.add(grad_tokens, *near, *c_last)
    near = s_last.near() + s_last.far()

    decoded = pl.pallas_call(
        functools.partial(decode_kernel, slots, wins),
        name="decode",
        grid=(steps,),
        in_specs=[by_step(rows_w, dec_width), info_spec, whole((2, dec_width))],
        out_specs=by_step(cells_w, dec_width),
        out_shape=sd((total * GRID, dec_width), BF),
        scratch_shapes=[pltpu.VMEM((3 * 32, dec_width // 2), BF)],
        compiler_params=params(),
        cost_estimate=cost(1e9, 7e6, weight=20),
    )(held(e_got, s_last.blocks[0], z_one), info_got, vec_dec)


    lines_late, z_late = finish(dev, meta, [s_mid, s_last], False, decoded, *near)
    (grad_two,) = totals(z_two, [s_two])
    grad_one, grad_dec = totals(z_one, [s_one])
    grad_out, grad_qkv, *vec_grads = last_sums(
        z_late, [s_mid, s_last], D, gw, [v.shape[0] for v in vectors]
    )
    vec_grads = [v.reshape(-1) for v in vec_grads]
    (gg1, gb1, gbq, gbv, gbo, gg2, gb2, gbf2, gbf1, gbdec, gmask) = vec_grads
    return (decoded, grad_tokens, gg1, gb1, grad_qkv, gbq, gbv, grad_out, gbo, gg2, gb2, grad_one,
            gbf1, grad_two, gbf2, grad_dec, gbdec, gmask)


def solution(mesh):
    mat, vec = P("dp", None), P("dp")
    in_specs = (mat, vec, vec, mat, vec, vec, mat, vec, vec, vec, mat, vec, mat, vec, mat, vec, vec,
                mat, vec, vec, vec, mat)
    out_specs = (mat, mat, vec, vec, mat, vec, vec, mat, vec, vec, vec, mat, vec, mat, vec, mat, vec,
                 vec)
    return jax.shard_map(local, mesh=mesh, in_specs=in_specs, out_specs=out_specs, check_vma=False)
```
